32 devices in a mesh: seq: 4 (over y, x), fsdp: 8 (over z, core).
Axes of the slice: x: 2, y: 2, z: 4, core: 2. Of those that a mesh axis runs over, the one named last changes fastest.
Arguments:
- inputs: bfloat16 [2, 8, 1024, 2048], P(None, 'fsdp', 'seq'), may hold values from -6 to 6
- cotangent: bfloat16 [2, 8, 1024, 2048], P(None, 'fsdp', 'seq'), may hold values from -6 to 6
- segments: int32 [2, 8, 1024], P(None, 'fsdp'), may hold values from 0 to 3, as said below
- norm_in: bfloat16 [2048], P(('seq', 'fsdp')), may hold values from 0.25 to 1.75
- ssm_in: bfloat16 [2048, 6704], P(('seq', 'fsdp')), may hold values from -0.125 to 0.125
- attn_in: bfloat16 [2048, 1536], P(('seq', 'fsdp')), may hold values from -0.125 to 0.125
- conv_w: bfloat16 [4, 3584], P(None, ('seq', 'fsdp')), may hold values from -3 to 3
- conv_b: bfloat16 [3584], P(('seq', 'fsdp')), may hold values from -0.5 to 0.5
- a_log: bfloat16 [48], replicated, may hold values from 0 to 2.765625
- dt_bias: bfloat16 [48], replicated, may hold values from -4 to -1
- d_skip: bfloat16 [48], replicated, may hold values from 0.5 to 1.5
- ssm_out: bfloat16 [3072, 2048], P(('seq', 'fsdp')), may hold values from -0.109375 to 0.109375
- attn_out: bfloat16 [1024, 2048], P(('seq', 'fsdp')), may hold values from -1.5 to 1.5
- norm_ffn: bfloat16 [2048], P(('seq', 'fsdp')), may hold values from 0.25 to 1.75
- w_gate: bfloat16 [2048, 4096], P(('seq', 'fsdp')), may hold values from -0.125 to 0.125
- w_up: bfloat16 [2048, 4096], P(('seq', 'fsdp')), may hold values from -0.125 to 0.125
- w_down: bfloat16 [4096, 2048], P(('seq', 'fsdp')), may hold values from -0.09375 to 0.09375
Outputs:
- outputs: bfloat16 [2, 8, 1024, 2048], P(None, 'fsdp', 'seq')
- input_grad: bfloat16 [2, 8, 1024, 2048], P(None, 'fsdp', 'seq')
- norm_in_grad: float32 [2048], P(('seq', 'fsdp'))
- ssm_in_grad: float32 [2048, 6704], P(('seq', 'fsdp'))
- attn_in_grad: float32 [2048, 1536], P(('seq', 'fsdp'))
- conv_w_grad: float32 [4, 3584], P(None, ('seq', 'fsdp'))
- conv_b_grad: float32 [3584], P(('seq', 'fsdp'))
- a_log_grad: float32 [48], replicated
- dt_bias_grad: float32 [48], replicated
- d_skip_grad: float32 [48], replicated
- ssm_out_grad: float32 [3072, 2048], P(('seq', 'fsdp'))
- attn_out_grad: float32 [1024, 2048], P(('seq', 'fsdp'))
- norm_ffn_grad: float32 [2048], P(('seq', 'fsdp'))
- w_gate_grad: float32 [2048, 4096], P(('seq', 'fsdp'))
- w_up_grad: float32 [2048, 4096], P(('seq', 'fsdp'))
- w_down_grad: float32 [4096, 2048], P(('seq', 'fsdp'))
The draws below stay inside these ranges and needn't reach their ends.
Inputs may be any that keep to these rules, and one draw needn't show every extreme that they name: `segments`: segment numbers never fall along a sequence.
All inputs are finite; a program needn't handle non-finite values.
Results may differ from the reference program's by a relative error of at most 0.013.
The reference program's roundings to bfloat16 on the way count: a program that leaves them out, or rounds other values in their place, can miss the bound.
Values may be sent and summed in bfloat16 or wider, within the bound.
No kernel may reach another device: no remote copies, remote signals or barrier semaphores. Data moves between devices by JAX's collectives and lax.ppermute only.
A program may use at most 512 MiB of HBM per device.

```python
import jax
import jax.numpy as jnp
from jax import lax

D = 2048
SSM_HEADS = 48
STATE = 256
CONV = 4
Q_HEADS = 8
KV_HEADS = 2
HEAD_DIM = 128
FF = 4096
LENGTH = 1024
MICRO = 2
SPAN = 128
ATT_BLOCK = 512
TOK_SLICE = 256
GROUPS = 8
SSM_INNER = 3072
CONV_CH = 3584
IN_COLS = 6704
ATT_COLS = 1536


def draw_segments(key, part):
    key = jax.random.fold_in(key, 11)
    key_chosen, key_first, key_last, key_cuts = jax.random.split(key, 4)
    chosen = jax.random.randint(key_chosen, (1, GROUPS, 1), 0, MICRO)
    batch_ids = jnp.arange(MICRO, dtype=jnp.int32)[:, None, None]
    first_cut = jax.random.randint(key_first, (MICRO, GROUPS, 1), 1, TOK_SLICE)
    last_cut = jax.random.randint(key_last, (MICRO, GROUPS, 1), LENGTH - TOK_SLICE + 1, LENGTH)
    long_cuts = jnp.concatenate([first_cut, last_cut, last_cut], axis=2)
    free_cuts = jax.random.randint(key_cuts, (MICRO, GROUPS, 3), 1, LENGTH)
    cuts = jnp.where(batch_ids == chosen, long_cuts, free_cuts)
    positions = jnp.arange(LENGTH, dtype=jnp.int32)
    passed = (positions[None, None, :, None] >= cuts[:, :, None, :]).astype(jnp.int32)
    return jnp.sum(passed, axis=3).astype(jnp.int32)


def steps_of(stream_key, shape, pieces, low, top_value):
    def one(dim, blocks):
        steps = jax.random.uniform(jax.random.fold_in(jax.random.fold_in(stream_key, 6), dim), (blocks,), jnp.float32, low / len(pieces), top_value / len(pieces))
        return jnp.repeat(jnp.exp(steps), shape[dim] // blocks).reshape((-1,) + (1,) * (len(shape) - dim - 1))

    factor_of = one(*pieces[0])
    for cut in pieces[1:]:
        factor_of = factor_of * one(*cut)
    return factor_of


def normal_values(key, extent, width, bound, cuts=(), held_as=jnp.bfloat16):
    factor_of = steps_of(key, extent, cuts, -0.22, 0.18) if cuts else 1.0
    values = jax.random.normal(key, extent, jnp.float32) * width * factor_of
    return jnp.minimum(jnp.maximum(values, -bound), bound).astype(held_as)


def setup_inputs(seed: int = 0) -> dict:
    seeds = jax.random.split(jax.random.key(seed), 18)
    return {
        "inputs": normal_values(seeds[0], (MICRO, GROUPS, LENGTH, D), 1.0, 6.0, ((1, 8), (2, 4))),
        "cotangent": normal_values(seeds[1], (MICRO, GROUPS, LENGTH, D), 1.0, 6.0, ((1, 8), (2, 4))),
        "segments": draw_segments(jax.random.fold_in(seeds[17], 71), 0),
        "norm_in": jnp.clip(1.0 + 0.15 * jax.random.normal(seeds[3], (D,), jnp.float32), 0.25, 1.75).astype(jnp.bfloat16),
        "ssm_in": normal_values(seeds[4], (D, IN_COLS), D ** -0.5, 0.125, ((0, 32),)),
        "attn_in": normal_values(seeds[5], (D, ATT_COLS), D ** -0.5, 0.125, ((0, 32),)),
        "conv_w": normal_values(seeds[6], (CONV, CONV_CH), CONV ** -0.5, 3.0, ((1, 32),)),
        "conv_b": jnp.clip(jax.random.uniform(seeds[7], (CONV_CH,), jnp.float32, -0.5, 0.5) * steps_of(seeds[7], (CONV_CH,), ((0, 32),), -0.4, 0.0), -0.5, 0.5).astype(jnp.bfloat16),
        "a_log": jnp.clip(jax.random.uniform(seeds[8], (SSM_HEADS,), jnp.float32, 0.0, 2.765625), 0.0, 2.765625).astype(jnp.bfloat16),
        "dt_bias": jnp.clip(jax.random.uniform(seeds[9], (SSM_HEADS,), jnp.float32, -4.0, -1.0), -4.0, -1.0).astype(jnp.bfloat16),
        "d_skip": jnp.clip(jax.random.uniform(seeds[10], (SSM_HEADS,), jnp.float32, 0.5, 1.5), 0.5, 1.5).astype(jnp.bfloat16),
        "ssm_out": normal_values(seeds[11], (SSM_INNER, D), SSM_INNER ** -0.5, 0.109375, ((0, 32),)),
        "attn_out": normal_values(seeds[12], (Q_HEADS * HEAD_DIM, D), (Q_HEADS * HEAD_DIM // 64) ** -0.5, 1.5, ((0, 32),)),
        "norm_ffn": jnp.clip(1.0 + 0.15 * jax.random.normal(seeds[13], (D,), jnp.float32), 0.25, 1.75).astype(jnp.bfloat16),
        "w_gate": normal_values(seeds[14], (D, FF), D ** -0.5, 0.125, ((0, 32),)),
        "w_up": normal_values(seeds[15], (D, FF), D ** -0.5, 0.125, ((0, 32),)),
        "w_down": normal_values(seeds[16], (FF, D), FF ** -0.5, 0.09375, ((0, 32),)),
    }


PRECISE = lax.Precision.HIGHEST
EPSILON = 1e-05
ROPE_BASE = 10000.0

@jax.custom_vjp
def low(v):
    return lax.optimization_barrier(v.astype(jnp.bfloat16)).astype(jnp.float32)

@jax.custom_vjp
def low_back(v):
    return v

def low_keep(v):
    return (low(v), None)

def low_pass(kept, grad):
    return (grad,)

def back_keep(v):
    return (v, None)

def back_low(kept, grad):
    return (low(grad),)
low.defvjp(low_keep, low_pass)
low_back.defvjp(back_keep, back_low)

def matmul(left, right):
    return jnp.dot(left, right, precision=PRECISE, preferred_element_type=jnp.float32)

def rms_norm(token_rows, gain_vec):
    inv_scale = lax.rsqrt(lax.optimization_barrier(jnp.mean(token_rows * token_rows, axis=-1, keepdims=True)) + EPSILON)
    return token_rows * inv_scale * gain_vec

def repeat_heads(kv_rows, groups):
    length = kv_rows.shape[0]
    shaped = kv_rows.reshape(length, -1, 1, HEAD_DIM)
    return jnp.broadcast_to(shaped, (length, shaped.shape[1], groups, HEAD_DIM)).reshape(length, -1)

def rotate(head_rows, positions):
    half_width = head_rows.shape[-1] // 2
    frequency = ROPE_BASE ** (-jnp.arange(half_width).astype(jnp.float32) / half_width)
    angles = positions.astype(jnp.float32)[:, None] * frequency[None, :]
    cosine = jnp.cos(angles)[:, None, :]
    sine_part = jnp.sin(angles)[:, None, :]
    lead_half = head_rows[..., :half_width]
    tail_half = head_rows[..., half_width:]
    return jnp.concatenate([lead_half * cosine - tail_half * sine_part, tail_half * cosine + lead_half * sine_part], axis=-1)

def causal_conv(channels, segment, conv_weight, conv_bias):
    length = channels.shape[0]
    summed = jnp.broadcast_to(conv_bias[None, :], channels.shape)
    for offset in range(CONV):
        shifted = jnp.pad(channels, ((offset, 0), (0, 0)))[:length]
        earlier = jnp.pad(segment, (offset, 0), constant_values=-1)[:length]
        keep_mask = (earlier == segment).astype(jnp.float32)
        summed = summed + conv_weight[CONV - 1 - offset][None, :] * shifted * keep_mask[:, None]
    return jax.nn.silu(summed)

def ssd_scan(x_heads, log_decay, step_size, b_rows, c_rows, segment):
    length, head_count, head_width = x_heads.shape
    block_count = length // SPAN
    seq_items = (x_heads.reshape(block_count, SPAN, head_count, head_width), log_decay.reshape(block_count, SPAN, head_count), step_size.reshape(block_count, SPAN, head_count), b_rows.reshape(block_count, SPAN, STATE), c_rows.reshape(block_count, SPAN, STATE), segment.reshape(block_count, SPAN))
    lower_mask = jnp.tril(jnp.ones((SPAN, SPAN), dtype=bool))

    def block_step(block_carry, block_items):
        ssm_state, last_segment = block_carry
        x_block, decay_block, step_block, b_block, c_block, seg_block = block_items
        cumulative = jnp.cumsum(decay_block, axis=0)
        same_doc = ((seg_block[:, None] == seg_block[None, :]) & lower_mask)[:, :, None]
        decay_gap = cumulative[:, None, :] - cumulative[None, :, :]
        inner_weight = jnp.where(same_doc, jnp.exp(jnp.where(same_doc, decay_gap, 0.0)), 0.0)
        block_scores = jnp.dot(c_block, b_block.T, precision=PRECISE)
        mixing = inner_weight * block_scores[:, :, None] * step_block[None, :, :]
        y_inner = jnp.einsum('tsh,shp->thp', mixing, x_block, precision=PRECISE)
        carry_keep = (seg_block == last_segment).astype(jnp.float32)
        state_weight = jnp.exp(cumulative) * carry_keep[:, None]
        from_state = jnp.einsum('tn,hpn->thp', c_block, ssm_state, precision=PRECISE) * state_weight[:, :, None]
        end_keep = (seg_block == seg_block[-1]).astype(jnp.float32)
        input_weight = jnp.exp(cumulative[-1][None, :] - cumulative) * step_block * end_keep[:, None]
        state_keep = jnp.exp(cumulative[-1]) * (seg_block[-1] == last_segment).astype(jnp.float32)
        new_state = ssm_state * state_keep[:, None, None] + jnp.einsum('sh,shp,sn->hpn', input_weight, x_block, b_block, precision=PRECISE)
        return ((new_state, seg_block[-1]), y_inner + from_state)
    start_carry = (jnp.zeros((head_count, head_width, STATE), jnp.float32), jnp.array(-1, jnp.int32))
    unused, y_blocks = lax.scan(jax.checkpoint(block_step), start_carry, seq_items)
    return y_blocks.reshape(length, head_count, head_width)

def attend(q_rot, k_rot, value_heads, segment):
    length, head_count, head_width = q_rot.shape
    block_count = length // ATT_BLOCK
    positions = jnp.arange(length, dtype=jnp.int32)

    def one_block(block_index):
        first_row = block_index * ATT_BLOCK
        q_block = lax.dynamic_slice_in_dim(q_rot, first_row, ATT_BLOCK, 0)
        seg_query = lax.dynamic_slice_in_dim(segment, first_row, ATT_BLOCK, 0)
        pos_query = first_row + jnp.arange(ATT_BLOCK, dtype=jnp.int32)
        scores = jnp.einsum('qhe,khe->hqk', q_block, k_rot, precision=PRECISE) * head_width ** (-0.5)
        allowed = (pos_query[:, None] >= positions[None, :]) & (seg_query[:, None] == segment[None, :])
        scores = jnp.where(allowed[None, :, :], scores, -1e+30)
        attn_probs = low(jax.nn.softmax(scores, axis=-1))
        return jnp.einsum('hqk,khe->qhe', attn_probs, value_heads, precision=PRECISE)
    blocks = lax.map(jax.checkpoint(one_block), jnp.arange(block_count, dtype=jnp.int32))
    return blocks.reshape(length, head_count, head_width)

def mixer_heads(x_part, dt_part, query_rows, key_rep, value_rep, bc_part, segment, conv_weight, conv_bias, log_rate, step_bias, skip_gain):
    length = x_part.shape[0]
    inner_width = x_part.shape[1]
    head_count = dt_part.shape[1]
    conv_out = low(causal_conv(jnp.concatenate([x_part, bc_part], axis=1), segment, conv_weight, conv_bias))
    x_heads = conv_out[:, :inner_width].reshape(length, head_count, inner_width // head_count)
    b_rows = conv_out[:, inner_width:inner_width + STATE]
    c_rows = conv_out[:, inner_width + STATE:]
    step_size = jax.nn.softplus(dt_part + step_bias[None, :])
    log_decay = -jnp.exp(log_rate)[None, :] * step_size
    y_heads = ssd_scan(x_heads, log_decay, step_size, b_rows, c_rows, segment) + skip_gain[None, :, None] * x_heads
    y_rows = low_back(low(y_heads.reshape(length, inner_width)))
    positions = jnp.arange(length, dtype=jnp.int32)
    query_heads = query_rows.shape[1] // HEAD_DIM
    q_rot = low(rotate(query_rows.reshape(length, query_heads, HEAD_DIM), positions))
    k_rot = low(rotate(key_rep.reshape(length, query_heads, HEAD_DIM), positions))
    attended = attend(q_rot, k_rot, value_rep.reshape(length, query_heads, HEAD_DIM), segment)
    attended = low_back(low(attended.reshape(length, query_heads * HEAD_DIM)))
    return (y_rows, attended)

def forward(token_rows, segment, params):
    norm_in, ssm_in, attn_in, conv_w, conv_b, a_log, dt_bias, d_skip, ssm_out, attn_out, norm_ffn, w_gate, w_up, w_down = params
    hidden_in = low(rms_norm(token_rows, norm_in))
    projected = matmul(hidden_in, ssm_in)
    gate_z = low_back(projected[:, :SSM_INNER])
    x_part = low_back(low(projected[:, SSM_INNER:2 * SSM_INNER]))
    bc_part = low_back(low(projected[:, 2 * SSM_INNER:2 * SSM_INNER + 2 * STATE]))
    dt_part = low_back(low(projected[:, 2 * SSM_INNER + 2 * STATE:]))
    attn_rows = matmul(hidden_in, attn_in)
    q_width = Q_HEADS * HEAD_DIM
    k_width = KV_HEADS * HEAD_DIM
    query_rows = low_back(low(attn_rows[:, :q_width]))
    key_rows = low(low_back(attn_rows[:, q_width:q_width + k_width]))
    value_rows = low(low_back(attn_rows[:, q_width + k_width:]))
    groups = Q_HEADS // KV_HEADS
    key_rep = low_back(repeat_heads(key_rows, groups))
    value_rep = low_back(repeat_heads(value_rows, groups))
    y_rows, attended = mixer_heads(x_part, dt_part, query_rows, key_rep, value_rep, bc_part, segment, conv_w, conv_b, a_log, dt_bias, d_skip)
    gated_rows = low(y_rows * jax.nn.silu(gate_z))
    mixed_rows = low_back(matmul(gated_rows, ssm_out) + matmul(attended, attn_out))
    middle = token_rows + mixed_rows
    hidden_ffn = low(rms_norm(middle, norm_ffn))
    gate_pre = low_back(matmul(hidden_ffn, w_gate))
    up_pre = low_back(matmul(hidden_ffn, w_up))
    activated = low(jax.nn.silu(gate_pre) * up_pre)
    return middle + matmul(activated, w_down)

def reference(inputs, cotangent, segments, norm_in, ssm_in, attn_in, conv_w, conv_b, a_log, dt_bias, d_skip, ssm_out, attn_out, norm_ffn, w_gate, w_up, w_down):
    params = tuple((weight.astype(jnp.float32) for weight in (norm_in, ssm_in, attn_in, conv_w, conv_b, a_log, dt_bias, d_skip, ssm_out, attn_out, norm_ffn, w_gate, w_up, w_down)))
    seq_count = MICRO * GROUPS
    flat_rows = inputs.astype(jnp.float32).reshape(seq_count, LENGTH, D)
    flat_cot = cotangent.astype(jnp.float32).reshape(seq_count, LENGTH, D)
    flat_seg = segments.reshape(seq_count, LENGTH)

    def one_sequence(grad_sums, seq_items):
        token_rows, seq_cot, segment = seq_items

        def apply_layer(layer_in, layer_params):
            return forward(layer_in, segment, layer_params)
        result, pullback = jax.vjp(apply_layer, token_rows, params)
        row_grad, param_grads = pullback(seq_cot)
        grad_sums = jax.tree.map(jnp.add, grad_sums, param_grads)
        return (grad_sums, (result.astype(jnp.bfloat16), row_grad.astype(jnp.bfloat16)))
    start_sums = tuple((jnp.zeros_like(weight) for weight in params))
    grad_sums, (results, row_grads) = lax.scan(one_sequence, start_sums, (flat_rows, flat_cot, flat_seg))
    return (results.reshape(inputs.shape), row_grads.reshape(inputs.shape), grad_sums[0], grad_sums[1], grad_sums[2], grad_sums[3], grad_sums[4], grad_sums[5], grad_sums[6], grad_sums[7], grad_sums[8], grad_sums[9], grad_sums[10], grad_sums[11], grad_sums[12], grad_sums[13])
```

```python
import jax
import jax.numpy as jnp
from jax import lax
from jax.sharding import PartitionSpec as P

SSM_HEADS = 48
SSM_DIM = 64
STATE = 256
CONV = 4
Q_HEADS = 8
KV_HEADS = 2
HEAD_DIM = 128
MICRO = 2
SPAN = 128
ATT_BLOCK = 512
SSM_INNER = 3072
CONV_CH = 3584


PRECISE = lax.Precision.HIGHEST
EPSILON = 1e-05
ROPE_BASE = 10000.0


def round_plain(value):
    return lax.optimization_barrier(value.astype(jnp.bfloat16)).astype(jnp.float32)


def round_keep(value):
    return (round_plain(value), None)


def round_pass(kept, grad):
    return (grad,)


def make_rounder():
    rounder = jax.custom_vjp(round_plain)
    rounder.defvjp(round_keep, round_pass)
    return rounder


def rotate(head_rows, positions):
    half_width = head_rows.shape[-1] // 2
    frequency = ROPE_BASE ** (-jnp.arange(half_width).astype(jnp.float32) / half_width)
    angles = positions.astype(jnp.float32)[:, None] * frequency[None, :]
    cosine = jnp.cos(angles)[:, None, :]
    sine_part = jnp.sin(angles)[:, None, :]
    lead_half = head_rows[..., :half_width]
    tail_half = head_rows[..., half_width:]
    return jnp.concatenate(
        [lead_half * cosine - tail_half * sine_part, tail_half * cosine + lead_half * sine_part],
        axis=-1,
    )


def causal_conv(channels, segment, conv_weight, conv_bias):
    length = channels.shape[0]
    summed = jnp.broadcast_to(conv_bias[None, :], channels.shape)
    for offset in range(CONV):
        shifted = jnp.pad(channels, ((offset, 0), (0, 0)))[:length]
        earlier = jnp.pad(segment, (offset, 0), constant_values=-1)[:length]
        keep_mask = (earlier == segment).astype(jnp.float32)
        summed = summed + conv_weight[CONV - 1 - offset][None, :] * shifted * keep_mask[:, None]
    return jax.nn.silu(summed)


def ssd_scan(x_heads, log_decay, step_size, b_rows, c_rows, segment):
    length, head_count, head_width = x_heads.shape
    block_count = length // SPAN
    seq_items = (
        x_heads.reshape(block_count, SPAN, head_count, head_width),
        log_decay.reshape(block_count, SPAN, head_count),
        step_size.reshape(block_count, SPAN, head_count),
        b_rows.reshape(block_count, SPAN, STATE),
        c_rows.reshape(block_count, SPAN, STATE),
        segment.reshape(block_count, SPAN),
    )
    lower_mask = jnp.tril(jnp.ones((SPAN, SPAN), dtype=bool))

    def block_step(block_carry, block_items):
        ssm_state, last_segment = block_carry
        x_block, decay_block, step_block, b_block, c_block, seg_block = block_items
        cumulative = jnp.cumsum(decay_block, axis=0)
        same_doc = ((seg_block[:, None] == seg_block[None, :]) & lower_mask)[:, :, None]
        decay_gap = cumulative[:, None, :] - cumulative[None, :, :]
        inner_weight = jnp.where(same_doc, jnp.exp(jnp.where(same_doc, decay_gap, 0.0)), 0.0)
        block_scores = jnp.dot(c_block, b_block.T, precision=PRECISE)
        mixing = inner_weight * block_scores[:, :, None] * step_block[None, :, :]
        y_inner = jnp.einsum("tsh,shp->thp", mixing, x_block, precision=PRECISE)
        carry_keep = (seg_block == last_segment).astype(jnp.float32)
        state_weight = jnp.exp(cumulative) * carry_keep[:, None]
        from_state = (
            jnp.einsum("tn,hpn->thp", c_block, ssm_state, precision=PRECISE)
            * state_weight[:, :, None]
        )
        end_keep = (seg_block == seg_block[-1]).astype(jnp.float32)
        input_weight = (
            jnp.exp(cumulative[-1][None, :] - cumulative) * step_block * end_keep[:, None]
        )
        state_keep = jnp.exp(cumulative[-1]) * (seg_block[-1] == last_segment).astype(jnp.float32)
        new_state = ssm_state * state_keep[:, None, None] + jnp.einsum(
            "sh,shp,sn->hpn", input_weight, x_block, b_block, precision=PRECISE
        )
        return ((new_state, seg_block[-1]), y_inner + from_state)

    start_carry = (
        jnp.zeros((head_count, head_width, STATE), jnp.float32),
        jnp.array(-1, jnp.int32),
    )
    unused, y_blocks = lax.scan(jax.checkpoint(block_step), start_carry, seq_items)
    return y_blocks.reshape(length, head_count, head_width)


def attend(q_rot, k_rot, value_heads, segment):
    length, head_count, head_width = q_rot.shape
    block_count = length // ATT_BLOCK
    positions = jnp.arange(length, dtype=jnp.int32)
    rounder = make_rounder()

    def one_block(block_index):
        first_row = block_index * ATT_BLOCK
        q_block = lax.dynamic_slice_in_dim(q_rot, first_row, ATT_BLOCK, 0)
        seg_query = lax.dynamic_slice_in_dim(segment, first_row, ATT_BLOCK, 0)
        pos_query = first_row + jnp.arange(ATT_BLOCK, dtype=jnp.int32)
        scores = jnp.einsum("qhe,khe->hqk", q_block, k_rot, precision=PRECISE) * head_width ** (
            -0.5
        )
        allowed = (pos_query[:, None] >= positions[None, :]) & (
            seg_query[:, None] == segment[None, :]
        )
        scores = jnp.where(allowed[None, :, :], scores, -1e30)
        attn_probs = rounder(jax.nn.softmax(scores, axis=-1))
        return jnp.einsum("hqk,khe->qhe", attn_probs, value_heads, precision=PRECISE)

    blocks = lax.map(jax.checkpoint(one_block), jnp.arange(block_count, dtype=jnp.int32))
    return blocks.reshape(length, head_count, head_width)


def mixer_heads(
    x_part,
    dt_part,
    query_rows,
    key_rep,
    value_rep,
    bc_part,
    segment,
    conv_weight,
    conv_bias,
    log_rate,
    step_bias,
    skip_gain,
):
    rounder = make_rounder()
    length = x_part.shape[0]
    inner_width = x_part.shape[1]
    head_count = dt_part.shape[1]
    conv_out = rounder(
        causal_conv(jnp.concatenate([x_part, bc_part], axis=1), segment, conv_weight, conv_bias)
    )
    x_heads = conv_out[:, :inner_width].reshape(length, head_count, inner_width // head_count)
    b_rows = conv_out[:, inner_width : inner_width + STATE]
    c_rows = conv_out[:, inner_width + STATE :]
    step_size = jax.nn.softplus(dt_part + step_bias[None, :])
    log_decay = -jnp.exp(log_rate)[None, :] * step_size
    y_heads = (
        ssd_scan(x_heads, log_decay, step_size, b_rows, c_rows, segment)
        + skip_gain[None, :, None] * x_heads
    )
    y_rows = rounder(y_heads.reshape(length, inner_width))
    positions = jnp.arange(length, dtype=jnp.int32)
    query_heads = query_rows.shape[1] // HEAD_DIM
    q_rot = rounder(rotate(query_rows.reshape(length, query_heads, HEAD_DIM), positions))
    k_rot = rounder(rotate(key_rep.reshape(length, query_heads, HEAD_DIM), positions))
    attended = attend(q_rot, k_rot, value_rep.reshape(length, query_heads, HEAD_DIM), segment)
    attended = rounder(attended.reshape(length, query_heads * HEAD_DIM))
    return (y_rows, attended)


def norm_forward(token_rows, gain_vec):
    inv_scale = lax.rsqrt(jnp.mean(token_rows * token_rows, axis=-1, keepdims=True) + EPSILON)
    return (token_rows * inv_scale * gain_vec, inv_scale)


def norm_backward(token_rows, inv_scale, gain_vec, grad_rows):
    normed = token_rows * inv_scale
    gain_grad = jnp.sum(normed * grad_rows, axis=0)
    weighted = grad_rows * gain_vec
    row_grad = inv_scale * (weighted - normed * jnp.mean(weighted * normed, axis=-1, keepdims=True))
    return (row_grad, gain_grad)


def repeat_heads(kv_rows, groups):
    length = kv_rows.shape[0]
    shaped = kv_rows.reshape(length, -1, 1, HEAD_DIM)
    return jnp.broadcast_to(shaped, (length, shaped.shape[1], groups, HEAD_DIM)).reshape(length, -1)


def fold_heads(rep_rows, groups):
    length = rep_rows.shape[0]
    summed = jnp.sum(rep_rows.astype(jnp.float32).reshape(length, -1, groups, HEAD_DIM), axis=2)
    return summed.reshape(length, -1).astype(jnp.bfloat16)


def matmul_rows(left, right):
    return jnp.einsum("tc,cd->td", left, right, preferred_element_type=jnp.float32)


def matmul_back(left, right):
    return jnp.einsum("td,cd->tc", left, right, preferred_element_type=jnp.float32)


def weight_grad(left, right):
    return jnp.einsum("tc,td->cd", left, right, preferred_element_type=jnp.float32)


def peers(count, flip):
    return [(i, i ^ flip) for i in range(count)]


def gather_tokens(rows):
    count = lax.axis_size("seq")
    index = lax.axis_index("seq")
    tokens = rows.shape[0]
    whole = jnp.zeros((count * tokens, rows.shape[1]), rows.dtype)
    for flip in range(count):
        part = rows if flip == 0 else lax.ppermute(rows, "seq", peers(count, flip))
        whole = lax.dynamic_update_slice_in_dim(whole, part, (index ^ flip) * tokens, 0)
    return whole


def scatter_tokens(product):
    count = lax.axis_size("seq")
    index = lax.axis_index("seq")
    arrived = []
    for flip in range(count - 1, 0, -1):
        part = product(index ^ flip).astype(jnp.bfloat16)
        arrived.append(lax.ppermute(part, "seq", peers(count, flip)))
    total = product(index)
    for part in arrived:
        total = total + part.astype(jnp.float32)
    return total


def add_small(vector):
    for axis in ("fsdp", "seq"):
        count = lax.axis_size(axis)
        flip = 1
        while flip < count:
            vector = vector + lax.ppermute(vector, axis, peers(count, flip))
            flip *= 2
    return vector


def spread_columns(stacked):
    mine = lax.all_to_all(stacked, "seq", split_axis=0, concat_axis=0, tiled=True)
    whole = lax.all_gather(mine.reshape(-1, mine.shape[-1]), "fsdp", axis=0, tiled=True)
    return whole


def collect_columns(grad):
    count = lax.axis_size("seq")
    part = lax.psum_scatter(grad.astype(jnp.bfloat16), "fsdp", scatter_dimension=0, tiled=True)
    part = part.reshape(count, -1, part.shape[-1])
    return lax.all_to_all(part, "seq", split_axis=0, concat_axis=0, tiled=True)


def collect_rows(grad):
    return lax.psum_scatter(
        grad.astype(jnp.bfloat16), "fsdp", scatter_dimension=0, tiled=True
    ).astype(jnp.float32)


def to_gathered(rows):
    seq, fsdp = lax.axis_size("seq"), lax.axis_size("fsdp")
    shape = rows.shape
    split = rows.reshape(shape[:-1] + (seq, fsdp, -1))
    return jnp.swapaxes(split, -3, -2).reshape(shape)


def from_gathered(rows):
    seq, fsdp = lax.axis_size("seq"), lax.axis_size("fsdp")
    shape = rows.shape
    split = rows.reshape(shape[:-1] + (fsdp, seq, -1))
    return jnp.swapaxes(split, -3, -2).reshape(shape)


def inv_rms(token_rows):
    return lax.rsqrt(jnp.mean(token_rows * token_rows, axis=-1, keepdims=True) + EPSILON)


def on_device(
    inputs,
    cotangent,
    segments,
    norm_in,
    ssm_in,
    attn_in,
    conv_w,
    conv_b,
    a_log,
    dt_bias,
    d_skip,
    ssm_out,
    attn_out,
    norm_ffn,
    w_gate,
    w_up,
    w_down,
):
    f32, bf16 = jnp.float32, jnp.bfloat16
    seq = lax.axis_size("seq")
    fsdp = lax.axis_size("fsdp")
    index = lax.axis_index("seq")
    rows = ssm_in.shape[0]
    tokens = inputs.shape[2]
    heads = SSM_HEADS // seq
    inner = heads * SSM_DIM
    query_heads = Q_HEADS // seq
    q_width = query_heads * HEAD_DIM
    groups = Q_HEADS // KV_HEADS
    kv_of = [(s * query_heads) // groups for s in range(seq)]
    head_start = index * heads
    inner_start = index * inner
    rate_local = lax.dynamic_slice_in_dim(a_log.astype(f32), head_start, heads)
    bias_local = lax.dynamic_slice_in_dim(dt_bias.astype(f32), head_start, heads)
    skip_local = lax.dynamic_slice_in_dim(d_skip.astype(f32), head_start, heads)

    def by_seq(block):
        return jnp.swapaxes(block.reshape(rows, seq, -1), 0, 1)

    def for_all(block):
        return jnp.broadcast_to(block[None], (seq,) + block.shape)

    channels = conv_b.shape[0]
    conv_pack = jnp.concatenate([conv_w, conv_b[None]], axis=0).reshape(-1)
    conv_cols = -(-conv_pack.shape[0] // rows)
    conv_pack = jnp.pad(conv_pack, (0, conv_cols * rows - conv_pack.shape[0]))
    misc = jnp.concatenate([norm_in[:, None], norm_ffn[:, None], conv_pack.reshape(rows, conv_cols)], axis=1)
    misc_pad = -(heads + misc.shape[1]) % 128
    z_end, x_end, bc_end = SSM_INNER, 2 * SSM_INNER, 2 * SSM_INNER + 2 * STATE
    first_send = jnp.concatenate(
        [
            by_seq(ssm_in[:, z_end:x_end]),
            for_all(ssm_in[:, x_end:bc_end]),
            by_seq(ssm_in[:, bc_end:]),
            for_all(jnp.pad(misc, ((0, 0), (0, misc_pad)))),
        ],
        axis=2,
    )
    q_end = Q_HEADS * HEAD_DIM
    kv_end = q_end + KV_HEADS * HEAD_DIM

    def by_kv(block):
        return jnp.stack([block[:, h * HEAD_DIM : (h + 1) * HEAD_DIM] for h in kv_of])

    second_send = jnp.concatenate(
        [
            by_seq(ssm_in[:, :z_end]),
            by_seq(attn_in[:, :q_end]),
            by_kv(attn_in[:, q_end:kv_end]),
            by_kv(attn_in[:, kv_end:]),
        ],
        axis=2,
    )
    ffn_send = jnp.concatenate([by_seq(w_gate), by_seq(w_up)], axis=2)
    first_w = spread_columns(first_send)
    second_w = spread_columns(second_send)
    whole_ssm_out = lax.all_gather(ssm_out, "fsdp", axis=0, tiled=True)
    whole_attn_out = lax.all_gather(attn_out, "fsdp", axis=0, tiled=True)
    gate_up_w = spread_columns(ffn_send)
    down_w = lax.all_gather(w_down, "fsdp", axis=0, tiled=True)
    units = down_w.shape[0]

    misc_at = inner + 2 * STATE + heads
    small = first_w[:, misc_at : misc_at + misc.shape[1]]
    gain_in = small[:, 0].astype(f32)
    gain_ffn = from_gathered(small[:, 1].astype(f32))
    conv_all = small[:, 2:].reshape(fsdp, seq, -1)[:, :, : (CONV + 1) * channels]
    conv_all = conv_all.reshape(fsdp, seq, CONV + 1, channels).transpose(2, 1, 0, 3)
    conv_all = conv_all.reshape(CONV + 1, CONV_CH).astype(f32)
    conv_local = jnp.concatenate(
        [lax.dynamic_slice_in_dim(conv_all, inner_start, inner, 1), conv_all[:, SSM_INNER:]], axis=1
    )

    micro = range(MICRO)
    token_rows = [inputs[m, 0].astype(f32) for m in micro]
    rows_all = [gather_tokens(to_gathered(inputs[m, 0])) for m in micro]
    cot_all = [gather_tokens(cotangent[m, 0]) for m in micro]
    hidden_all, normed_all = [], []
    mixer_out, pullbacks, gate_zs, middles, dts = [], [], [], [], []
    for m in micro:
        segment = segments[m, 0]
        wide = rows_all[m].astype(f32)
        normed = wide * inv_rms(wide)
        hidden = (normed * gain_in).astype(bf16)
        hidden_all.append(hidden)
        first = matmul_rows(hidden, first_w).astype(bf16)
        second = matmul_rows(hidden, second_w)
        gate_z = second[:, :inner]
        attn_rows = second[:, inner:].astype(bf16).astype(f32)

        def local_mixer(x_part, dt_part, query, key, value, bc_part, weight, bias, rate, step_bias, skip):
            key_rep = jnp.tile(key, (1, query_heads))
            value_rep = jnp.tile(value, (1, query_heads))
            return mixer_heads(
                x_part, dt_part, query, key_rep, value_rep, bc_part, segment, weight, bias, rate, step_bias, skip
            )

        (y_rows, attended), pullback = jax.vjp(
            local_mixer,
            first[:, :inner].astype(f32),
            first[:, inner + 2 * STATE : inner + 2 * STATE + heads].astype(f32),
            attn_rows[:, :q_width],
            attn_rows[:, q_width : q_width + HEAD_DIM],
            attn_rows[:, q_width + HEAD_DIM :],
            first[:, inner : inner + 2 * STATE].astype(f32),
            conv_local[:CONV],
            conv_local[CONV],
            rate_local,
            bias_local,
            skip_local,
        )
        gate_zs.append(gate_z)
        pullbacks.append(pullback)
        gated = (y_rows * jax.nn.silu(gate_z)).astype(bf16)
        attended = attended.astype(bf16)
        mixer_out.append((y_rows, gated, attended))

        def mixed_rows(block):
            g = lax.dynamic_slice_in_dim(gated, block * tokens, tokens, 0)
            a = lax.dynamic_slice_in_dim(attended, block * tokens, tokens, 0)
            return matmul_rows(g, whole_ssm_out) + matmul_rows(a, whole_attn_out)

        middles.append(token_rows[m] + scatter_tokens(mixed_rows))

    outputs, grad_middles, ffn_grads = [], [], []
    gain_ffn_grad = 0.0
    for m in micro:
        middle = middles[m]
        scale = inv_rms(middle)
        normed = middle * scale
        hidden = gather_tokens(to_gathered((normed * gain_ffn).astype(bf16)))
        gate_up = matmul_rows(hidden, gate_up_w)
        gate_pre, up_pre = gate_up[:, :units], gate_up[:, units:]
        sig = jax.nn.sigmoid(gate_pre)
        activated = (gate_pre * sig * up_pre).astype(bf16)

        def out_rows(block):
            return matmul_rows(lax.dynamic_slice_in_dim(activated, block * tokens, tokens, 0), down_w)

        outputs.append((middle + scatter_tokens(out_rows)).astype(bf16))
        grad_act = matmul_back(cot_all[m], down_w)
        grad_up = grad_act * gate_pre * sig
        grad_gate = grad_act * up_pre * sig * (1.0 + gate_pre * (1.0 - sig))
        grad_gu = jnp.concatenate([grad_gate, grad_up], axis=1).astype(bf16)

        def hidden_rows(block):
            return matmul_back(lax.dynamic_slice_in_dim(grad_gu, block * tokens, tokens, 0), gate_up_w)

        grad_hidden = from_gathered(scatter_tokens(hidden_rows))
        gain_ffn_grad = gain_ffn_grad + jnp.sum(normed * grad_hidden, axis=0)
        weighted = grad_hidden * gain_ffn
        grad_norm = scale * (weighted - normed * jnp.mean(weighted * normed, axis=-1, keepdims=True))
        grad_middles.append(cotangent[m, 0].astype(f32) + grad_norm)
        ffn_grads.append((weight_grad(hidden, grad_gu), weight_grad(activated, cot_all[m])))
    gate_up_grad = collect_columns(ffn_grads[0][0] + ffn_grads[1][0])
    down_grad = collect_rows(ffn_grads[0][1] + ffn_grads[1][1])

    input_grads, mixer_grads = [], []
    conv_grad = rate_sum = bias_sum = skip_sum = gain_in_grad = 0.0
    for m in micro:
        y_rows, gated, attended = mixer_out[m]
        grad_mixed = gather_tokens(grad_middles[m].astype(bf16))
        grad_gated = matmul_back(grad_mixed, whole_ssm_out)
        grad_attended = matmul_back(grad_mixed, whole_attn_out).astype(bf16)
        gate_z = gate_zs[m]
        sig = jax.nn.sigmoid(gate_z)
        grad_y = (grad_gated * gate_z * sig).astype(bf16)
        grad_z = (grad_gated * y_rows * sig * (1.0 + gate_z * (1.0 - sig))).astype(bf16)
        (g_x, g_dt, g_query, g_key, g_value, g_bc, g_w, g_b, g_rate, g_bias, g_skip) = pullbacks[m](
            (grad_y.astype(f32), grad_attended.astype(f32))
        )
        conv_grad = conv_grad + jnp.concatenate([g_w, g_b[None]], axis=0)
        rate_sum, bias_sum, skip_sum = rate_sum + g_rate, bias_sum + g_bias, skip_sum + g_skip
        first_grad = jnp.concatenate([g_x, g_bc, g_dt], axis=1).astype(bf16)
        first_grad = jnp.pad(first_grad, ((0, 0), (0, first_w.shape[1] - first_grad.shape[1])))
        second_grad = jnp.concatenate(
            [grad_z, g_query.astype(bf16), g_key.astype(bf16), g_value.astype(bf16)], axis=1
        )

        def in_rows(block):
            one = lax.dynamic_slice_in_dim(first_grad, block * tokens, tokens, 0)
            two = lax.dynamic_slice_in_dim(second_grad, block * tokens, tokens, 0)
            return matmul_back(one, first_w) + matmul_back(two, second_w)

        grad_hidden = from_gathered(scatter_tokens(in_rows))
        gain_row = from_gathered(gain_in)
        scale = inv_rms(token_rows[m])
        normed = token_rows[m] * scale
        gain_in_grad = gain_in_grad + jnp.sum(normed * grad_hidden, axis=0)
        weighted = grad_hidden * gain_row
        grad_norm = scale * (weighted - normed * jnp.mean(weighted * normed, axis=-1, keepdims=True))
        input_grads.append((grad_middles[m] + grad_norm).astype(bf16))
        mixer_grads.append(
            (
                weight_grad(hidden_all[m], first_grad),
                weight_grad(hidden_all[m], second_grad),
                weight_grad(gated, grad_mixed),
                weight_grad(attended, grad_mixed),
            )
        )
    first_sum, second_sum, ssm_out_sum, attn_out_sum = (a + b for a, b in zip(*mixer_grads))
    ssm_out_grad = collect_rows(ssm_out_sum)
    attn_out_grad = collect_rows(attn_out_sum)
    second_back = collect_columns(second_sum).astype(f32)
    first_back = collect_columns(first_sum).astype(f32)

    def own_columns(block):
        return jnp.swapaxes(block, 0, 1).reshape(rows, -1)

    ssm_in_grad = jnp.concatenate(
        [
            own_columns(second_back[:, :, :inner]),
            own_columns(first_back[:, :, :inner]),
            jnp.sum(first_back[:, :, inner : inner + 2 * STATE], axis=0),
            own_columns(first_back[:, :, inner + 2 * STATE : inner + 2 * STATE + heads]),
        ],
        axis=1,
    )

    def kv_columns(block):
        return jnp.concatenate(
            [sum(block[s] for s in range(seq) if kv_of[s] == h) for h in range(KV_HEADS)], axis=1
        )

    attn_in_grad = jnp.concatenate(
        [
            own_columns(second_back[:, :, inner : inner + q_width]),
            kv_columns(second_back[:, :, inner + q_width : inner + q_width + HEAD_DIM]),
            kv_columns(second_back[:, :, inner + q_width + HEAD_DIM :]),
        ],
        axis=1,
    )
    gate_up_grad = gate_up_grad.astype(f32)
    gate_grad = own_columns(gate_up_grad[:, :, :units])
    up_grad = own_columns(gate_up_grad[:, :, units:])

    conv_whole = jnp.zeros((CONV + 1, CONV_CH), f32)
    conv_whole = lax.dynamic_update_slice_in_dim(conv_whole, conv_grad[:, :inner], inner_start, 1)
    conv_whole = lax.dynamic_update_slice_in_dim(conv_whole, conv_grad[:, inner:], SSM_INNER, 1)
    head_sums = lax.dynamic_update_slice_in_dim(
        jnp.zeros((3, SSM_HEADS), f32), jnp.stack([rate_sum, bias_sum, skip_sum]), head_start, 1
    )
    pieces = [conv_whole.reshape(-1), head_sums.reshape(-1), gain_in_grad, gain_ffn_grad]
    ends = [0]
    for piece in pieces:
        ends.append(ends[-1] + piece.shape[0])
    total = add_small(jnp.concatenate(pieces))
    conv_total, head_total, gain_in_total, gain_ffn_total = (
        total[a:b] for a, b in zip(ends[:-1], ends[1:])
    )
    place = index * fsdp + lax.axis_index("fsdp")
    conv_total = lax.dynamic_slice_in_dim(conv_total.reshape(CONV + 1, CONV_CH), place * channels, channels, 1)
    head_total = head_total.reshape(3, SSM_HEADS)
    return (
        jnp.stack(outputs)[:, None],
        jnp.stack(input_grads)[:, None],
        lax.dynamic_slice_in_dim(gain_in_total, place * rows, rows),
        ssm_in_grad,
        attn_in_grad,
        conv_total[:CONV],
        conv_total[CONV],
        head_total[0],
        head_total[1],
        head_total[2],
        ssm_out_grad,
        attn_out_grad,
        lax.dynamic_slice_in_dim(gain_ffn_total, place * rows, rows),
        gate_grad,
        up_grad,
        down_grad,
    )


def solution(mesh):
    return jax.shard_map(
        on_device,
        mesh=mesh,
        in_specs=(
            P(None, "fsdp", "seq", None),
            P(None, "fsdp", "seq", None),
            P(None, "fsdp", None),
            P(("seq", "fsdp")),
            P(("seq", "fsdp"), None),
            P(("seq", "fsdp"), None),
            P(None, ("seq", "fsdp")),
            P(("seq", "fsdp")),
            P(),
            P(),
            P(),
            P(("seq", "fsdp"), None),
            P(("seq", "fsdp"), None),
            P(("seq", "fsdp")),
            P(("seq", "fsdp"), None),
            P(("seq", "fsdp"), None),
            P(("seq", "fsdp"), None),
        ),
        out_specs=(
            P(None, "fsdp", "seq", None),
            P(None, "fsdp", "seq", None),
            P(("seq", "fsdp")),
            P(("seq", "fsdp"), None),
            P(("seq", "fsdp"), None),
            P(None, ("seq", "fsdp")),
            P(("seq", "fsdp")),
            P(),
            P(),
            P(),
            P(("seq", "fsdp"), None),
            P(("seq", "fsdp"), None),
            P(("seq", "fsdp")),
            P(("seq", "fsdp"), None),
            P(("seq", "fsdp"), None),
            P(("seq", "fsdp"), None),
        ),
        check_vma=False,
    )
```

```python
import functools

import jax
import jax.numpy as jnp
from jax import lax
from jax.experimental import pallas as pl
from jax.experimental.pallas import tpu as pltpu
from jax.sharding import PartitionSpec as P

SSM_HEADS = 48
SSM_DIM = 64
STATE = 256
CONV = 4
Q_HEADS = 8
KV_HEADS = 2
HEAD_DIM = 128
MICRO = 2
SPAN = 128
SSM_INNER = 3072
CONV_CH = 3584
ATT_ROWS = 256
VMEM_BYTES = 48 * 1024 * 1024


PRECISE = lax.Precision.HIGHEST
EPSILON = 1e-05
ROPE_BASE = 10000.0


def lanes_iota(shape):
    return lax.broadcasted_iota(jnp.int32, shape, 1)


def rows_iota(shape):
    return lax.broadcasted_iota(jnp.int32, shape, 0)


def dot_last(left, right):
    return lax.dot_general(left, right, (((1,), (1,)), ((), ())), preferred_element_type=jnp.float32)


def dot_first(left, right):
    return lax.dot_general(left, right, (((0,), (0,)), ((), ())), preferred_element_type=jnp.float32)


def dot_plain(left, right):
    return jnp.dot(left, right, preferred_element_type=jnp.float32)


def head_steps(block, head_ref, heads):
    pre = block.astype(jnp.float32) + head_ref[0:1, :]
    live = lanes_iota(pre.shape) < heads
    pre = jnp.where(live, pre, 0.0)
    step = jnp.maximum(pre, 0.0) + jnp.log1p(jnp.exp(-jnp.abs(pre)))
    step = jnp.where(live, step, 0.0)
    rate = -jnp.exp(head_ref[1:2, :])
    decay = rate * step
    lower = (rows_iota((SPAN, SPAN)) >= lanes_iota((SPAN, SPAN))).astype(jnp.float32)
    total = jnp.dot(lower, decay, precision=PRECISE, preferred_element_type=jnp.float32)
    return step, rate, decay, total, pre


def convolve(ubuf, aux_ref, conv_ref, lanes):
    acc = conv_ref[CONV : CONV + 1, lanes] + conv_ref[CONV - 1 : CONV, lanes] * ubuf[8 : 8 + SPAN, lanes]
    for offset in range(1, CONV):
        shifted = ubuf[8 - offset : 8 - offset + SPAN, lanes]
        weight = conv_ref[CONV - 1 - offset : CONV - offset, lanes]
        acc = acc + weight * shifted * aux_ref[:, 2 + offset : 3 + offset]
    return acc


def pair_of(values, first_head, low_lanes):
    one = jnp.broadcast_to(values[:, first_head : first_head + 1], (SPAN, 128))
    two = jnp.broadcast_to(values[:, first_head + 1 : first_head + 2], (SPAN, 128))
    return one, two, jnp.where(low_lanes, one, two)


def ssd_forward_kernel(
    heads, first_ref, aux_ref, seg_ref, conv_ref, head_ref, skip_ref, y_ref, start_ref, ubuf, taps, state
):
    f32, bf16 = jnp.float32, jnp.bfloat16
    inner = heads * SSM_DIM
    width = inner + 2 * STATE

    @pl.when(pl.program_id(0) == 0)
    def _():
        ubuf[SPAN : SPAN + 8, :] = jnp.zeros((8, width), f32)
        state[...] = jnp.zeros((STATE, inner), f32)

    ubuf[0:8, :] = ubuf[SPAN : SPAN + 8, :]
    ubuf[8 : 8 + SPAN, :] = first_ref[:, :width].astype(f32)
    for lane in range(0, width, 128):
        lanes = slice(lane, lane + 128)
        pre = convolve(ubuf, aux_ref, conv_ref, lanes)
        taps[:, lanes] = (pre * jax.nn.sigmoid(pre)).astype(bf16)
    step, rate, decay, total, unused = head_steps(first_ref[:, width : width + 128], head_ref, heads)
    total_rows = total.T
    low_lanes = lanes_iota((SPAN, 128)) < SSM_DIM
    same = (aux_ref[:, 0:1] == seg_ref[0]) & (rows_iota((SPAN, SPAN)) >= lanes_iota((SPAN, SPAN)))
    b_rows = taps[:, inner : inner + STATE]
    c_rows = taps[:, inner + STATE :]
    b_cols = b_rows.astype(f32).T.astype(bf16)
    scores = dot_last(c_rows, b_rows)
    carry_keep = aux_ref[:, 1:2]
    end_keep = aux_ref[:, 2:3]
    for pair in range(heads // 2):
        lanes = slice(pair * 128, pair * 128 + 128)
        sum_one, sum_two, sums = pair_of(total, 2 * pair, low_lanes)
        steps = pair_of(step, 2 * pair, low_lanes)[2]
        row_one = total_rows[2 * pair : 2 * pair + 1, :]
        row_two = total_rows[2 * pair + 1 : 2 * pair + 2, :]
        mix_one = (jnp.exp(jnp.where(same, sum_one - row_one, -1e30)) * scores).astype(bf16)
        mix_two = (jnp.exp(jnp.where(same, sum_two - row_two, -1e30)) * scores).astype(bf16)
        x = taps[:, lanes].astype(f32)
        stepped = (x * steps).astype(bf16)
        none = jnp.zeros_like(stepped)
        split = jnp.concatenate(
            [jnp.where(low_lanes, stepped, none), jnp.where(low_lanes, none, stepped)], axis=0
        )
        held = state[:, lanes]
        held_low = held.astype(bf16)
        start_ref[0, :, lanes] = held_low
        y = dot_plain(jnp.concatenate([mix_one, mix_two], axis=1), split)
        y = y + jnp.exp(sums) * carry_keep * dot_plain(c_rows, held_low)
        y_ref[:, lanes] = (y + skip_ref[0:1, lanes] * x).astype(bf16)
        last = sums[SPAN - 1 : SPAN, :]
        weighted = (jnp.exp(last - sums) * end_keep * stepped.astype(f32)).astype(bf16)
        kept = jnp.exp(last) * aux_ref[SPAN - 1 : SPAN, 1:2]
        state[:, lanes] = held * kept + dot_plain(b_cols, weighted)


def ssd_backward_kernel(
    heads,
    first_ref,
    before_ref,
    aux_ref,
    seg_ref,
    conv_ref,
    head_ref,
    skip_ref,
    start_ref,
    dy_ref,
    grad_ref,
    conv_grad_ref,
    head_grad_ref,
    skip_grad_ref,
    ubuf,
    taps,
    slope,
    gbuf,
    dstate,
):
    f32, bf16 = jnp.float32, jnp.bfloat16
    inner = heads * SSM_DIM
    width = inner + 2 * STATE

    @pl.when(pl.program_id(0) == 0)
    def _():
        gbuf[0:8, :] = jnp.zeros((8, width), f32)
        dstate[...] = jnp.zeros((STATE, inner), f32)
        conv_grad_ref[...] = jnp.zeros(conv_grad_ref.shape, f32)
        head_grad_ref[...] = jnp.zeros(head_grad_ref.shape, f32)
        skip_grad_ref[...] = jnp.zeros(skip_grad_ref.shape, f32)

    ubuf[0:8, :] = before_ref[8:16, :width].astype(f32)
    ubuf[8 : 8 + SPAN, :] = first_ref[:, :width].astype(f32)
    gbuf[SPAN : SPAN + 8, :] = gbuf[0:8, :]
    for lane in range(0, width, 128):
        lanes = slice(lane, lane + 128)
        pre = convolve(ubuf, aux_ref, conv_ref, lanes)
        sig = jax.nn.sigmoid(pre)
        taps[:, lanes] = (pre * sig).astype(bf16)
        slope[:, lanes] = sig * (1.0 + pre * (1.0 - sig))
    step, rate, decay, total, pre_step = head_steps(first_ref[:, width : width + 128], head_ref, heads)
    total_rows = total.T
    square = (SPAN, SPAN)
    low_lanes = lanes_iota((SPAN, 128)) < SSM_DIM
    low_row = lanes_iota((1, 128)) < SSM_DIM
    same = (aux_ref[:, 0:1] == seg_ref[0]) & (rows_iota(square) >= lanes_iota(square))
    b_rows = taps[:, inner : inner + STATE]
    c_rows = taps[:, inner + STATE :]
    c_cols = c_rows.astype(f32).T.astype(bf16)
    scores = dot_last(c_rows, b_rows)
    carry_keep = aux_ref[:, 1:2]
    end_keep = aux_ref[:, 2:3]
    head_lane = lanes_iota((SPAN, 128))
    is_last = rows_iota((SPAN, 1)) == SPAN - 1
    grad_scores = jnp.zeros(square, f32)
    grad_b = jnp.zeros((SPAN, STATE), f32)
    grad_c = jnp.zeros((SPAN, STATE), f32)
    grad_total = jnp.zeros((SPAN, 128), f32)
    grad_step = jnp.zeros((SPAN, 128), f32)
    for pair in range(heads // 2):
        lanes = slice(pair * 128, pair * 128 + 128)
        sum_one, sum_two, sums = pair_of(total, 2 * pair, low_lanes)
        steps = pair_of(step, 2 * pair, low_lanes)[2]
        row_one = total_rows[2 * pair : 2 * pair + 1, :]
        row_two = total_rows[2 * pair + 1 : 2 * pair + 2, :]
        decay_one = jnp.exp(jnp.where(same, sum_one - row_one, -1e30))
        decay_two = jnp.exp(jnp.where(same, sum_two - row_two, -1e30))
        mix_one = (decay_one * scores).astype(bf16)
        mix_two = (decay_two * scores).astype(bf16)
        x = taps[:, lanes].astype(f32)
        stepped = (x * steps).astype(bf16)
        none = jnp.zeros_like(stepped)
        x_one = jnp.where(low_lanes, stepped, none)
        x_two = jnp.where(low_lanes, none, stepped)
        dy_low = dy_ref[:, lanes]
        dy = dy_low.astype(f32)
        dy_one = jnp.where(low_lanes, dy_low, none)
        dy_two = jnp.where(low_lanes, none, dy_low)
        grad_scores = grad_scores + dot_last(dy_one, stepped) * decay_one + dot_last(dy_two, stepped) * decay_two
        y = dot_plain(
            jnp.concatenate([mix_one, mix_two], axis=1), jnp.concatenate([x_one, x_two], axis=0)
        )
        grad_in = dot_first(
            jnp.concatenate([mix_one, mix_two], axis=0), jnp.concatenate([dy_one, dy_two], axis=0)
        )
        held = start_ref[0, :, lanes]
        dheld = dstate[:, lanes]
        dheld_low = dheld.astype(bf16)
        grown = jnp.exp(sums) * carry_keep
        y = y + grown * dot_plain(c_rows, held)
        grown_dy = (grown * dy).astype(bf16)
        last = sums[SPAN - 1 : SPAN, :]
        fade = jnp.exp(last - sums) * end_keep
        stepped_wide = stepped.astype(f32)
        weighted = (fade * stepped_wide).astype(bf16)
        from_end = dot_plain(b_rows, dheld_low)
        grad_in = grad_in + fade * from_end
        grad_c = grad_c + dot_last(grown_dy, held)
        grad_b = grad_b + dot_last(weighted, dheld_low)
        kept = jnp.exp(last) * aux_ref[SPAN - 1 : SPAN, 1:2]
        ends = jnp.sum(fade * stepped_wide * from_end, axis=0, keepdims=True) + kept * jnp.sum(
            dheld * held.astype(f32), axis=0, keepdims=True
        )
        dstate[:, lanes] = dheld * kept + dot_plain(c_cols, grown_dy)
        gaps = dy * y - stepped_wide * grad_in
        by_step = x * grad_in
        for half in range(2):
            keep = low_lanes if half == 0 else ~low_lanes
            keep_row = low_row if half == 0 else ~low_row
            end_sum = jnp.sum(jnp.where(keep_row, ends, 0.0), axis=1, keepdims=True)
            gap_sum = jnp.sum(jnp.where(keep, gaps, 0.0), axis=1, keepdims=True)
            gap_sum = gap_sum + jnp.where(is_last, end_sum, 0.0)
            step_sum = jnp.sum(jnp.where(keep, by_step, 0.0), axis=1, keepdims=True)
            here = head_lane == 2 * pair + half
            grad_total = jnp.where(here, gap_sum, grad_total)
            grad_step = jnp.where(here, step_sum, grad_step)
        skip = skip_ref[0:1, lanes]
        skip_grad_ref[0:1, lanes] += jnp.sum(dy * x, axis=0, keepdims=True)
        gbuf[0:SPAN, lanes] = (steps * grad_in + skip * dy) * slope[:, lanes]
    low_scores = grad_scores.astype(bf16)
    grad_c = grad_c + dot_plain(low_scores, b_rows)
    grad_b = grad_b + dot_first(low_scores, c_rows)
    gbuf[0:SPAN, inner : inner + STATE] = grad_b * slope[:, inner : inner + STATE]
    gbuf[0:SPAN, inner + STATE : width] = grad_c * slope[:, inner + STATE : width]

    upper = (rows_iota(square) <= lanes_iota(square)).astype(f32)
    grad_decay = jnp.dot(upper, grad_total, precision=PRECISE, preferred_element_type=f32)
    grad_pre = (grad_step + rate * grad_decay) * jax.nn.sigmoid(pre_step)
    grad_pre = jnp.where(head_lane < heads, grad_pre, 0.0)
    grad_ref[:, width : width + 128] = grad_pre.astype(bf16)
    head_grad_ref[0:1, :] += jnp.sum(grad_decay * decay, axis=0, keepdims=True)
    head_grad_ref[1:2, :] += jnp.sum(grad_pre, axis=0, keepdims=True)

    for lane in range(0, width, 128):
        lanes = slice(lane, lane + 128)
        grad = gbuf[0:SPAN, lanes]
        conv_grad_ref[CONV : CONV + 1, lanes] += jnp.sum(grad, axis=0, keepdims=True)
        conv_grad_ref[CONV - 1 : CONV, lanes] += jnp.sum(grad * ubuf[8 : 8 + SPAN, lanes], axis=0, keepdims=True)
        acc = conv_ref[CONV - 1 : CONV, lanes] * grad
        for offset in range(1, CONV):
            at = CONV - 1 - offset
            shifted = ubuf[8 - offset : 8 - offset + SPAN, lanes] * aux_ref[:, 2 + offset : 3 + offset]
            conv_grad_ref[at : at + 1, lanes] += jnp.sum(grad * shifted, axis=0, keepdims=True)
            later = gbuf[offset : offset + SPAN, lanes] * aux_ref[:, 5 + offset : 6 + offset]
            acc = acc + conv_ref[at : at + 1, lanes] * later
        grad_ref[:, lanes] = acc.astype(bf16)


def token_aux(segment):
    length = segment.shape[0]
    ends = segment.reshape(-1, SPAN)[:, -1]
    end_of = jnp.repeat(ends, SPAN)
    before = jnp.repeat(jnp.concatenate([jnp.full((1,), -1, segment.dtype), ends[:-1]]), SPAN)
    columns = [segment, segment == before, segment == end_of]
    for offset in range(1, CONV):
        columns.append(jnp.pad(segment, (offset, 0), constant_values=-1)[:length] == segment)
    for offset in range(1, CONV):
        columns.append(jnp.pad(segment, (0, offset), constant_values=-1)[offset:] == segment)
    columns = [column.astype(jnp.float32) for column in columns]
    return jnp.stack(columns + [jnp.zeros((length,), jnp.float32)] * (16 - len(columns)), axis=1)


def ssd_specs(heads, wide, order):
    inner = heads * SSM_DIM
    width = inner + 2 * STATE
    return [
        pl.BlockSpec((SPAN, wide), lambda i: (order(i), 0)),
        pl.BlockSpec((SPAN, 16), lambda i: (order(i), 0)),
        pl.BlockSpec((1, 1, SPAN), lambda i: (order(i), 0, 0)),
        pl.BlockSpec((8, width), lambda i: (0, 0)),
        pl.BlockSpec((8, 128), lambda i: (0, 0)),
        pl.BlockSpec((8, inner), lambda i: (0, 0)),
    ]


def ssd_forward(first, aux, seg_rows, conv, head, skip, heads):
    length, wide = first.shape
    inner = heads * SSM_DIM
    width = inner + 2 * STATE
    blocks = length // SPAN
    return pl.pallas_call(
        functools.partial(ssd_forward_kernel, heads),
        grid=(blocks,),
        in_specs=ssd_specs(heads, wide, lambda i: i),
        out_specs=[
            pl.BlockSpec((SPAN, inner), lambda i: (i, 0)),
            pl.BlockSpec((1, STATE, inner), lambda i: (i, 0, 0)),
        ],
        out_shape=[
            jax.ShapeDtypeStruct((length, inner), jnp.bfloat16),
            jax.ShapeDtypeStruct((blocks, STATE, inner), jnp.bfloat16),
        ],
        scratch_shapes=[
            pltpu.VMEM((SPAN + 8, width), jnp.float32),
            pltpu.VMEM((SPAN, width), jnp.bfloat16),
            pltpu.VMEM((STATE, inner), jnp.float32),
        ],
        compiler_params=pltpu.CompilerParams(
            dimension_semantics=("arbitrary",), vmem_limit_bytes=VMEM_BYTES
        ),
        cost_estimate=pl.CostEstimate(
            flops=60_000_000_000 * heads // 12, bytes_accessed=12_000_000, transcendentals=4_000_000
        ),
        name="ssd_forward",
    )(first, aux, seg_rows, conv, head, skip)


def ssd_backward(first, aux, seg_rows, conv, head, skip, starts, dy, heads):
    length, wide = first.shape
    inner = heads * SSM_DIM
    width = inner + 2 * STATE
    blocks = length // SPAN
    specs = ssd_specs(heads, wide, lambda i: blocks - 1 - i)
    per_block = SPAN // 16
    specs.insert(
        1, pl.BlockSpec((16, wide), lambda i: (jnp.maximum((blocks - 1 - i) * per_block - 1, 0), 0))
    )
    specs += [
        pl.BlockSpec((1, STATE, inner), lambda i: (blocks - 1 - i, 0, 0)),
        pl.BlockSpec((SPAN, inner), lambda i: (blocks - 1 - i, 0)),
    ]
    return pl.pallas_call(
        functools.partial(ssd_backward_kernel, heads),
        grid=(blocks,),
        in_specs=specs,
        out_specs=[
            pl.BlockSpec((SPAN, wide), lambda i: (blocks - 1 - i, 0)),
            pl.BlockSpec((8, width), lambda i: (0, 0)),
            pl.BlockSpec((8, 128), lambda i: (0, 0)),
            pl.BlockSpec((8, inner), lambda i: (0, 0)),
        ],
        out_shape=[
            jax.ShapeDtypeStruct((length, wide), jnp.bfloat16),
            jax.ShapeDtypeStruct((8, width), jnp.float32),
            jax.ShapeDtypeStruct((8, 128), jnp.float32),
            jax.ShapeDtypeStruct((8, inner), jnp.float32),
        ],
        scratch_shapes=[
            pltpu.VMEM((SPAN + 8, width), jnp.float32),
            pltpu.VMEM((SPAN, width), jnp.bfloat16),
            pltpu.VMEM((SPAN, width), jnp.float32),
            pltpu.VMEM((SPAN + 8, width), jnp.float32),
            pltpu.VMEM((STATE, inner), jnp.float32),
        ],
        compiler_params=pltpu.CompilerParams(
            dimension_semantics=("arbitrary",), vmem_limit_bytes=VMEM_BYTES
        ),
        cost_estimate=pl.CostEstimate(
            flops=120_000_000_000 * heads // 12, bytes_accessed=16_000_000, transcendentals=5_000_000
        ),
        name="ssd_backward",
    )(first, first, aux, seg_rows, conv, head, skip, starts, dy)


def rotary_tables(length):
    half = HEAD_DIM // 2
    frequency = ROPE_BASE ** (-jnp.arange(half).astype(jnp.float32) / half)
    angles = jnp.arange(length, dtype=jnp.int32).astype(jnp.float32)[:, None] * frequency[None, :]
    cosine, sine = jnp.cos(angles), jnp.sin(angles)
    return jnp.concatenate([cosine, cosine], axis=1), jnp.concatenate([-sine, sine], axis=1)


def turn(rows, cosine, sine):
    wide = rows.astype(jnp.float32)
    return (wide * cosine + pltpu.roll(wide, HEAD_DIM // 2, 1) * sine).astype(jnp.bfloat16)


def turn_back(grads, cosine, sine):
    return (grads * cosine + pltpu.roll(grads * sine, HEAD_DIM // 2, 1)).astype(jnp.bfloat16)


def block_scores(q_block, k_part, first_row, seg_col, seg_row):
    scores = dot_last(q_block, k_part) * HEAD_DIM ** (-0.5)
    shape = scores.shape
    allowed = (rows_iota(shape) + first_row >= lanes_iota(shape)) & (seg_col == seg_row)
    return jnp.where(allowed, scores, -1e30)


def attend_forward_kernel(query_heads, block, qkv_ref, cos_ref, sin_ref, aux_ref, seg_ref, out_ref, lse_ref, k_rot):
    length = qkv_ref.shape[0]
    q_width = query_heads * HEAD_DIM
    k_rot[...] = turn(qkv_ref[:, q_width : q_width + HEAD_DIM], cos_ref[...], sin_ref[...])
    for start in range(0, length, block):
        rows = slice(start, start + block)
        end = start + block
        for head in range(query_heads):
            lanes = slice(head * HEAD_DIM, (head + 1) * HEAD_DIM)
            q_block = turn(qkv_ref[rows, lanes], cos_ref[rows, :], sin_ref[rows, :])
            scores = block_scores(q_block, k_rot[:end, :], start, aux_ref[rows, 0:1], seg_ref[:, :end])
            top = jnp.max(scores, axis=1, keepdims=True)
            raised = jnp.exp(scores - top)
            total = jnp.sum(raised, axis=1, keepdims=True)
            probs = (raised * (1.0 / total)).astype(jnp.bfloat16)
            value = qkv_ref[:end, q_width + HEAD_DIM :]
            out_ref[rows, lanes] = dot_plain(probs, value).astype(jnp.bfloat16)
            lse_ref[rows, head : head + 1] = top + jnp.log(total)


def attend_backward_kernel(
    query_heads, block, qkv_ref, cos_ref, sin_ref, aux_ref, seg_ref, lse_ref, grad_ref, out_ref, k_rot, dk, dv
):
    f32, bf16 = jnp.float32, jnp.bfloat16
    length = qkv_ref.shape[0]
    q_width = query_heads * HEAD_DIM
    k_rot[...] = turn(qkv_ref[:, q_width : q_width + HEAD_DIM], cos_ref[...], sin_ref[...])
    dk[...] = jnp.zeros(dk.shape, f32)
    dv[...] = jnp.zeros(dv.shape, f32)
    for start in range(0, length, block):
        rows = slice(start, start + block)
        end = start + block
        for head in range(query_heads):
            lanes = slice(head * HEAD_DIM, (head + 1) * HEAD_DIM)
            cosine, sine = cos_ref[rows, :], sin_ref[rows, :]
            q_block = turn(qkv_ref[rows, lanes], cosine, sine)
            scores = block_scores(q_block, k_rot[:end, :], start, aux_ref[rows, 0:1], seg_ref[:, :end])
            probs = jnp.exp(scores - lse_ref[rows, head : head + 1])
            grad = grad_ref[rows, lanes]
            grad_probs = dot_last(grad, qkv_ref[:end, q_width + HEAD_DIM :])
            mean = jnp.sum(grad_probs * probs, axis=1, keepdims=True)
            grad_scores = (probs * (grad_probs - mean) * HEAD_DIM ** (-0.5)).astype(bf16)
            out_ref[rows, lanes] = turn_back(dot_plain(grad_scores, k_rot[:end, :]), cosine, sine)
            dk[:end, :] += dot_first(grad_scores, q_block)
            dv[:end, :] += dot_first(probs.astype(bf16), grad)
    out_ref[:, q_width : q_width + HEAD_DIM] = turn_back(dk[...], cos_ref[...], sin_ref[...])
    out_ref[:, q_width + HEAD_DIM :] = dv[...].astype(bf16)


def attend_forward(qkv, tables, aux, seg_row, query_heads):
    length = qkv.shape[0]
    return pl.pallas_call(
        functools.partial(attend_forward_kernel, query_heads, min(ATT_ROWS, length)),
        out_shape=[
            jax.ShapeDtypeStruct((length, query_heads * HEAD_DIM), jnp.bfloat16),
            jax.ShapeDtypeStruct((length, 8), jnp.float32),
        ],
        scratch_shapes=[pltpu.VMEM((length, HEAD_DIM), jnp.bfloat16)],
        compiler_params=pltpu.CompilerParams(vmem_limit_bytes=VMEM_BYTES),
        cost_estimate=pl.CostEstimate(
            flops=8_000_000_000 * query_heads, bytes_accessed=4_000_000, transcendentals=1_000_000
        ),
        name="attend_forward",
    )(qkv, tables[0], tables[1], aux, seg_row)


def attend_backward(qkv, tables, aux, seg_row, lse, grad, query_heads):
    length = qkv.shape[0]
    return pl.pallas_call(
        functools.partial(attend_backward_kernel, query_heads, min(ATT_ROWS, length)),
        out_shape=jax.ShapeDtypeStruct(qkv.shape, jnp.bfloat16),
        scratch_shapes=[
            pltpu.VMEM((length, HEAD_DIM), jnp.bfloat16),
            pltpu.VMEM((length, HEAD_DIM), jnp.float32),
            pltpu.VMEM((length, HEAD_DIM), jnp.float32),
        ],
        compiler_params=pltpu.CompilerParams(vmem_limit_bytes=VMEM_BYTES),
        cost_estimate=pl.CostEstimate(
            flops=20_000_000_000 * query_heads, bytes_accessed=6_000_000, transcendentals=1_000_000
        ),
        name="attend_backward",
    )(qkv, tables[0], tables[1], aux, seg_row, lse, grad)


def matmul_rows(left, right):
    return jnp.einsum("tc,cd->td", left, right, preferred_element_type=jnp.float32)


def matmul_back(left, right):
    return jnp.einsum("td,cd->tc", left, right, preferred_element_type=jnp.float32)


def weight_grad(left, right):
    return jnp.einsum("tc,td->cd", left, right, preferred_element_type=jnp.float32)


def peers(count, flip):
    return [(i, i ^ flip) for i in range(count)]


def gather_tokens(rows):
    count = lax.axis_size("seq")
    index = lax.axis_index("seq")
    tokens = rows.shape[0]
    whole = jnp.zeros((count * tokens, rows.shape[1]), rows.dtype)
    for flip in range(count):
        part = rows if flip == 0 else lax.ppermute(rows, "seq", peers(count, flip))
        whole = lax.dynamic_update_slice_in_dim(whole, part, (index ^ flip) * tokens, 0)
    return whole


def scatter_tokens(product):
    count = lax.axis_size("seq")
    index = lax.axis_index("seq")
    arrived = []
    for flip in range(count - 1, 0, -1):
        part = product(index ^ flip).astype(jnp.bfloat16)
        arrived.append(lax.ppermute(part, "seq", peers(count, flip)))
    total = product(index)
    for part in arrived:
        total = total + part.astype(jnp.float32)
    return total


def add_small(vector):
    for axis in ("fsdp", "seq"):
        count = lax.axis_size(axis)
        flip = 1
        while flip < count:
            vector = vector + lax.ppermute(vector, axis, peers(count, flip))
            flip *= 2
    return vector


def spread_columns(stacked):
    mine = lax.all_to_all(stacked, "seq", split_axis=0, concat_axis=0, tiled=True)
    whole = lax.all_gather(mine.reshape(-1, mine.shape[-1]), "fsdp", axis=0, tiled=True)
    return whole


def collect_columns(grad):
    count = lax.axis_size("seq")
    part = lax.psum_scatter(grad.astype(jnp.bfloat16), "fsdp", scatter_dimension=0, tiled=True)
    part = part.reshape(count, -1, part.shape[-1])
    return lax.all_to_all(part, "seq", split_axis=0, concat_axis=0, tiled=True)


def collect_rows(grad):
    return lax.psum_scatter(
        grad.astype(jnp.bfloat16), "fsdp", scatter_dimension=0, tiled=True
    ).astype(jnp.float32)


def to_gathered(rows):
    seq, fsdp = lax.axis_size("seq"), lax.axis_size("fsdp")
    shape = rows.shape
    split = rows.reshape(shape[:-1] + (seq, fsdp, -1))
    return jnp.swapaxes(split, -3, -2).reshape(shape)


def from_gathered(rows):
    seq, fsdp = lax.axis_size("seq"), lax.axis_size("fsdp")
    shape = rows.shape
    split = rows.reshape(shape[:-1] + (fsdp, seq, -1))
    return jnp.swapaxes(split, -3, -2).reshape(shape)


def inv_rms(token_rows):
    return lax.rsqrt(jnp.mean(token_rows * token_rows, axis=-1, keepdims=True) + EPSILON)


def on_device(
    inputs,
    cotangent,
    segments,
    norm_in,
    ssm_in,
    attn_in,
    conv_w,
    conv_b,
    a_log,
    dt_bias,
    d_skip,
    ssm_out,
    attn_out,
    norm_ffn,
    w_gate,
    w_up,
    w_down,
):
    f32, bf16 = jnp.float32, jnp.bfloat16
    seq = lax.axis_size("seq")
    fsdp = lax.axis_size("fsdp")
    index = lax.axis_index("seq")
    rows = ssm_in.shape[0]
    tokens = inputs.shape[2]
    heads = SSM_HEADS // seq
    inner = heads * SSM_DIM
    query_heads = Q_HEADS // seq
    q_width = query_heads * HEAD_DIM
    groups = Q_HEADS // KV_HEADS
    kv_of = [(s * query_heads) // groups for s in range(seq)]
    head_start = index * heads
    inner_start = index * inner
    rate_local = lax.dynamic_slice_in_dim(a_log.astype(f32), head_start, heads)
    bias_local = lax.dynamic_slice_in_dim(dt_bias.astype(f32), head_start, heads)
    skip_local = lax.dynamic_slice_in_dim(d_skip.astype(f32), head_start, heads)

    def by_seq(block):
        return jnp.swapaxes(block.reshape(rows, seq, -1), 0, 1)

    def for_all(block):
        return jnp.broadcast_to(block[None], (seq,) + block.shape)

    channels = conv_b.shape[0]
    conv_pack = jnp.concatenate([conv_w, conv_b[None]], axis=0).reshape(-1)
    conv_cols = -(-conv_pack.shape[0] // rows)
    conv_pack = jnp.pad(conv_pack, (0, conv_cols * rows - conv_pack.shape[0]))
    misc = jnp.concatenate([norm_in[:, None], norm_ffn[:, None], conv_pack.reshape(rows, conv_cols)], axis=1)
    misc_pad = -(heads + misc.shape[1]) % 128
    z_end, x_end, bc_end = SSM_INNER, 2 * SSM_INNER, 2 * SSM_INNER + 2 * STATE
    first_send = jnp.concatenate(
        [
            by_seq(ssm_in[:, z_end:x_end]),
            for_all(ssm_in[:, x_end:bc_end]),
            by_seq(ssm_in[:, bc_end:]),
            for_all(jnp.pad(misc, ((0, 0), (0, misc_pad)))),
        ],
        axis=2,
    )
    q_end = Q_HEADS * HEAD_DIM
    kv_end = q_end + KV_HEADS * HEAD_DIM

    def by_kv(block):
        return jnp.stack([block[:, h * HEAD_DIM : (h + 1) * HEAD_DIM] for h in kv_of])

    second_send = jnp.concatenate(
        [
            by_seq(ssm_in[:, :z_end]),
            by_seq(attn_in[:, :q_end]),
            by_kv(attn_in[:, q_end:kv_end]),
            by_kv(attn_in[:, kv_end:]),
        ],
        axis=2,
    )
    ffn_send = jnp.concatenate([by_seq(w_gate), by_seq(w_up)], axis=2)
    first_w = spread_columns(first_send)
    second_w = spread_columns(second_send)
    whole_ssm_out = lax.all_gather(ssm_out, "fsdp", axis=0, tiled=True)
    whole_attn_out = lax.all_gather(attn_out, "fsdp", axis=0, tiled=True)
    gate_up_w = spread_columns(ffn_send)
    down_w = lax.all_gather(w_down, "fsdp", axis=0, tiled=True)
    units = down_w.shape[0]

    misc_at = inner + 2 * STATE + heads
    small = first_w[:, misc_at : misc_at + misc.shape[1]]
    gain_in = small[:, 0].astype(f32)
    gain_ffn = from_gathered(small[:, 1].astype(f32))
    conv_all = small[:, 2:].reshape(fsdp, seq, -1)[:, :, : (CONV + 1) * channels]
    conv_all = conv_all.reshape(fsdp, seq, CONV + 1, channels).transpose(2, 1, 0, 3)
    conv_all = conv_all.reshape(CONV + 1, CONV_CH).astype(f32)
    conv_local = jnp.concatenate(
        [lax.dynamic_slice_in_dim(conv_all, inner_start, inner, 1), conv_all[:, SSM_INNER:]], axis=1
    )

    conv_table = jnp.pad(conv_local, ((0, 8 - CONV - 1), (0, 0)))
    head_table = jnp.pad(jnp.stack([bias_local, rate_local]), ((0, 6), (0, 128 - heads)))
    skip_table = jnp.broadcast_to(jnp.repeat(skip_local, SSM_DIM)[None], (8, inner))
    tables = rotary_tables(segments.shape[2])
    z_w, qkv_w = second_w[:, :inner], second_w[:, inner:]

    micro = range(MICRO)
    token_rows = [inputs[m, 0].astype(f32) for m in micro]
    rows_all = [gather_tokens(to_gathered(inputs[m, 0])) for m in micro]
    cot_all = [gather_tokens(cotangent[m, 0]) for m in micro]
    hidden_all, normed_all = [], []
    mixer_out, kept, gate_zs, middles = [], [], [], []
    for m in micro:
        segment = segments[m, 0]
        aux = token_aux(segment)
        seg_float = segment.astype(f32)
        seg_blocks, seg_row = seg_float.reshape(-1, 1, SPAN), seg_float[None]
        wide = rows_all[m].astype(f32)
        normed = wide * inv_rms(wide)
        hidden = (normed * gain_in).astype(bf16)
        hidden_all.append(hidden)
        first = matmul_rows(hidden, first_w).astype(bf16)
        gate_z = matmul_rows(hidden, z_w)
        qkv = matmul_rows(hidden, qkv_w).astype(bf16)
        y_rows, starts = ssd_forward(first, aux, seg_blocks, conv_table, head_table, skip_table, heads)
        attended, lse = attend_forward(qkv, tables, aux, seg_row, query_heads)
        gate_zs.append(gate_z)
        kept.append((first, aux, seg_blocks, seg_row, starts, qkv, lse))
        gated = (y_rows.astype(f32) * jax.nn.silu(gate_z)).astype(bf16)
        mixer_out.append((y_rows, gated, attended))

        def mixed_rows(block):
            g = lax.dynamic_slice_in_dim(gated, block * tokens, tokens, 0)
            a = lax.dynamic_slice_in_dim(attended, block * tokens, tokens, 0)
            return matmul_rows(g, whole_ssm_out) + matmul_rows(a, whole_attn_out)

        middles.append(token_rows[m] + scatter_tokens(mixed_rows))

    outputs, grad_middles, ffn_grads = [], [], []
    gain_ffn_grad = 0.0
    for m in micro:
        middle = middles[m]
        scale = inv_rms(middle)
        normed = middle * scale
        hidden = gather_tokens(to_gathered((normed * gain_ffn).astype(bf16)))
        gate_up = matmul_rows(hidden, gate_up_w)
        gate_pre, up_pre = gate_up[:, :units], gate_up[:, units:]
        sig = jax.nn.sigmoid(gate_pre)
        activated = (gate_pre * sig * up_pre).astype(bf16)

        def out_rows(block):
            return matmul_rows(lax.dynamic_slice_in_dim(activated, block * tokens, tokens, 0), down_w)

        outputs.append((middle + scatter_tokens(out_rows)).astype(bf16))
        grad_act = matmul_back(cot_all[m], down_w)
        grad_up = grad_act * gate_pre * sig
        grad_gate = grad_act * up_pre * sig * (1.0 + gate_pre * (1.0 - sig))
        grad_gu = jnp.concatenate([grad_gate, grad_up], axis=1).astype(bf16)

        def hidden_rows(block):
            return matmul_back(lax.dynamic_slice_in_dim(grad_gu, block * tokens, tokens, 0), gate_up_w)

        grad_hidden = from_gathered(scatter_tokens(hidden_rows))
        gain_ffn_grad = gain_ffn_grad + jnp.sum(normed * grad_hidden, axis=0)
        weighted = grad_hidden * gain_ffn
        grad_norm = scale * (weighted - normed * jnp.mean(weighted * normed, axis=-1, keepdims=True))
        grad_middles.append(cotangent[m, 0].astype(f32) + grad_norm)
        ffn_grads.append((weight_grad(hidden, grad_gu), weight_grad(activated, cot_all[m])))
    gate_up_grad = collect_columns(ffn_grads[0][0] + ffn_grads[1][0])
    down_grad = collect_rows(ffn_grads[0][1] + ffn_grads[1][1])

    input_grads, mixer_grads = [], []
    conv_grad = rate_sum = bias_sum = skip_sum = gain_in_grad = 0.0
    for m in micro:
        y_rows, gated, attended = mixer_out[m]
        grad_mixed = gather_tokens(grad_middles[m].astype(bf16))
        grad_gated = matmul_back(grad_mixed, whole_ssm_out)
        grad_attended = matmul_back(grad_mixed, whole_attn_out).astype(bf16)
        gate_z = gate_zs[m]
        sig = jax.nn.sigmoid(gate_z)
        grad_y = (grad_gated * gate_z * sig).astype(bf16)
        y_wide = y_rows.astype(f32)
        grad_z = (grad_gated * y_wide * sig * (1.0 + gate_z * (1.0 - sig))).astype(bf16)
        first, aux, seg_blocks, seg_row, starts, qkv, lse = kept[m]
        grad_qkv = attend_backward(qkv, tables, aux, seg_row, lse, grad_attended, query_heads)
        first_grad, g_conv, g_head, g_skip = ssd_backward(
            first, aux, seg_blocks, conv_table, head_table, skip_table, starts, grad_y, heads
        )
        conv_grad = conv_grad + g_conv[: CONV + 1]
        rate_sum, bias_sum = rate_sum + g_head[0, :heads], bias_sum + g_head[1, :heads]
        skip_sum = skip_sum + jnp.sum(g_skip[0].reshape(heads, SSM_DIM), axis=1)

        def in_rows(block):
            one = lax.dynamic_slice_in_dim(first_grad, block * tokens, tokens, 0)
            two = lax.dynamic_slice_in_dim(grad_z, block * tokens, tokens, 0)
            three = lax.dynamic_slice_in_dim(grad_qkv, block * tokens, tokens, 0)
            return matmul_back(one, first_w) + matmul_back(two, z_w) + matmul_back(three, qkv_w)

        grad_hidden = from_gathered(scatter_tokens(in_rows))
        gain_row = from_gathered(gain_in)
        scale = inv_rms(token_rows[m])
        normed = token_rows[m] * scale
        gain_in_grad = gain_in_grad + jnp.sum(normed * grad_hidden, axis=0)
        weighted = grad_hidden * gain_row
        grad_norm = scale * (weighted - normed * jnp.mean(weighted * normed, axis=-1, keepdims=True))
        input_grads.append((grad_middles[m] + grad_norm).astype(bf16))
        mixer_grads.append(
            (
                weight_grad(hidden_all[m], first_grad),
                weight_grad(hidden_all[m], grad_z),
                weight_grad(hidden_all[m], grad_qkv),
                weight_grad(gated, grad_mixed),
                weight_grad(attended, grad_mixed),
            )
        )
    first_sum, z_sum, qkv_sum, ssm_out_sum, attn_out_sum = (a + b for a, b in zip(*mixer_grads))
    ssm_out_grad = collect_rows(ssm_out_sum)
    attn_out_grad = collect_rows(attn_out_sum)
    z_back = collect_columns(z_sum).astype(f32)
    qkv_back = collect_columns(qkv_sum).astype(f32)
    first_back = collect_columns(first_sum).astype(f32)

    def own_columns(block):
        return jnp.swapaxes(block, 0, 1).reshape(rows, -1)

    ssm_in_grad = jnp.concatenate(
        [
            own_columns(z_back),
            own_columns(first_back[:, :, :inner]),
            jnp.sum(first_back[:, :, inner : inner + 2 * STATE], axis=0),
            own_columns(first_back[:, :, inner + 2 * STATE : inner + 2 * STATE + heads]),
        ],
        axis=1,
    )

    def kv_columns(block):
        return jnp.concatenate(
            [sum(block[s] for s in range(seq) if kv_of[s] == h) for h in range(KV_HEADS)], axis=1
        )

    attn_in_grad = jnp.concatenate(
        [
            own_columns(qkv_back[:, :, :q_width]),
            kv_columns(qkv_back[:, :, q_width : q_width + HEAD_DIM]),
            kv_columns(qkv_back[:, :, q_width + HEAD_DIM :]),
        ],
        axis=1,
    )
    gate_up_grad = gate_up_grad.astype(f32)
    gate_grad = own_columns(gate_up_grad[:, :, :units])
    up_grad = own_columns(gate_up_grad[:, :, units:])

    conv_whole = jnp.zeros((CONV + 1, CONV_CH), f32)
    conv_whole = lax.dynamic_update_slice_in_dim(conv_whole, conv_grad[:, :inner], inner_start, 1)
    conv_whole = lax.dynamic_update_slice_in_dim(conv_whole, conv_grad[:, inner:], SSM_INNER, 1)
    head_sums = lax.dynamic_update_slice_in_dim(
        jnp.zeros((3, SSM_HEADS), f32), jnp.stack([rate_sum, bias_sum, skip_sum]), head_start, 1
    )
    pieces = [conv_whole.reshape(-1), head_sums.reshape(-1), gain_in_grad, gain_ffn_grad]
    ends = [0]
    for piece in pieces:
        ends.append(ends[-1] + piece.shape[0])
    total = add_small(jnp.concatenate(pieces))
    conv_total, head_total, gain_in_total, gain_ffn_total = (
        total[a:b] for a, b in zip(ends[:-1], ends[1:])
    )
    place = index * fsdp + lax.axis_index("fsdp")
    conv_total = lax.dynamic_slice_in_dim(conv_total.reshape(CONV + 1, CONV_CH), place * channels, channels, 1)
    head_total = head_total.reshape(3, SSM_HEADS)
    return (
        jnp.stack(outputs)[:, None],
        jnp.stack(input_grads)[:, None],
        lax.dynamic_slice_in_dim(gain_in_total, place * rows, rows),
        ssm_in_grad,
        attn_in_grad,
        conv_total[:CONV],
        conv_total[CONV],
        head_total[0],
        head_total[1],
        head_total[2],
        ssm_out_grad,
        attn_out_grad,
        lax.dynamic_slice_in_dim(gain_ffn_total, place * rows, rows),
        gate_grad,
        up_grad,
        down_grad,
    )


def solution(mesh):
    return jax.shard_map(
        on_device,
        mesh=mesh,
        in_specs=(
            P(None, "fsdp", "seq", None),
            P(None, "fsdp", "seq", None),
            P(None, "fsdp", None),
            P(("seq", "fsdp")),
            P(("seq", "fsdp"), None),
            P(("seq", "fsdp"), None),
            P(None, ("seq", "fsdp")),
            P(("seq", "fsdp")),
            P(),
            P(),
            P(),
            P(("seq", "fsdp"), None),
            P(("seq", "fsdp"), None),
            P(("seq", "fsdp")),
            P(("seq", "fsdp"), None),
            P(("seq", "fsdp"), None),
            P(("seq", "fsdp"), None),
        ),
        out_specs=(
            P(None, "fsdp", "seq", None),
            P(None, "fsdp", "seq", None),
            P(("seq", "fsdp")),
            P(("seq", "fsdp"), None),
            P(("seq", "fsdp"), None),
            P(None, ("seq", "fsdp")),
            P(("seq", "fsdp")),
            P(),
            P(),
            P(),
            P(("seq", "fsdp"), None),
            P(("seq", "fsdp"), None),
            P(("seq", "fsdp")),
            P(("seq", "fsdp"), None),
            P(("seq", "fsdp"), None),
            P(("seq", "fsdp"), None),
        ),
        check_vma=False,
    )
```

```python
import functools

import jax
import jax.numpy as jnp
from jax import lax
from jax.experimental import pallas as pl
from jax.experimental.pallas import tpu as pltpu
from jax.sharding import PartitionSpec as P

SSM_HEADS = 48
SSM_DIM = 64
STATE = 256
CONV = 4
Q_HEADS = 8
KV_HEADS = 2
HEAD_DIM = 128
MICRO = 2
SPAN = 128
SSM_INNER = 3072
CONV_CH = 3584
ATT_ROWS = 256
VMEM_BYTES = 48 * 1024 * 1024


PRECISE = lax.Precision.HIGHEST
EPSILON = 1e-05
ROPE_BASE = 10000.0


def lanes_iota(shape):
    return lax.broadcasted_iota(jnp.int32, shape, 1)


def rows_iota(shape):
    return lax.broadcasted_iota(jnp.int32, shape, 0)


def dot_last(left, right):
    return lax.dot_general(left, right, (((1,), (1,)), ((), ())), preferred_element_type=jnp.float32)


def dot_first(left, right):
    return lax.dot_general(left, right, (((0,), (0,)), ((), ())), preferred_element_type=jnp.float32)


def dot_plain(left, right):
    return jnp.dot(left, right, preferred_element_type=jnp.float32)


def head_steps(block, head_ref, heads):
    pre = block.astype(jnp.float32) + head_ref[0:1, :]
    live = lanes_iota(pre.shape) < heads
    pre = jnp.where(live, pre, 0.0)
    step = jnp.maximum(pre, 0.0) + jnp.log1p(jnp.exp(-jnp.abs(pre)))
    step = jnp.where(live, step, 0.0)
    rate = -jnp.exp(head_ref[1:2, :])
    decay = rate * step
    lower = (rows_iota((SPAN, SPAN)) >= lanes_iota((SPAN, SPAN))).astype(jnp.float32)
    total = jnp.dot(lower, decay, precision=PRECISE, preferred_element_type=jnp.float32)
    return step, rate, decay, total, pre


def convolve(ubuf, aux_ref, conv_ref, lanes):
    acc = conv_ref[CONV : CONV + 1, lanes] + conv_ref[CONV - 1 : CONV, lanes] * ubuf[8 : 8 + SPAN, lanes]
    for offset in range(1, CONV):
        shifted = ubuf[8 - offset : 8 - offset + SPAN, lanes]
        weight = conv_ref[CONV - 1 - offset : CONV - offset, lanes]
        acc = acc + weight * shifted * aux_ref[:, 2 + offset : 3 + offset]
    return acc


def pair_of(values, first_head, low_lanes):
    one = jnp.broadcast_to(values[:, first_head : first_head + 1], (SPAN, 128))
    two = jnp.broadcast_to(values[:, first_head + 1 : first_head + 2], (SPAN, 128))
    return one, two, jnp.where(low_lanes, one, two)


def ssd_forward_kernel(
    heads,
    order_ref,
    first_ref,
    aux_ref,
    seg_ref,
    conv_ref,
    head_ref,
    skip_ref,
    y_ref,
    start_ref,
    ubuf,
    taps,
    state,
):
    f32, bf16 = jnp.float32, jnp.bfloat16
    inner = heads * SSM_DIM
    width = inner + 2 * STATE

    @pl.when(pl.program_id(0) == 0)
    def _():
        ubuf[SPAN : SPAN + 8, :] = jnp.zeros((8, width), f32)
        state[...] = jnp.zeros((STATE, inner), f32)

    ubuf[0:8, :] = ubuf[SPAN : SPAN + 8, :]
    ubuf[8 : 8 + SPAN, :] = first_ref[:, :width].astype(f32)
    for lane in range(0, width, 128):
        lanes = slice(lane, lane + 128)
        pre = convolve(ubuf, aux_ref, conv_ref, lanes)
        taps[:, lanes] = (pre * jax.nn.sigmoid(pre)).astype(bf16)
    step, rate, decay, total, unused = head_steps(first_ref[:, width:], head_ref, heads)
    total_rows = total.T
    low_lanes = lanes_iota((SPAN, 128)) < SSM_DIM
    same = (aux_ref[:, 0:1] == seg_ref[0]) & (rows_iota((SPAN, SPAN)) >= lanes_iota((SPAN, SPAN)))
    b_rows = taps[:, inner : inner + STATE]
    c_rows = taps[:, inner + STATE :]
    b_cols = b_rows.astype(f32).T.astype(bf16)
    scores = dot_last(c_rows, b_rows)
    carry_keep = aux_ref[:, 1:2]
    end_keep = aux_ref[:, 2:3]
    for pair in range(heads // 2):
        lanes = slice(pair * 128, pair * 128 + 128)
        sum_one, sum_two, sums = pair_of(total, 2 * pair, low_lanes)
        steps = pair_of(step, 2 * pair, low_lanes)[2]
        row_one = total_rows[2 * pair : 2 * pair + 1, :]
        row_two = total_rows[2 * pair + 1 : 2 * pair + 2, :]
        mix_one = (jnp.exp(jnp.where(same, sum_one - row_one, -1e30)) * scores).astype(bf16)
        mix_two = (jnp.exp(jnp.where(same, sum_two - row_two, -1e30)) * scores).astype(bf16)
        x = taps[:, lanes].astype(f32)
        stepped = (x * steps).astype(bf16)
        none = jnp.zeros_like(stepped)
        split = jnp.concatenate(
            [jnp.where(low_lanes, stepped, none), jnp.where(low_lanes, none, stepped)], axis=0
        )
        held = state[:, lanes]
        held_low = held.astype(bf16)
        start_ref[0, :, lanes] = held_low
        y = dot_plain(jnp.concatenate([mix_one, mix_two], axis=1), split)
        y = y + jnp.exp(sums) * carry_keep * dot_plain(c_rows, held_low)
        y_ref[:, lanes] = (y + skip_ref[0:1, lanes] * x).astype(bf16)
        last = sums[SPAN - 1 : SPAN, :]
        weighted = (jnp.exp(last - sums) * end_keep * stepped.astype(f32)).astype(bf16)
        kept = jnp.exp(last) * aux_ref[SPAN - 1 : SPAN, 1:2]
        state[:, lanes] = held * kept + dot_plain(b_cols, weighted)


def ssd_backward_kernel(
    heads,
    order_ref,
    first_ref,
    before_ref,
    aux_ref,
    seg_ref,
    conv_ref,
    head_ref,
    skip_ref,
    start_ref,
    dy_ref,
    grad_ref,
    conv_grad_ref,
    head_grad_ref,
    skip_grad_ref,
    ubuf,
    taps,
    slope,
    gbuf,
    dstate,
):
    f32, bf16 = jnp.float32, jnp.bfloat16
    inner = heads * SSM_DIM
    width = inner + 2 * STATE

    @pl.when(pl.program_id(0) == 0)
    def _():
        gbuf[0:8, :] = jnp.zeros((8, width), f32)
        dstate[...] = jnp.zeros((STATE, inner), f32)
        conv_grad_ref[...] = jnp.zeros(conv_grad_ref.shape, f32)
        head_grad_ref[...] = jnp.zeros(head_grad_ref.shape, f32)
        skip_grad_ref[...] = jnp.zeros(skip_grad_ref.shape, f32)

    ubuf[0:8, :] = before_ref[8:16, :width].astype(f32)
    ubuf[8 : 8 + SPAN, :] = first_ref[:, :width].astype(f32)
    gbuf[SPAN : SPAN + 8, :] = gbuf[0:8, :]
    for lane in range(0, width, 128):
        lanes = slice(lane, lane + 128)
        pre = convolve(ubuf, aux_ref, conv_ref, lanes)
        sig = jax.nn.sigmoid(pre)
        taps[:, lanes] = (pre * sig).astype(bf16)
        slope[:, lanes] = sig * (1.0 + pre * (1.0 - sig))
    step, rate, decay, total, pre_step = head_steps(first_ref[:, width:], head_ref, heads)
    total_rows = total.T
    square = (SPAN, SPAN)
    low_lanes = lanes_iota((SPAN, 128)) < SSM_DIM
    low_row = lanes_iota((1, 128)) < SSM_DIM
    same = (aux_ref[:, 0:1] == seg_ref[0]) & (rows_iota(square) >= lanes_iota(square))
    b_rows = taps[:, inner : inner + STATE]
    c_rows = taps[:, inner + STATE :]
    c_cols = c_rows.astype(f32).T.astype(bf16)
    scores = dot_last(c_rows, b_rows)
    carry_keep = aux_ref[:, 1:2]
    end_keep = aux_ref[:, 2:3]
    head_lane = lanes_iota((SPAN, 128))
    is_last = rows_iota((SPAN, 1)) == SPAN - 1
    grad_scores = jnp.zeros(square, f32)
    grad_b = jnp.zeros((SPAN, STATE), f32)
    grad_c = jnp.zeros((SPAN, STATE), f32)
    grad_total = jnp.zeros((SPAN, 128), f32)
    grad_step = jnp.zeros((SPAN, 128), f32)
    for pair in range(heads // 2):
        lanes = slice(pair * 128, pair * 128 + 128)
        sum_one, sum_two, sums = pair_of(total, 2 * pair, low_lanes)
        steps = pair_of(step, 2 * pair, low_lanes)[2]
        row_one = total_rows[2 * pair : 2 * pair + 1, :]
        row_two = total_rows[2 * pair + 1 : 2 * pair + 2, :]
        decay_one = jnp.exp(jnp.where(same, sum_one - row_one, -1e30))
        decay_two = jnp.exp(jnp.where(same, sum_two - row_two, -1e30))
        mix_one = (decay_one * scores).astype(bf16)
        mix_two = (decay_two * scores).astype(bf16)
        x = taps[:, lanes].astype(f32)
        stepped = (x * steps).astype(bf16)
        none = jnp.zeros_like(stepped)
        x_one = jnp.where(low_lanes, stepped, none)
        x_two = jnp.where(low_lanes, none, stepped)
        dy_low = dy_ref[:, lanes]
        dy = dy_low.astype(f32)
        dy_one = jnp.where(low_lanes, dy_low, none)
        dy_two = jnp.where(low_lanes, none, dy_low)
        grad_scores = grad_scores + dot_last(dy_one, stepped) * decay_one + dot_last(dy_two, stepped) * decay_two
        y = dot_plain(
            jnp.concatenate([mix_one, mix_two], axis=1), jnp.concatenate([x_one, x_two], axis=0)
        )
        grad_in = dot_first(
            jnp.concatenate([mix_one, mix_two], axis=0), jnp.concatenate([dy_one, dy_two], axis=0)
        )
        held = start_ref[0, :, lanes]
        dheld = dstate[:, lanes]
        dheld_low = dheld.astype(bf16)
        grown = jnp.exp(sums) * carry_keep
        y = y + grown * dot_plain(c_rows, held)
        grown_dy = (grown * dy).astype(bf16)
        last = sums[SPAN - 1 : SPAN, :]
        fade = jnp.exp(last - sums) * end_keep
        stepped_wide = stepped.astype(f32)
        weighted = (fade * stepped_wide).astype(bf16)
        from_end = dot_plain(b_rows, dheld_low)
        grad_in = grad_in + fade * from_end
        grad_c = grad_c + dot_last(grown_dy, held)
        grad_b = grad_b + dot_last(weighted, dheld_low)
        kept = jnp.exp(last) * aux_ref[SPAN - 1 : SPAN, 1:2]
        ends = jnp.sum(fade * stepped_wide * from_end, axis=0, keepdims=True) + kept * jnp.sum(
            dheld * held.astype(f32), axis=0, keepdims=True
        )
        dstate[:, lanes] = dheld * kept + dot_plain(c_cols, grown_dy)
        gaps = dy * y - stepped_wide * grad_in
        by_step = x * grad_in
        for half in range(2):
            keep = low_lanes if half == 0 else ~low_lanes
            keep_row = low_row if half == 0 else ~low_row
            end_sum = jnp.sum(jnp.where(keep_row, ends, 0.0), axis=1, keepdims=True)
            gap_sum = jnp.sum(jnp.where(keep, gaps, 0.0), axis=1, keepdims=True)
            gap_sum = gap_sum + jnp.where(is_last, end_sum, 0.0)
            step_sum = jnp.sum(jnp.where(keep, by_step, 0.0), axis=1, keepdims=True)
            here = head_lane == 2 * pair + half
            grad_total = jnp.where(here, gap_sum, grad_total)
            grad_step = jnp.where(here, step_sum, grad_step)
        skip = skip_ref[0:1, lanes]
        skip_grad_ref[0:1, lanes] += jnp.sum(dy * x, axis=0, keepdims=True)
        gbuf[0:SPAN, lanes] = (steps * grad_in + skip * dy) * slope[:, lanes]
    low_scores = grad_scores.astype(bf16)
    grad_c = grad_c + dot_plain(low_scores, b_rows)
    grad_b = grad_b + dot_first(low_scores, c_rows)
    gbuf[0:SPAN, inner : inner + STATE] = grad_b * slope[:, inner : inner + STATE]
    gbuf[0:SPAN, inner + STATE : width] = grad_c * slope[:, inner + STATE : width]

    upper = (rows_iota(square) <= lanes_iota(square)).astype(f32)
    grad_decay = jnp.dot(upper, grad_total, precision=PRECISE, preferred_element_type=f32)
    grad_pre = (grad_step + rate * grad_decay) * jax.nn.sigmoid(pre_step)
    grad_pre = jnp.where(head_lane < heads, grad_pre, 0.0)
    grad_ref[:, width:] = grad_pre.astype(bf16)
    head_grad_ref[0:1, :] += jnp.sum(grad_decay * decay, axis=0, keepdims=True)
    head_grad_ref[1:2, :] += jnp.sum(grad_pre, axis=0, keepdims=True)

    for lane in range(0, width, 128):
        lanes = slice(lane, lane + 128)
        grad = gbuf[0:SPAN, lanes]
        conv_grad_ref[CONV : CONV + 1, lanes] += jnp.sum(grad, axis=0, keepdims=True)
        conv_grad_ref[CONV - 1 : CONV, lanes] += jnp.sum(grad * ubuf[8 : 8 + SPAN, lanes], axis=0, keepdims=True)
        acc = conv_ref[CONV - 1 : CONV, lanes] * grad
        for offset in range(1, CONV):
            at = CONV - 1 - offset
            shifted = ubuf[8 - offset : 8 - offset + SPAN, lanes] * aux_ref[:, 2 + offset : 3 + offset]
            conv_grad_ref[at : at + 1, lanes] += jnp.sum(grad * shifted, axis=0, keepdims=True)
            later = gbuf[offset : offset + SPAN, lanes] * aux_ref[:, 5 + offset : 6 + offset]
            acc = acc + conv_ref[at : at + 1, lanes] * later
        grad_ref[:, lanes] = acc.astype(bf16)


def token_aux(segment):
    length = segment.shape[0]
    ends = segment.reshape(-1, SPAN)[:, -1]
    end_of = jnp.repeat(ends, SPAN)
    before = jnp.repeat(jnp.concatenate([jnp.full((1,), -1, segment.dtype), ends[:-1]]), SPAN)
    columns = [segment, segment == before, segment == end_of]
    for offset in range(1, CONV):
        columns.append(jnp.pad(segment, (offset, 0), constant_values=-1)[:length] == segment)
    for offset in range(1, CONV):
        columns.append(jnp.pad(segment, (0, offset), constant_values=-1)[offset:] == segment)
    columns = [column.astype(jnp.float32) for column in columns]
    return jnp.stack(columns + [jnp.zeros((length,), jnp.float32)] * (16 - len(columns)), axis=1)


def ssd_specs(heads, at):
    inner = heads * SSM_DIM
    width = inner + 2 * STATE
    return [
        pl.BlockSpec((SPAN, width + 128), lambda i, order: (order[at(i)], 0)),
        pl.BlockSpec((SPAN, 16), lambda i, order: (at(i), 0)),
        pl.BlockSpec((1, 1, SPAN), lambda i, order: (at(i), 0, 0)),
        pl.BlockSpec((8, width), lambda i, order: (0, 0)),
        pl.BlockSpec((8, 128), lambda i, order: (0, 0)),
        pl.BlockSpec((8, inner), lambda i, order: (0, 0)),
    ]


def ssd_forward(order, first, aux, seg_rows, conv, head, skip, heads):
    length = first.shape[0]
    inner = heads * SSM_DIM
    width = inner + 2 * STATE
    blocks = length // SPAN
    return pl.pallas_call(
        functools.partial(ssd_forward_kernel, heads),
        grid_spec=pltpu.PrefetchScalarGridSpec(
            num_scalar_prefetch=1,
            grid=(blocks,),
            in_specs=ssd_specs(heads, lambda i: i),
            out_specs=[
                pl.BlockSpec((SPAN, inner), lambda i, order: (order[i], 0)),
                pl.BlockSpec((1, STATE, inner), lambda i, order: (i, 0, 0)),
            ],
            scratch_shapes=[
                pltpu.VMEM((SPAN + 8, width), jnp.float32),
                pltpu.VMEM((SPAN, width), jnp.bfloat16),
                pltpu.VMEM((STATE, inner), jnp.float32),
            ],
        ),
        out_shape=[
            jax.ShapeDtypeStruct((length, inner), jnp.bfloat16),
            jax.ShapeDtypeStruct((blocks, STATE, inner), jnp.bfloat16),
        ],
        compiler_params=pltpu.CompilerParams(
            dimension_semantics=("arbitrary",), vmem_limit_bytes=VMEM_BYTES
        ),
        cost_estimate=pl.CostEstimate(
            flops=8_000_000_000 * heads // 12, bytes_accessed=12_000_000, transcendentals=4_000_000
        ),
        name="ssd_forward",
    )(order, first, aux, seg_rows, conv, head, skip)


def ssd_backward(order, first, aux, seg_rows, conv, head, skip, starts, dy, heads):
    length = first.shape[0]
    inner = heads * SSM_DIM
    width = inner + 2 * STATE
    blocks = length // SPAN
    per_block = SPAN // 16

    def at(i):
        return blocks - 1 - i

    specs = ssd_specs(heads, at)
    specs.insert(
        1,
        pl.BlockSpec(
            (16, width + 128), lambda i, order: (order[jnp.maximum(at(i) - 1, 0)] * per_block + per_block - 1, 0)
        ),
    )
    specs += [
        pl.BlockSpec((1, STATE, inner), lambda i, order: (at(i), 0, 0)),
        pl.BlockSpec((SPAN, inner), lambda i, order: (order[at(i)], 0)),
    ]
    return pl.pallas_call(
        functools.partial(ssd_backward_kernel, heads),
        grid_spec=pltpu.PrefetchScalarGridSpec(
            num_scalar_prefetch=1,
            grid=(blocks,),
            in_specs=specs,
            out_specs=[
                pl.BlockSpec((SPAN, width + 128), lambda i, order: (order[at(i)], 0)),
                pl.BlockSpec((8, width), lambda i, order: (0, 0)),
                pl.BlockSpec((8, 128), lambda i, order: (0, 0)),
                pl.BlockSpec((8, inner), lambda i, order: (0, 0)),
            ],
            scratch_shapes=[
                pltpu.VMEM((SPAN + 8, width), jnp.float32),
                pltpu.VMEM((SPAN, width), jnp.bfloat16),
                pltpu.VMEM((SPAN, width), jnp.float32),
                pltpu.VMEM((SPAN + 8, width), jnp.float32),
                pltpu.VMEM((STATE, inner), jnp.float32),
            ],
        ),
        out_shape=[
            jax.ShapeDtypeStruct((length, width + 128), jnp.bfloat16),
            jax.ShapeDtypeStruct((8, width), jnp.float32),
            jax.ShapeDtypeStruct((8, 128), jnp.float32),
            jax.ShapeDtypeStruct((8, inner), jnp.float32),
        ],
        compiler_params=pltpu.CompilerParams(
            dimension_semantics=("arbitrary",), vmem_limit_bytes=VMEM_BYTES
        ),
        cost_estimate=pl.CostEstimate(
            flops=30_000_000_000 * heads // 12, bytes_accessed=16_000_000, transcendentals=5_000_000
        ),
        name="ssd_backward",
    )(order, first, first, aux, seg_rows, conv, head, skip, starts, dy)


def rotary_tables(length):
    half = HEAD_DIM // 2
    frequency = ROPE_BASE ** (-jnp.arange(half).astype(jnp.float32) / half)
    angles = jnp.arange(length, dtype=jnp.int32).astype(jnp.float32)[:, None] * frequency[None, :]
    cosine, sine = jnp.cos(angles), jnp.sin(angles)
    return jnp.concatenate([cosine, cosine], axis=1), jnp.concatenate([-sine, sine], axis=1)


def turn(rows, cosine, sine):
    wide = rows.astype(jnp.float32)
    return (wide * cosine + pltpu.roll(wide, HEAD_DIM // 2, 1) * sine).astype(jnp.bfloat16)


def turn_back(grads, cosine, sine):
    return (grads * cosine + pltpu.roll(grads * sine, HEAD_DIM // 2, 1)).astype(jnp.bfloat16)


def block_scores(q_block, k_part, first_row, seg_col, seg_row):
    scores = dot_last(q_block, k_part) * HEAD_DIM ** (-0.5)
    shape = scores.shape
    allowed = (rows_iota(shape) + first_row >= lanes_iota(shape)) & (seg_col == seg_row)
    return jnp.where(allowed, scores, -1e30)


def place_of(order_ref, block):
    return pl.ds(pl.multiple_of(order_ref[block] * SPAN, SPAN), SPAN)


def load_keys(order_ref, qkv_ref, q_width, cos_ref, sin_ref, k_rot, value):
    for block in range(qkv_ref.shape[0] // SPAN):
        there, here = place_of(order_ref, block), slice(block * SPAN, (block + 1) * SPAN)
        k_rot[here, :] = turn(qkv_ref[there, q_width : q_width + HEAD_DIM], cos_ref[here, :], sin_ref[here, :])
        value[here, :] = qkv_ref[there, q_width + HEAD_DIM : q_width + 2 * HEAD_DIM]


def load_rows(order_ref, ref, start, count, lanes):
    blocks = range(start // SPAN, (start + count) // SPAN)
    return jnp.concatenate([ref[place_of(order_ref, block), lanes] for block in blocks], axis=0)


def store_rows(order_ref, ref, start, lanes, values):
    for part in range(values.shape[0] // SPAN):
        ref[place_of(order_ref, start // SPAN + part), lanes] = values[part * SPAN : (part + 1) * SPAN, :]


def attend_forward_kernel(
    query_heads, block, order_ref, qkv_ref, cos_ref, sin_ref, aux_ref, seg_ref, out_ref, lse_ref, k_rot, value
):
    length = qkv_ref.shape[0]
    load_keys(order_ref, qkv_ref, query_heads * HEAD_DIM, cos_ref, sin_ref, k_rot, value)
    for start in range(0, length, block):
        rows = slice(start, start + block)
        end = start + block
        for head in range(query_heads):
            lanes = slice(head * HEAD_DIM, (head + 1) * HEAD_DIM)
            q_rows = load_rows(order_ref, qkv_ref, start, block, lanes)
            q_block = turn(q_rows, cos_ref[rows, :], sin_ref[rows, :])
            scores = block_scores(q_block, k_rot[:end, :], start, aux_ref[rows, 0:1], seg_ref[:, :end])
            top = jnp.max(scores, axis=1, keepdims=True)
            raised = jnp.exp(scores - top)
            total = jnp.sum(raised, axis=1, keepdims=True)
            probs = (raised * (1.0 / total)).astype(jnp.bfloat16)
            store_rows(order_ref, out_ref, start, lanes, dot_plain(probs, value[:end, :]).astype(jnp.bfloat16))
            lse_ref[rows, head : head + 1] = top + jnp.log(total)


def attend_backward_kernel(
    query_heads,
    block,
    order_ref,
    qkv_ref,
    cos_ref,
    sin_ref,
    aux_ref,
    seg_ref,
    lse_ref,
    grad_ref,
    out_ref,
    k_rot,
    value,
    dk,
    dv,
):
    f32, bf16 = jnp.float32, jnp.bfloat16
    length = qkv_ref.shape[0]
    q_width = query_heads * HEAD_DIM
    load_keys(order_ref, qkv_ref, q_width, cos_ref, sin_ref, k_rot, value)
    dk[...] = jnp.zeros(dk.shape, f32)
    dv[...] = jnp.zeros(dv.shape, f32)
    for start in range(0, length, block):
        rows = slice(start, start + block)
        end = start + block
        for head in range(query_heads):
            lanes = slice(head * HEAD_DIM, (head + 1) * HEAD_DIM)
            cosine, sine = cos_ref[rows, :], sin_ref[rows, :]
            q_block = turn(load_rows(order_ref, qkv_ref, start, block, lanes), cosine, sine)
            scores = block_scores(q_block, k_rot[:end, :], start, aux_ref[rows, 0:1], seg_ref[:, :end])
            probs = jnp.exp(scores - lse_ref[rows, head : head + 1])
            grad = load_rows(order_ref, grad_ref, start, block, lanes)
            grad_probs = dot_last(grad, value[:end, :])
            mean = jnp.sum(grad_probs * probs, axis=1, keepdims=True)
            grad_scores = (probs * (grad_probs - mean) * HEAD_DIM ** (-0.5)).astype(bf16)
            grad_query = turn_back(dot_plain(grad_scores, k_rot[:end, :]), cosine, sine)
            store_rows(order_ref, out_ref, start, lanes, grad_query)
            dk[:end, :] += dot_first(grad_scores, q_block)
            dv[:end, :] += dot_first(probs.astype(bf16), grad)
    k_lanes = slice(q_width, q_width + HEAD_DIM)
    v_lanes = slice(q_width + HEAD_DIM, q_width + 2 * HEAD_DIM)
    store_rows(order_ref, out_ref, 0, k_lanes, turn_back(dk[...], cos_ref[...], sin_ref[...]))
    store_rows(order_ref, out_ref, 0, v_lanes, dv[...].astype(bf16))


def attend_specs(arrays):
    return [pl.BlockSpec(memory_space=pltpu.SMEM)] + [pl.BlockSpec(memory_space=pltpu.VMEM)] * arrays


def attend_forward(order, early, tables, aux, seg_row, query_heads):
    length = early.shape[0]
    return pl.pallas_call(
        functools.partial(attend_forward_kernel, query_heads, min(ATT_ROWS, length)),
        in_specs=attend_specs(5),
        out_shape=[
            jax.ShapeDtypeStruct((length, query_heads * HEAD_DIM), jnp.bfloat16),
            jax.ShapeDtypeStruct((length, 8), jnp.float32),
        ],
        scratch_shapes=[pltpu.VMEM((length, HEAD_DIM), jnp.bfloat16), pltpu.VMEM((length, HEAD_DIM), jnp.bfloat16)],
        compiler_params=pltpu.CompilerParams(vmem_limit_bytes=VMEM_BYTES),
        cost_estimate=pl.CostEstimate(
            flops=2_000_000_000 * query_heads, bytes_accessed=4_000_000, transcendentals=1_000_000
        ),
        name="attend_forward",
    )(order, early, tables[0], tables[1], aux, seg_row)


def attend_backward(order, early, tables, aux, seg_row, lse, grad, query_heads):
    length = early.shape[0]
    return pl.pallas_call(
        functools.partial(attend_backward_kernel, query_heads, min(ATT_ROWS, length)),
        in_specs=attend_specs(7),
        out_shape=jax.ShapeDtypeStruct((length, (query_heads + 2) * HEAD_DIM), jnp.bfloat16),
        scratch_shapes=[
            pltpu.VMEM((length, HEAD_DIM), jnp.bfloat16),
            pltpu.VMEM((length, HEAD_DIM), jnp.bfloat16),
            pltpu.VMEM((length, HEAD_DIM), jnp.float32),
            pltpu.VMEM((length, HEAD_DIM), jnp.float32),
        ],
        compiler_params=pltpu.CompilerParams(vmem_limit_bytes=VMEM_BYTES),
        cost_estimate=pl.CostEstimate(
            flops=4_000_000_000 * query_heads, bytes_accessed=6_000_000, transcendentals=1_000_000
        ),
        name="attend_backward",
    )(order, early, tables[0], tables[1], aux, seg_row, lse, grad)


def after_kernel(*refs):
    pass


def after(value, *others):
    return pl.pallas_call(
        after_kernel,
        in_specs=[pl.BlockSpec(memory_space=pl.ANY)] * (1 + len(others)),
        out_specs=pl.BlockSpec(memory_space=pl.ANY),
        out_shape=jax.ShapeDtypeStruct(value.shape, value.dtype),
        input_output_aliases={0: 0},
        name="after",
    )(value, *others)


def move_blocks(tiles, width, here, there):
    per = 128 // width
    lane = lanes_iota(tiles[0].shape)
    moved = []
    for tile in range(len(tiles)):
        out = None
        for part in range(per):
            source = there(tile * per + part)
            piece = tiles[source // per]
            shift = ((part - source % per) * width) % 128
            if shift:
                piece = pltpu.roll(piece, shift, 1)
            out = piece if out is None else jnp.where(lane >= part * width, piece, out)
        moved.append(out)
    return moved


def to_gathered_tiles(tiles, width, seq, fsdp):
    return move_blocks(tiles, width, None, lambda b: (b % seq) * fsdp + b // seq)


def from_gathered_tiles(tiles, width, seq, fsdp):
    return move_blocks(tiles, width, None, lambda b: (b % fsdp) * seq + b // fsdp)


def tiles_of(array):
    return [array[:, lane : lane + 128] for lane in range(0, array.shape[1], 128)]


def add_arrived(split, own, arrived):
    total = own[...]
    if split:
        first = pl.program_id(0) == 0
        one, one_late, two, two_late = (ref[...].astype(jnp.float32) for ref in arrived)
        return total + jnp.where(first, one + one_late, two + two_late)
    for ref in arrived:
        total = total + ref[...].astype(jnp.float32)
    return total


def row_sum(tiles):
    total = tiles[0]
    for tile in tiles[1:]:
        total = total + tile
    return jnp.sum(total, axis=1, keepdims=True)


def store_block(blocks, value):
    for block, out in enumerate(blocks):

        @pl.when(pl.program_id(0) == block)
        def _(out=out):
            out[...] = value


def middle_kernel(split, places, count, own, rows, gain, *refs):
    arrived, outs = refs[:count], refs[count:]
    blocks, middle_ref = outs[: places[3]], outs[places[3]]
    middle = rows[...].astype(jnp.float32) + add_arrived(split, own, arrived)
    middle_ref[...] = middle
    mean = jnp.sum(middle * middle, axis=1, keepdims=True) / middle.shape[1]
    hidden = middle * lax.rsqrt(mean + EPSILON) * gain[0:1, :]
    moved = jnp.concatenate(to_gathered_tiles(tiles_of(hidden), *places[:3]), axis=1).astype(jnp.bfloat16)
    store_block(blocks, moved)


def norm_back_kernel(split, places, count, skip, in_blocks, own, rows, passed, gain, *refs):
    arrived, outs = refs[:count], refs[count + skip :]
    grads = add_arrived(split, own, arrived)
    grads = jnp.concatenate(from_gathered_tiles(tiles_of(grads), *places[:3]), axis=1)
    wide = rows[...].astype(jnp.float32)
    width = wide.shape[1]
    scale = lax.rsqrt(jnp.sum(wide * wide, axis=1, keepdims=True) / width + EPSILON)
    normed = wide * scale
    weighted = grads * gain[0:1, :]
    mean = jnp.sum(weighted * normed, axis=1, keepdims=True) / width
    total = passed[...].astype(jnp.float32) + scale * (weighted - normed * mean)
    if in_blocks:
        store_block(outs[: places[3]], total.astype(jnp.bfloat16))
        outs[-2][...] = total
    else:
        outs[0][...] = total.astype(jnp.bfloat16)
    gain_grad = outs[-1]

    @pl.when(pl.program_id(0) == 0)
    def _():
        gain_grad[...] = jnp.zeros(gain_grad.shape, jnp.float32)

    gain_grad[0:1, :] += jnp.sum(normed * grads, axis=0, keepdims=True)


def rows_call(kernel, tokens, width, split, inputs, gain, arrived, outs, deps, name):
    block = pl.BlockSpec((SPAN, width), lambda i: (i, 0))
    whole = pl.BlockSpec((8, width), lambda i: (0, 0))
    fixed = pl.BlockSpec((SPAN, width), lambda i: (0, 0))
    out_specs = [whole if shape[0] == 8 else fixed if shape[0] == SPAN else block for shape, dtype in outs]
    return pl.pallas_call(
        kernel,
        grid=(tokens // SPAN,),
        in_specs=[block] * len(inputs)
        + [whole]
        + [fixed if split else block] * len(arrived)
        + [pl.BlockSpec(memory_space=pl.ANY)] * len(deps),
        out_specs=out_specs,
        out_shape=[jax.ShapeDtypeStruct(shape, dtype) for shape, dtype in outs],
        compiler_params=pltpu.CompilerParams(
            dimension_semantics=("arbitrary",), vmem_limit_bytes=VMEM_BYTES
        ),
        cost_estimate=pl.CostEstimate(flops=40 * tokens * width, bytes_accessed=20 * tokens * width, transcendentals=0),
        name=name,
    )(*inputs, gain, *arrived, *deps)


def norm_pieces_kernel(gain, *refs):
    pieces, out = refs[:-1], refs[-1]
    for block, piece in enumerate(pieces):

        @pl.when(pl.program_id(0) == block)
        def _(piece=piece):
            wide = piece[...].astype(jnp.float32)
            mean = jnp.sum(wide * wide, axis=1, keepdims=True) / wide.shape[1]
            out[...] = (wide * lax.rsqrt(mean + EPSILON) * gain[0:1, :]).astype(jnp.bfloat16)


def norm_pieces(pieces, gain):
    width = pieces[0].shape[1]
    length = len(pieces) * SPAN
    return pl.pallas_call(
        norm_pieces_kernel,
        grid=(len(pieces),),
        in_specs=[pl.BlockSpec((8, width), lambda i: (0, 0))]
        + [pl.BlockSpec((SPAN, width), lambda i: (0, 0)) for piece in pieces],
        out_specs=pl.BlockSpec((SPAN, width), lambda i: (i, 0)),
        out_shape=jax.ShapeDtypeStruct((length, width), jnp.bfloat16),
        compiler_params=pltpu.CompilerParams(
            dimension_semantics=("arbitrary",), vmem_limit_bytes=VMEM_BYTES
        ),
        cost_estimate=pl.CostEstimate(flops=6 * length * width, bytes_accessed=4 * length * width, transcendentals=0),
        name="norm_pieces",
    )(gain, *pieces)


def assemble_kernel(count, *refs):
    pieces, out, held, sems = refs[:count], refs[-3], refs[-2], refs[-1]
    places = [pl.ds(block * SPAN, SPAN) for block in range(count)]
    loads = [pltpu.make_async_copy(pieces[b], held.at[places[b]], sems.at[0, b]) for b in range(count)]
    stores = [pltpu.make_async_copy(held.at[places[b]], out.at[places[b]], sems.at[1, b]) for b in range(count)]
    for load in loads:
        load.start()
    for load, store in zip(loads, stores):
        load.wait()
        store.start()
    for store in stores:
        store.wait()


def assemble(pieces, *deps):
    width = pieces[0].shape[1]
    length = len(pieces) * SPAN
    return pl.pallas_call(
        functools.partial(assemble_kernel, len(pieces)),
        in_specs=[pl.BlockSpec(memory_space=pl.ANY)] * (len(pieces) + len(deps)),
        out_specs=pl.BlockSpec(memory_space=pl.ANY),
        out_shape=jax.ShapeDtypeStruct((length, width), pieces[0].dtype),
        scratch_shapes=[
            pltpu.VMEM((length, width), pieces[0].dtype),
            pltpu.SemaphoreType.DMA((2, len(pieces))),
        ],
        compiler_params=pltpu.CompilerParams(vmem_limit_bytes=VMEM_BYTES),
        cost_estimate=pl.CostEstimate(flops=0, bytes_accessed=4 * length * width, transcendentals=0),
        name="assemble",
    )(*pieces, *deps)


def gathered_blocks_kernel(places, rows, *outs):
    for block, out in enumerate(outs):

        @pl.when(pl.program_id(0) == block)
        def _(out=out):
            moved = to_gathered_tiles(tiles_of(rows[...].astype(jnp.float32)), *places)
            out[...] = jnp.concatenate(moved, axis=1).astype(out.dtype)


def gathered_blocks(rows, places):
    tokens, width = rows.shape
    blocks = tokens // SPAN
    return pl.pallas_call(
        functools.partial(gathered_blocks_kernel, places),
        grid=(blocks,),
        in_specs=[pl.BlockSpec((SPAN, width), lambda i: (i, 0))],
        out_specs=[pl.BlockSpec((SPAN, width), lambda i: (0, 0))] * blocks,
        out_shape=[jax.ShapeDtypeStruct((SPAN, width), rows.dtype)] * blocks,
        compiler_params=pltpu.CompilerParams(
            dimension_semantics=("arbitrary",), vmem_limit_bytes=VMEM_BYTES
        ),
        cost_estimate=pl.CostEstimate(flops=4 * tokens * width, bytes_accessed=4 * tokens * width, transcendentals=0),
        name="gathered_blocks",
    )(rows)


def matmul_rows(left, right):
    return jnp.einsum("tc,cd->td", left, right, preferred_element_type=jnp.float32)


def matmul_back(left, right):
    return jnp.einsum("td,cd->tc", left, right, preferred_element_type=jnp.float32)


def weight_grad(left, right):
    return jnp.einsum("tc,td->cd", left, right, preferred_element_type=jnp.float32)


def peers(count, flip):
    return [(i, i ^ flip) for i in range(count)]


def swap(value, flip):
    return lax.ppermute(value, "seq", peers(lax.axis_size("seq"), flip))


def balanced(tokens):
    return lax.axis_size("seq") == 4 and tokens == 2 * SPAN


def block_places(tokens):
    index = lax.axis_index("seq")
    halves = tokens // SPAN
    blocks = jnp.arange(lax.axis_size("seq") * halves, dtype=jnp.int32)
    place = (blocks // halves) ^ index
    place = place * halves + blocks % halves
    if balanced(tokens):
        place = jnp.array([0, 1, 2, 7, 6, 4, 3, 5], jnp.int32)[place]
    return place


def fetch_tokens(halves):
    if balanced(len(halves) * SPAN):
        a, b = halves
        one_a, two_b = swap(a, 1), swap(b, 2)
        three_a, three_b = swap(one_a, 2), swap(two_b, 1)
        one_b, two_a = swap(b, 1), swap(a, 2)
        return [a, b, one_a, three_a, two_b, three_b, two_a, one_b]
    return list(halves) + [swap(half, flip) for flip in range(1, lax.axis_size("seq")) for half in halves]


def scatter_tokens(product, tokens, hold=()):
    f32, bf16 = jnp.float32, jnp.bfloat16

    def held(part):
        return after(part, *hold) if hold else part

    if balanced(tokens):
        to_one = product(tokens, 2 * tokens).astype(bf16)
        from_one = swap(held(to_one), 1)
        to_two = product(2 * tokens, 3 * tokens).astype(bf16)
        from_two = swap(held(to_two), 2)
        second = product(3 * tokens, 4 * tokens, to_one, to_two)
        own = product(0, tokens, to_one, to_two)
        two_a = (second[:SPAN] + from_one[SPAN:].astype(f32)).astype(bf16)
        one_b = (second[SPAN:] + from_two[SPAN:].astype(f32)).astype(bf16)
        return own, (from_one, swap(two_a, 2), from_two, swap(one_b, 1)), (to_one, to_two, second, own)
    sent = [
        product(flip * tokens, (flip + 1) * tokens).astype(bf16) for flip in range(1, lax.axis_size("seq"))
    ]
    own = product(0, tokens, *sent)
    return own, tuple(swap(held(part), flip + 1) for flip, part in enumerate(sent)), (*sent, own)


def cut_rows(whole, start, end, deps):
    part = whole[start:end]
    return after(part, *deps) if deps else part


def add_small(vector):
    for axis in ("fsdp", "seq"):
        count = lax.axis_size(axis)
        flip = 1
        while flip < count:
            vector = vector + lax.ppermute(vector, axis, peers(count, flip))
            flip *= 2
    return vector


def trade(stacked):
    return lax.all_to_all(stacked, "seq", split_axis=0, concat_axis=0, tiled=True)


def gather_weights(rows):
    return lax.all_gather(rows.reshape(-1, rows.shape[-1]), "fsdp", axis=0, tiled=True)


def spread_sums(grad):
    return lax.psum_scatter(grad, "fsdp", scatter_dimension=0, tiled=True)


def to_gathered(rows):
    seq, fsdp = lax.axis_size("seq"), lax.axis_size("fsdp")
    shape = rows.shape
    split = rows.reshape(shape[:-1] + (seq, fsdp, -1))
    return jnp.swapaxes(split, -3, -2).reshape(shape)


def from_gathered(rows):
    seq, fsdp = lax.axis_size("seq"), lax.axis_size("fsdp")
    shape = rows.shape
    split = rows.reshape(shape[:-1] + (fsdp, seq, -1))
    return jnp.swapaxes(split, -3, -2).reshape(shape)


def on_device(
    inputs,
    cotangent,
    segments,
    norm_in,
    ssm_in,
    attn_in,
    conv_w,
    conv_b,
    a_log,
    dt_bias,
    d_skip,
    ssm_out,
    attn_out,
    norm_ffn,
    w_gate,
    w_up,
    w_down,
):
    f32, bf16 = jnp.float32, jnp.bfloat16
    seq = lax.axis_size("seq")
    fsdp = lax.axis_size("fsdp")
    index = lax.axis_index("seq")
    rows = ssm_in.shape[0]
    tokens = inputs.shape[2]
    length = segments.shape[2]
    heads = SSM_HEADS // seq
    inner = heads * SSM_DIM
    query_heads = Q_HEADS // seq
    q_width = query_heads * HEAD_DIM
    qkv_width = q_width + 2 * HEAD_DIM
    groups = Q_HEADS // KV_HEADS
    kv_of = [(s * query_heads) // groups for s in range(seq)]
    head_start = index * heads
    inner_start = index * inner
    z_end, x_end, bc_end = SSM_INNER, 2 * SSM_INNER, 2 * SSM_INNER + 2 * STATE
    q_end = Q_HEADS * HEAD_DIM
    kv_end = q_end + KV_HEADS * HEAD_DIM

    def by_seq(block):
        return jnp.swapaxes(block.reshape(rows, seq, -1), 0, 1)

    def for_all(block):
        return jnp.broadcast_to(block[None], (seq,) + block.shape)

    def by_kv(block):
        return jnp.stack([block[:, h * HEAD_DIM : (h + 1) * HEAD_DIM] for h in kv_of])

    channels = conv_b.shape[0]
    conv_pack = jnp.concatenate([conv_w, conv_b[None]], axis=0).reshape(-1)
    conv_cols = -(-conv_pack.shape[0] // rows)
    conv_pack = jnp.pad(conv_pack, (0, conv_cols * rows - conv_pack.shape[0])).reshape(rows, conv_cols)
    misc = jnp.concatenate([norm_in[:, None], norm_ffn[:, None], conv_pack], axis=1)
    misc = jnp.pad(misc, ((0, 0), (0, 128 - misc.shape[1])))
    early_send = jnp.concatenate(
        [by_seq(attn_in[:, :q_end]), by_kv(attn_in[:, q_end:kv_end]), by_kv(attn_in[:, kv_end:]), for_all(misc)],
        axis=2,
    )
    halves = tokens // SPAN
    places = (rows, seq, fsdp, halves)
    mine = gathered_blocks(inputs[0, 0], places[:3])
    dt_block = jnp.pad(by_seq(ssm_in[:, bc_end:]), ((0, 0), (0, 0), (0, 128 - heads)))
    first_send = jnp.concatenate(
        [by_seq(ssm_in[:, z_end:x_end]), for_all(ssm_in[:, x_end:bc_end]), dt_block], axis=2
    )
    start_mine = trade(after(jnp.concatenate([early_send, first_send], axis=2), *mine))
    early_mine, first_mine = start_mine[:, :, : early_send.shape[2]], start_mine[:, :, early_send.shape[2] :]
    pieces = [fetch_tokens([after(half, start_mine) for half in mine])]
    out_send = jnp.concatenate([ssm_out, attn_out], axis=0)
    later_send = jnp.concatenate([by_seq(ssm_in[:, :z_end]), by_seq(w_gate), by_seq(w_up)], axis=2)
    early_w = gather_weights(early_mine)
    first_w = gather_weights(first_mine)
    out_rows = ssm_out.shape[0]
    units = w_down.shape[0] * fsdp
    small = early_w[:, qkv_width:]

    def gain_rows(gain):
        return jnp.broadcast_to(gain.astype(f32)[None], (8, gain.shape[0]))

    gain_in_gathered = gain_rows(small[:, 0])
    gain_in = gain_rows(from_gathered(small[:, 0]))
    gain_ffn = gain_rows(from_gathered(small[:, 1]))
    conv_all = small[:, 2 : 2 + conv_cols].reshape(fsdp, seq, -1)[:, :, : (CONV + 1) * channels]
    conv_all = conv_all.reshape(fsdp, seq, CONV + 1, channels).transpose(2, 1, 0, 3)
    conv_all = conv_all.reshape(CONV + 1, CONV_CH).astype(f32)
    conv_local = jnp.concatenate(
        [lax.dynamic_slice_in_dim(conv_all, inner_start, inner, 1), conv_all[:, SSM_INNER:]], axis=1
    )
    conv_table = jnp.pad(conv_local, ((0, 8 - CONV - 1), (0, 0)))
    rate_local = lax.dynamic_slice_in_dim(a_log.astype(f32), head_start, heads)
    bias_local = lax.dynamic_slice_in_dim(dt_bias.astype(f32), head_start, heads)
    skip_local = lax.dynamic_slice_in_dim(d_skip.astype(f32), head_start, heads)
    head_table = jnp.pad(jnp.stack([bias_local, rate_local]), ((0, 6), (0, 128 - heads)))
    skip_table = jnp.broadcast_to(jnp.repeat(skip_local, SSM_DIM)[None], (8, inner))
    tables = rotary_tables(length)
    order = block_places(tokens)

    micro = range(MICRO)
    auxes = [token_aux(segments[m, 0]) for m in micro]
    seg_blocks = [segments[m, 0].astype(f32).reshape(-1, 1, SPAN) for m in micro]
    seg_rows = [segments[m, 0].astype(f32)[None] for m in micro]
    split = balanced(tokens)
    width = inputs.shape[3]
    head_tables = (conv_table, head_table, skip_table)

    hiddens, earlies, attendeds, lses, firsts, ys, all_starts = [], [], [], [], [], [], []
    for m in range(1, MICRO):
        mine = gathered_blocks(inputs[m, 0], places[:3])
        pieces.append(fetch_tokens([after(half, *pieces[m - 1][-2:]) for half in mine]))
    cot_alls = []
    for m in micro:
        if m > 0:
            pieces[m][0] = after(pieces[m][0], ys[m - 1])
        hidden = norm_pieces(pieces[m], gain_in_gathered)
        early = matmul_rows(hidden, early_w).astype(bf16)
        attended, lse = attend_forward(order, early, tables, auxes[m], seg_rows[m], query_heads)
        earlies.append(early)
        attendeds.append(attended)
        lses.append(lse)
        if m == 0:
            later_mine = trade(after(later_send, attended))
            z_mine, ffn_mine = later_mine[:, :, :inner], later_mine[:, :, inner:]
            z_w = gather_weights(z_mine)
            out_send = after(out_send, z_mine)
            out_w = gather_weights(out_send)
            gate_up_w = gather_weights(after(ffn_mine, out_send))
        hidden = after(hidden, attended, *([later_mine] if m == 0 else cot_pieces))
        hiddens.append(hidden)
        first = matmul_rows(hidden, first_w).astype(bf16)
        behind = [first, *pieces[MICRO - 1][-2:]] if m == 0 else [first, *cot_pieces]
        blocks = [after(cotangent[m, 0, half * SPAN : (half + 1) * SPAN], *behind) for half in range(halves)]
        cot_pieces = fetch_tokens(blocks)
        cot_alls.append(assemble(cot_pieces))
        y_rows, starts = ssd_forward(order, first, auxes[m], seg_blocks[m], *head_tables, heads)
        firsts.append(first)
        ys.append(y_rows)
        all_starts.append(starts)
    down_w = gather_weights(after(w_down, ys[0]))
    out_w = out_w.reshape(fsdp, -1, out_w.shape[1])
    out_w = jnp.concatenate(
        [out_w[:, :out_rows].reshape(inner, -1), out_w[:, out_rows:].reshape(q_width, -1)], axis=0
    )
    side_w = jnp.concatenate([early_w[:, :qkv_width], z_w], axis=1)
    gate_zs, out_ins, mixeds = [], [], []

    def mixer_out(m, deps, hold=()):
        hiddens[m] = after(hiddens[m], *deps)
        gate_z = matmul_rows(hiddens[m], z_w)
        gated = (ys[m].astype(f32) * jax.nn.silu(gate_z)).astype(bf16)
        gate_zs.append(gate_z)
        out_in = jnp.concatenate([gated, attendeds[m]], axis=1)
        out_ins.append(out_in)

        def mixed_rows(start, end, *late):
            return matmul_rows(cut_rows(out_in, start, end, late), out_w)

        mixeds.append(scatter_tokens(mixed_rows, tokens, hold))

    middles, ffn_hiddens, activateds, grad_gus, grad_hiddens = [], [], [], [], []
    grad_middles, lows, gain_ffn_grads, grads_mixed = [], [], [], []

    def middle_forward(m, hold):
        own, arrived, sent = mixeds[m]
        *blocks, middle = rows_call(
            functools.partial(middle_kernel, split, places, len(arrived)),
            tokens,
            width,
            split,
            [own, inputs[m, 0]],
            gain_ffn,
            arrived,
            [((SPAN, width), bf16)] * halves + [((tokens, width), f32)],
            [],
            "middle",
        )
        middles.append(middle)
        if hold:
            blocks = [after(block, *hold) for block in blocks]
        ffn_hiddens.append(assemble(fetch_tokens(blocks)))

    def feed_forward(m, deps):
        ffn_hidden = after(ffn_hiddens[m], *deps)
        ffn_hiddens[m] = ffn_hidden
        gate_up = matmul_rows(ffn_hidden, gate_up_w)
        gate_pre, up_pre = gate_up[:, :units], gate_up[:, units:]
        sig = jax.nn.sigmoid(gate_pre)
        activateds.append((gate_pre * sig * up_pre).astype(bf16))
        grad_act = matmul_back(cot_alls[m], down_w)
        grad_up = grad_act * gate_pre * sig
        grad_gate = grad_act * up_pre * sig * (1.0 + gate_pre * (1.0 - sig))
        grad_gu = jnp.concatenate([grad_gate, grad_up], axis=1).astype(bf16)
        grad_gus.append(grad_gu)

        def hidden_rows(start, end, *late):
            return matmul_back(cut_rows(grad_gu, start, end, late), gate_up_w)

        grad_hiddens.append(scatter_tokens(hidden_rows, tokens))

    def middle_back(m, deps):
        own, arrived, sent = grad_hiddens[m]
        *blocks, wide, gain_grad = rows_call(
            functools.partial(norm_back_kernel, split, places, len(arrived), len(deps), True),
            tokens,
            width,
            split,
            [own, middles[m], cotangent[m, 0]],
            gain_ffn,
            arrived,
            [((SPAN, width), bf16)] * halves + [((tokens, width), f32), ((8, width), f32)],
            deps,
            "middle_back",
        )
        grad_middles.append(wide)
        lows.append(blocks[0])
        gain_ffn_grads.append(gain_grad[0])
        grads_mixed.append(assemble(fetch_tokens(blocks)))

    grad_ys, grad_sides, outs, back, in_backs, outputs = [], [], [], [], [], []

    def heads_back(m, deps):
        grad_mixed = after(grads_mixed[m], *deps)
        grads_mixed[m] = grad_mixed
        grad_gated = matmul_back(grad_mixed, out_w[:inner])
        grad_attended = matmul_back(grad_mixed, out_w[inner:]).astype(bf16)
        gate_z = gate_zs[m]
        sig = jax.nn.sigmoid(gate_z)
        y_wide = ys[m].astype(f32)
        grad_ys.append((grad_gated * gate_z * sig).astype(bf16))
        grad_z = (grad_gated * y_wide * sig * (1.0 + gate_z * (1.0 - sig))).astype(bf16)
        grad_qkv = attend_backward(
            order, earlies[m], tables, auxes[m], seg_rows[m], lses[m], grad_attended, query_heads
        )
        grad_sides.append(jnp.concatenate([grad_qkv, grad_z], axis=1))

    def output_rows(m, deps, hold=()):
        activateds[m] = after(activateds[m], *deps)

        def down_rows(start, end, *late):
            return matmul_rows(cut_rows(activateds[m], start, end, late), down_w)

        outs.append(scatter_tokens(down_rows, tokens, hold))

    def scan_back(m, deps):
        grad_y = after(grad_ys[m], *deps)
        back.append(
            ssd_backward(order, firsts[m], auxes[m], seg_blocks[m], *head_tables, all_starts[m], grad_y, heads)
        )

    def hidden_back(m, deps, hold=(), later=()):
        grad_first = after(back[m][0], *deps)

        def in_rows(start, end, *late):
            one = cut_rows(grad_first, start, end, late + tuple(later if late else ()))
            return matmul_back(one, first_w) + matmul_back(grad_sides[m][start:end], side_w)

        in_backs.append(scatter_tokens(in_rows, tokens, hold))

    def finish_input(m):
        own, arrived, sent = in_backs[m]
        low, gain_grad = rows_call(
            functools.partial(norm_back_kernel, split, places, len(arrived), 0, False),
            tokens,
            width,
            split,
            [own, inputs[m, 0], grad_middles[m]],
            gain_in,
            arrived,
            [((tokens, width), bf16), ((8, width), f32)],
            [],
            "input_back",
        )
        return low, gain_grad[0]

    def finish_output(m):
        own, arrived, sent = outs[m]
        if split:
            arrived = [
                jnp.concatenate([arrived[0][:SPAN], arrived[2][:SPAN]]),
                jnp.concatenate([arrived[1], arrived[3]]),
            ]
        return (middles[m] + own + sum(part.astype(f32) for part in arrived)).astype(bf16)

    def both(lefts, rights):
        return (weight_grad(lefts[0], rights[0]) + weight_grad(lefts[1], rights[1])).astype(bf16)

    def back_to_rows(part):
        return trade(part.reshape(seq, rows, -1)).astype(f32)

    def first_arrived(scattered):
        return scattered[1][::2]

    mixer_out(0, [ys[1], *cot_pieces[2:5]])
    middle_forward(0, ())
    mixer_out(1, mixeds[0][2], [ffn_hiddens[0]])
    feed_forward(0, mixeds[1][2])
    ffn_hiddens[0] = after(ffn_hiddens[0], *grad_hiddens[0][2])
    gate_up_sum = weight_grad(ffn_hiddens[0], grad_gus[0])
    activateds[0] = after(activateds[0], gate_up_sum)
    down_sum = weight_grad(activateds[0], cot_alls[0])
    middle_back(0, [gate_up_sum])
    middle_forward(1, [grads_mixed[0]])
    heads_back(0, [down_sum])
    output_rows(0, grad_sides, [ffn_hiddens[1]])
    feed_forward(1, outs[0][2])
    ffn_hiddens[1] = after(ffn_hiddens[1], *grad_hiddens[1][2])
    gate_up_sum = (gate_up_sum + weight_grad(ffn_hiddens[1], grad_gus[1])).astype(bf16)
    activateds[1] = after(activateds[1], gate_up_sum)
    down_sum = (down_sum + weight_grad(activateds[1], cot_alls[1])).astype(bf16)
    gate_up_part = spread_sums(gate_up_sum)
    down_part = spread_sums(down_sum)
    scan_back(0, [down_sum, *first_arrived(grad_hiddens[1])])
    outputs.append(finish_output(0))
    middle_back(1, [back[0][0], outputs[0]])
    hidden_back(0, [lows[1]], [grads_mixed[1]])
    output_rows(1, in_backs[0][2], [grads_mixed[1]])
    heads_back(1, [*outs[1][2], gate_up_part])
    gate_up_back = back_to_rows(gate_up_part)
    out_ins[0] = after(out_ins[0], grad_sides[1], gate_up_back)
    out_sum = both(out_ins, grads_mixed)
    out_sum = jnp.concatenate(
        [out_sum[:inner].reshape(fsdp, -1, width), out_sum[inner:].reshape(fsdp, -1, width)], axis=1
    ).reshape(inner + q_width, width)
    out_part = spread_sums(out_sum)
    hiddens[0] = after(hiddens[0], out_sum, down_part, *first_arrived(in_backs[0]))
    side_sum = both(hiddens, grad_sides)
    side_part = spread_sums(side_sum)
    input_grads, gain_in_grads = [], []
    low, gain_grad = finish_input(0)
    input_grads.append(low)
    gain_in_grads.append(gain_grad)
    scan_back(1, [side_sum, low, *first_arrived(outs[1])])
    outputs.append(finish_output(1))
    hiddens[0] = after(hiddens[0], outputs[1], out_part)
    first_sum = both(hiddens, [b[0] for b in back])
    first_part = spread_sums(first_sum)
    side_back = back_to_rows(side_part)
    hidden_back(1, [first_sum], (), [side_back])
    low, gain_grad = finish_input(1)
    input_grads.append(low)
    gain_in_grads.append(gain_grad)

    gain_in_grad = gain_in_grads[0] + gain_in_grads[1]
    gain_ffn_grad = gain_ffn_grads[0] + gain_ffn_grads[1]
    conv_grad = (back[0][1] + back[1][1])[: CONV + 1]
    head_grad = back[0][2] + back[1][2]
    rate_sum, bias_sum = head_grad[0, :heads], head_grad[1, :heads]
    skip_sum = jnp.sum((back[0][3] + back[1][3])[0].reshape(heads, SSM_DIM), axis=1)

    def own_columns(block):
        return jnp.swapaxes(block, 0, 1).reshape(rows, -1)

    def kv_columns(block):
        return jnp.concatenate(
            [sum(block[s] for s in range(seq) if kv_of[s] == h) for h in range(KV_HEADS)], axis=1
        )

    gate_grad = own_columns(gate_up_back[:, :, :units])
    up_grad = own_columns(gate_up_back[:, :, units:])
    first_back = back_to_rows(first_part)
    ssm_in_grad = jnp.concatenate(
        [
            own_columns(side_back[:, :, qkv_width:]),
            own_columns(first_back[:, :, :inner]),
            jnp.sum(first_back[:, :, inner : inner + 2 * STATE], axis=0),
            own_columns(first_back[:, :, inner + 2 * STATE : inner + 2 * STATE + heads]),
        ],
        axis=1,
    )
    attn_in_grad = jnp.concatenate(
        [
            own_columns(side_back[:, :, :q_width]),
            kv_columns(side_back[:, :, q_width : q_width + HEAD_DIM]),
            kv_columns(side_back[:, :, q_width + HEAD_DIM : qkv_width]),
        ],
        axis=1,
    )
    out_part = out_part.astype(f32)

    conv_whole = jnp.zeros((CONV + 1, CONV_CH), f32)
    conv_whole = lax.dynamic_update_slice_in_dim(conv_whole, conv_grad[:, :inner], inner_start, 1)
    conv_whole = lax.dynamic_update_slice_in_dim(conv_whole, conv_grad[:, inner:], SSM_INNER, 1)
    head_sums = lax.dynamic_update_slice_in_dim(
        jnp.zeros((3, SSM_HEADS), f32), jnp.stack([rate_sum, bias_sum, skip_sum]), head_start, 1
    )
    pieces = [conv_whole.reshape(-1), head_sums.reshape(-1), gain_in_grad, gain_ffn_grad]
    ends = [0]
    for piece in pieces:
        ends.append(ends[-1] + piece.shape[0])
    total = add_small(jnp.concatenate(pieces))
    conv_total, head_total, gain_in_total, gain_ffn_total = (
        total[a:b] for a, b in zip(ends[:-1], ends[1:])
    )
    place = index * fsdp + lax.axis_index("fsdp")
    conv_total = lax.dynamic_slice_in_dim(conv_total.reshape(CONV + 1, CONV_CH), place * channels, channels, 1)
    head_total = head_total.reshape(3, SSM_HEADS)
    return (
        jnp.stack(outputs)[:, None],
        jnp.stack(input_grads)[:, None],
        lax.dynamic_slice_in_dim(gain_in_total, place * rows, rows),
        ssm_in_grad,
        attn_in_grad,
        conv_total[:CONV],
        conv_total[CONV],
        head_total[0],
        head_total[1],
        head_total[2],
        out_part[:out_rows],
        out_part[out_rows:],
        lax.dynamic_slice_in_dim(gain_ffn_total, place * rows, rows),
        gate_grad,
        up_grad,
        down_part.astype(f32),
    )


def solution(mesh):
    return jax.shard_map(
        on_device,
        mesh=mesh,
        in_specs=(
            P(None, "fsdp", "seq", None),
            P(None, "fsdp", "seq", None),
            P(None, "fsdp", None),
            P(("seq", "fsdp")),
            P(("seq", "fsdp"), None),
            P(("seq", "fsdp"), None),
            P(None, ("seq", "fsdp")),
            P(("seq", "fsdp")),
            P(),
            P(),
            P(),
            P(("seq", "fsdp"), None),
            P(("seq", "fsdp"), None),
            P(("seq", "fsdp")),
            P(("seq", "fsdp"), None),
            P(("seq", "fsdp"), None),
            P(("seq", "fsdp"), None),
        ),
        out_specs=(
            P(None, "fsdp", "seq", None),
            P(None, "fsdp", "seq", None),
            P(("seq", "fsdp")),
            P(("seq", "fsdp"), None),
            P(("seq", "fsdp"), None),
            P(None, ("seq", "fsdp")),
            P(("seq", "fsdp")),
            P(),
            P(),
            P(),
            P(("seq", "fsdp"), None),
            P(("seq", "fsdp"), None),
            P(("seq", "fsdp")),
            P(("seq", "fsdp"), None),
            P(("seq", "fsdp"), None),
            P(("seq", "fsdp"), None),
        ),
        check_vma=False,
    )
```

```python
import functools

import jax
import jax.numpy as jnp
from jax import lax
from jax.experimental import pallas as pl
from jax.experimental.pallas import tpu as pltpu
from jax.sharding import PartitionSpec as P

SSM_HEADS = 48
SSM_DIM = 64
STATE = 256
CONV = 4
Q_HEADS = 8
KV_HEADS = 2
HEAD_DIM = 128
MICRO = 2
SPAN = 128
SSM_INNER = 3072
CONV_CH = 3584
ATT_ROWS = 256
VMEM_BYTES = 48 * 1024 * 1024


PRECISE = lax.Precision.HIGHEST
EPSILON = 1e-05
ROPE_BASE = 10000.0


def work(us):
    return pl.CostEstimate(flops=int(us * 1150000000), bytes_accessed=0, transcendentals=0)


def lanes_iota(shape):
    return lax.broadcasted_iota(jnp.int32, shape, 1)


def rows_iota(shape):
    return lax.broadcasted_iota(jnp.int32, shape, 0)


def dot_last(left, right):
    return lax.dot_general(left, right, (((1,), (1,)), ((), ())), preferred_element_type=jnp.float32)


def dot_first(left, right):
    return lax.dot_general(left, right, (((0,), (0,)), ((), ())), preferred_element_type=jnp.float32)


def dot_plain(left, right):
    return jnp.dot(left, right, preferred_element_type=jnp.float32)


def head_steps(block, head_ref, heads):
    pre = block.astype(jnp.float32) + head_ref[0:1, :]
    live = lanes_iota(pre.shape) < heads
    pre = jnp.where(live, pre, 0.0)
    step = jnp.maximum(pre, 0.0) + jnp.log1p(jnp.exp(-jnp.abs(pre)))
    step = jnp.where(live, step, 0.0)
    rate = -jnp.exp(head_ref[1:2, :])
    decay = rate * step
    lower = (rows_iota((SPAN, SPAN)) >= lanes_iota((SPAN, SPAN))).astype(jnp.float32)
    total = jnp.dot(lower, decay, precision=PRECISE, preferred_element_type=jnp.float32)
    return step, rate, decay, total, pre


def over_lanes(column):
    return jnp.broadcast_to(column, (column.shape[0], 128))


def convolve(ubuf, near, conv_ref, lanes):
    acc = conv_ref[CONV : CONV + 1, lanes] + conv_ref[CONV - 1 : CONV, lanes] * ubuf[8 : 8 + SPAN, lanes]
    for offset in range(1, CONV):
        shifted = ubuf[8 - offset : 8 - offset + SPAN, lanes]
        weight = conv_ref[CONV - 1 - offset : CONV - offset, lanes]
        acc = acc + weight * (shifted * near[offset])
    return acc


def pair_of(values, first_head, low_lanes):
    one = jnp.broadcast_to(values[:, first_head : first_head + 1], (SPAN, 128))
    two = jnp.broadcast_to(values[:, first_head + 1 : first_head + 2], (SPAN, 128))
    return one, two, jnp.where(low_lanes, one, two)


def ssd_forward_kernel(
    heads,
    order_ref,
    first_ref,
    aux_ref,
    seg_ref,
    conv_ref,
    head_ref,
    skip_ref,
    y_ref,
    start_ref,
    ubuf,
    taps,
    state,
):
    f32, bf16 = jnp.float32, jnp.bfloat16
    inner = heads * SSM_DIM
    width = inner + 2 * STATE

    @pl.when(pl.program_id(0) == 0)
    def _():
        ubuf[SPAN : SPAN + 8, :] = jnp.zeros((8, width), f32)
        state[...] = jnp.zeros((STATE, inner), f32)

    ubuf[0:8, :] = ubuf[SPAN : SPAN + 8, :]
    ubuf[8 : 8 + SPAN, :] = first_ref[:, :width].astype(f32)
    near = [None] + [over_lanes(aux_ref[:, 2 + offset : 3 + offset]) for offset in range(1, CONV)]
    for lane in range(0, width, 128):
        lanes = slice(lane, lane + 128)
        pre = convolve(ubuf, near, conv_ref, lanes)
        taps[:, lanes] = (pre * jax.nn.sigmoid(pre)).astype(bf16)
    step, rate, decay, total, unused = head_steps(first_ref[:, width:], head_ref, heads)
    total_rows = total.T
    low_lanes = lanes_iota((SPAN, 128)) < SSM_DIM
    same = (aux_ref[:, 0:1] == seg_ref[0]) & (rows_iota((SPAN, SPAN)) >= lanes_iota((SPAN, SPAN)))
    b_rows = taps[:, inner : inner + STATE]
    c_rows = taps[:, inner + STATE :]
    b_cols = b_rows.astype(f32).T.astype(bf16)
    scores = dot_last(c_rows, b_rows)
    carry_keep, end_keep = over_lanes(aux_ref[:, 1:2]), over_lanes(aux_ref[:, 2:3])
    for pair in range(heads // 2):
        lanes = slice(pair * 128, pair * 128 + 128)
        sum_one, sum_two, sums = pair_of(total, 2 * pair, low_lanes)
        steps = pair_of(step, 2 * pair, low_lanes)[2]
        row_one = total_rows[2 * pair : 2 * pair + 1, :]
        row_two = total_rows[2 * pair + 1 : 2 * pair + 2, :]
        mix_one = (jnp.exp(jnp.where(same, sum_one - row_one, -1e30)) * scores).astype(bf16)
        mix_two = (jnp.exp(jnp.where(same, sum_two - row_two, -1e30)) * scores).astype(bf16)
        x = taps[:, lanes].astype(f32)
        stepped = (x * steps).astype(bf16)
        none = jnp.zeros_like(stepped)
        split = jnp.concatenate(
            [jnp.where(low_lanes, stepped, none), jnp.where(low_lanes, none, stepped)], axis=0
        )
        held = state[:, lanes]
        held_low = held.astype(bf16)
        start_ref[0, :, lanes] = held_low
        y = dot_plain(jnp.concatenate([mix_one, mix_two], axis=1), split)
        y = y + jnp.exp(sums) * carry_keep * dot_plain(c_rows, held_low)
        y_ref[:, lanes] = (y + skip_ref[0:1, lanes] * x).astype(bf16)
        last = sums[SPAN - 1 : SPAN, :]
        weighted = (jnp.exp(last - sums) * end_keep * stepped.astype(f32)).astype(bf16)
        kept = jnp.exp(last) * aux_ref[SPAN - 1 : SPAN, 1:2]
        state[:, lanes] = held * kept + dot_plain(b_cols, weighted)


def halves_of(values):
    high = values.astype(jnp.bfloat16)
    return [high, (values - high.astype(jnp.float32)).astype(jnp.bfloat16)]


def ssd_backward_kernel(
    heads,
    order_ref,
    first_ref,
    before_ref,
    aux_ref,
    seg_ref,
    conv_ref,
    head_ref,
    skip_ref,
    start_ref,
    dy_ref,
    grad_ref,
    conv_grad_ref,
    head_grad_ref,
    skip_grad_ref,
    ubuf,
    taps,
    slope,
    gbuf,
    dstate,
):
    f32, bf16 = jnp.float32, jnp.bfloat16
    inner = heads * SSM_DIM
    width = inner + 2 * STATE

    @pl.when(pl.program_id(0) == 0)
    def _():
        gbuf[0:8, :] = jnp.zeros((8, width), f32)
        dstate[...] = jnp.zeros((STATE, inner), f32)
        conv_grad_ref[...] = jnp.zeros(conv_grad_ref.shape, f32)
        head_grad_ref[...] = jnp.zeros(head_grad_ref.shape, f32)
        skip_grad_ref[...] = jnp.zeros(skip_grad_ref.shape, f32)

    ubuf[0:8, :] = before_ref[8:16, :width].astype(f32)
    ubuf[8 : 8 + SPAN, :] = first_ref[:, :width].astype(f32)
    gbuf[SPAN : SPAN + 8, :] = gbuf[0:8, :]
    near = [None] + [over_lanes(aux_ref[:, 2 + offset : 3 + offset]) for offset in range(1, CONV)]
    for lane in range(0, width, 128):
        lanes = slice(lane, lane + 128)
        pre = convolve(ubuf, near, conv_ref, lanes)
        sig = jax.nn.sigmoid(pre)
        taps[:, lanes] = (pre * sig).astype(bf16)
        slope[:, lanes] = sig * (1.0 + pre * (1.0 - sig))
    step, rate, decay, total, pre_step = head_steps(first_ref[:, width:], head_ref, heads)
    total_rows = total.T
    square = (SPAN, SPAN)
    low_lanes = lanes_iota((SPAN, 128)) < SSM_DIM
    low_row = lanes_iota((1, 128)) < SSM_DIM
    head_row = lanes_iota((1, 128))
    same = (aux_ref[:, 0:1] == seg_ref[0]) & (rows_iota(square) >= lanes_iota(square))
    b_rows = taps[:, inner : inner + STATE]
    c_rows = taps[:, inner + STATE :]
    c_cols = c_rows.astype(f32).T.astype(bf16)
    scores = dot_last(c_rows, b_rows)
    carry_keep, end_keep = over_lanes(aux_ref[:, 1:2]), over_lanes(aux_ref[:, 2:3])
    head_lane = lanes_iota((SPAN, 128))
    is_last = rows_iota((SPAN, 1)) == SPAN - 1
    grad_scores = jnp.zeros(square, f32)
    grad_b = jnp.zeros((SPAN, STATE), f32)
    grad_c = jnp.zeros((SPAN, STATE), f32)
    grad_total = jnp.zeros((SPAN, 128), f32)
    grad_step = jnp.zeros((SPAN, 128), f32)
    for pair in range(heads // 2):
        lanes = slice(pair * 128, pair * 128 + 128)
        sum_one, sum_two, sums = pair_of(total, 2 * pair, low_lanes)
        steps = pair_of(step, 2 * pair, low_lanes)[2]
        row_one = total_rows[2 * pair : 2 * pair + 1, :]
        row_two = total_rows[2 * pair + 1 : 2 * pair + 2, :]
        decay_one = jnp.exp(jnp.where(same, sum_one - row_one, -1e30))
        decay_two = jnp.exp(jnp.where(same, sum_two - row_two, -1e30))
        mix_one = (decay_one * scores).astype(bf16)
        mix_two = (decay_two * scores).astype(bf16)
        x = taps[:, lanes].astype(f32)
        stepped = (x * steps).astype(bf16)
        none = jnp.zeros_like(stepped)
        x_one = jnp.where(low_lanes, stepped, none)
        x_two = jnp.where(low_lanes, none, stepped)
        dy_low = dy_ref[:, lanes]
        dy = dy_low.astype(f32)
        dy_one = jnp.where(low_lanes, dy_low, none)
        dy_two = jnp.where(low_lanes, none, dy_low)
        grad_scores = grad_scores + dot_last(dy_one, stepped) * decay_one + dot_last(dy_two, stepped) * decay_two
        y = dot_plain(
            jnp.concatenate([mix_one, mix_two], axis=1), jnp.concatenate([x_one, x_two], axis=0)
        )
        grad_in = dot_first(
            jnp.concatenate([mix_one, mix_two], axis=0), jnp.concatenate([dy_one, dy_two], axis=0)
        )
        held = start_ref[0, :, lanes]
        dheld = dstate[:, lanes]
        dheld_low = dheld.astype(bf16)
        grown = jnp.exp(sums) * carry_keep
        y = y + grown * dot_plain(c_rows, held)
        grown_dy = (grown * dy).astype(bf16)
        last = sums[SPAN - 1 : SPAN, :]
        fade = jnp.exp(last - sums) * end_keep
        stepped_wide = stepped.astype(f32)
        weighted = (fade * stepped_wide).astype(bf16)
        from_end = dot_plain(b_rows, dheld_low)
        grad_in = grad_in + fade * from_end
        grad_c = grad_c + dot_last(grown_dy, held)
        grad_b = grad_b + dot_last(weighted, dheld_low)
        kept = jnp.exp(last) * aux_ref[SPAN - 1 : SPAN, 1:2]
        ends = jnp.sum(fade * stepped_wide * from_end, axis=0, keepdims=True) + kept * jnp.sum(
            dheld * held.astype(f32), axis=0, keepdims=True
        )
        dstate[:, lanes] = dheld * kept + dot_plain(c_cols, grown_dy)
        gaps = dy * y - stepped_wide * grad_in
        by_step = x * grad_in
        ends_one = jnp.sum(jnp.where(low_row, ends, 0.0), axis=1, keepdims=True)
        ends_two = jnp.sum(jnp.where(low_row, 0.0, ends), axis=1, keepdims=True)
        ends_here = jnp.where(head_row == 2 * pair, ends_one, jnp.where(head_row == 2 * pair + 1, ends_two, 0.0))
        of_head = (lanes_iota(square) == 2 * pair + rows_iota(square) // SSM_DIM).astype(bf16)
        by_head = dot_plain(jnp.concatenate(halves_of(gaps) + halves_of(by_step), axis=0), of_head)
        grad_total = grad_total + by_head[:SPAN] + by_head[SPAN : 2 * SPAN] + jnp.where(is_last, ends_here, 0.0)
        grad_step = grad_step + by_head[2 * SPAN : 3 * SPAN] + by_head[3 * SPAN :]
        skip = skip_ref[0:1, lanes]
        skip_grad_ref[0:1, lanes] += jnp.sum(dy * x, axis=0, keepdims=True)
        gbuf[0:SPAN, lanes] = (steps * grad_in + skip * dy) * slope[:, lanes]
    low_scores = grad_scores.astype(bf16)
    grad_c = grad_c + dot_plain(low_scores, b_rows)
    grad_b = grad_b + dot_first(low_scores, c_rows)
    gbuf[0:SPAN, inner : inner + STATE] = grad_b * slope[:, inner : inner + STATE]
    gbuf[0:SPAN, inner + STATE : width] = grad_c * slope[:, inner + STATE : width]

    upper = (rows_iota(square) <= lanes_iota(square)).astype(f32)
    grad_decay = jnp.dot(upper, grad_total, precision=PRECISE, preferred_element_type=f32)
    grad_pre = (grad_step + rate * grad_decay) * jax.nn.sigmoid(pre_step)
    grad_pre = jnp.where(head_lane < heads, grad_pre, 0.0)
    grad_ref[:, width:] = grad_pre.astype(bf16)
    head_grad_ref[0:1, :] += jnp.sum(grad_decay * decay, axis=0, keepdims=True)
    head_grad_ref[1:2, :] += jnp.sum(grad_pre, axis=0, keepdims=True)

    ahead = [None] + [over_lanes(aux_ref[:, 5 + offset : 6 + offset]) for offset in range(1, CONV)]
    for lane in range(0, width, 128):
        lanes = slice(lane, lane + 128)
        grad = gbuf[0:SPAN, lanes]
        conv_grad_ref[CONV : CONV + 1, lanes] += jnp.sum(grad, axis=0, keepdims=True)
        conv_grad_ref[CONV - 1 : CONV, lanes] += jnp.sum(grad * ubuf[8 : 8 + SPAN, lanes], axis=0, keepdims=True)
        acc = conv_ref[CONV - 1 : CONV, lanes] * grad
        for offset in range(1, CONV):
            at = CONV - 1 - offset
            shifted = ubuf[8 - offset : 8 - offset + SPAN, lanes] * near[offset]
            conv_grad_ref[at : at + 1, lanes] += jnp.sum(grad * shifted, axis=0, keepdims=True)
            later = gbuf[offset : offset + SPAN, lanes] * ahead[offset]
            acc = acc + conv_ref[at : at + 1, lanes] * later
        grad_ref[:, lanes] = acc.astype(bf16)


def token_aux(segment):
    length = segment.shape[0]
    ends = segment.reshape(-1, SPAN)[:, -1]
    end_of = jnp.repeat(ends, SPAN)
    before = jnp.repeat(jnp.concatenate([jnp.full((1,), -1, segment.dtype), ends[:-1]]), SPAN)
    columns = [segment, segment == before, segment == end_of]
    for offset in range(1, CONV):
        columns.append(jnp.pad(segment, (offset, 0), constant_values=-1)[:length] == segment)
    for offset in range(1, CONV):
        columns.append(jnp.pad(segment, (0, offset), constant_values=-1)[offset:] == segment)
    columns = [column.astype(jnp.float32) for column in columns]
    return jnp.stack(columns + [jnp.zeros((length,), jnp.float32)] * (16 - len(columns)), axis=1)


def ssd_specs(heads, at):
    inner = heads * SSM_DIM
    width = inner + 2 * STATE
    return [
        pl.BlockSpec((SPAN, width + 128), lambda i, order: (order[at(i)], 0)),
        pl.BlockSpec((SPAN, 16), lambda i, order: (at(i), 0)),
        pl.BlockSpec((1, 1, SPAN), lambda i, order: (at(i), 0, 0)),
        pl.BlockSpec((8, width), lambda i, order: (0, 0)),
        pl.BlockSpec((8, 128), lambda i, order: (0, 0)),
        pl.BlockSpec((8, inner), lambda i, order: (0, 0)),
    ]


def ssd_forward(order, first, aux, seg_rows, conv, head, skip, heads):
    length = first.shape[0]
    inner = heads * SSM_DIM
    width = inner + 2 * STATE
    blocks = length // SPAN
    return pl.pallas_call(
        functools.partial(ssd_forward_kernel, heads),
        grid_spec=pltpu.PrefetchScalarGridSpec(
            num_scalar_prefetch=1,
            grid=(blocks,),
            in_specs=ssd_specs(heads, lambda i: i),
            out_specs=[
                pl.BlockSpec((SPAN, inner), lambda i, order: (order[i], 0)),
                pl.BlockSpec((1, STATE, inner), lambda i, order: (i, 0, 0)),
            ],
            scratch_shapes=[
                pltpu.VMEM((SPAN + 8, width), jnp.float32),
                pltpu.VMEM((SPAN, width), jnp.bfloat16),
                pltpu.VMEM((STATE, inner), jnp.float32),
            ],
        ),
        out_shape=[
            jax.ShapeDtypeStruct((length, inner), jnp.bfloat16),
            jax.ShapeDtypeStruct((blocks, STATE, inner), jnp.bfloat16),
        ],
        compiler_params=pltpu.CompilerParams(
            dimension_semantics=("arbitrary",), vmem_limit_bytes=VMEM_BYTES
        ),
        cost_estimate=work(15),
        name="ssd_forward",
    )(order, first, aux, seg_rows, conv, head, skip)


def ssd_backward(order, first, aux, seg_rows, conv, head, skip, starts, dy, heads):
    length = first.shape[0]
    inner = heads * SSM_DIM
    width = inner + 2 * STATE
    blocks = length // SPAN
    per_block = SPAN // 16

    def at(i):
        return blocks - 1 - i

    specs = ssd_specs(heads, at)
    specs.insert(
        1,
        pl.BlockSpec(
            (16, width + 128), lambda i, order: (order[jnp.maximum(at(i) - 1, 0)] * per_block + per_block - 1, 0)
        ),
    )
    specs += [
        pl.BlockSpec((1, STATE, inner), lambda i, order: (at(i), 0, 0)),
        pl.BlockSpec((SPAN, inner), lambda i, order: (order[at(i)], 0)),
    ]
    return pl.pallas_call(
        functools.partial(ssd_backward_kernel, heads),
        grid_spec=pltpu.PrefetchScalarGridSpec(
            num_scalar_prefetch=1,
            grid=(blocks,),
            in_specs=specs,
            out_specs=[
                pl.BlockSpec((SPAN, width + 128), lambda i, order: (order[at(i)], 0)),
                pl.BlockSpec((8, width), lambda i, order: (0, 0)),
                pl.BlockSpec((8, 128), lambda i, order: (0, 0)),
                pl.BlockSpec((8, inner), lambda i, order: (0, 0)),
            ],
            scratch_shapes=[
                pltpu.VMEM((SPAN + 8, width), jnp.float32),
                pltpu.VMEM((SPAN, width), jnp.bfloat16),
                pltpu.VMEM((SPAN, width), jnp.float32),
                pltpu.VMEM((SPAN + 8, width), jnp.float32),
                pltpu.VMEM((STATE, inner), jnp.float32),
            ],
        ),
        out_shape=[
            jax.ShapeDtypeStruct((length, width + 128), jnp.bfloat16),
            jax.ShapeDtypeStruct((8, width), jnp.float32),
            jax.ShapeDtypeStruct((8, 128), jnp.float32),
            jax.ShapeDtypeStruct((8, inner), jnp.float32),
        ],
        compiler_params=pltpu.CompilerParams(
            dimension_semantics=("arbitrary",), vmem_limit_bytes=VMEM_BYTES
        ),
        cost_estimate=work(53),
        name="ssd_backward",
    )(order, first, first, aux, seg_rows, conv, head, skip, starts, dy)


def rotary_tables(length):
    half = HEAD_DIM // 2
    frequency = ROPE_BASE ** (-jnp.arange(half).astype(jnp.float32) / half)
    angles = jnp.arange(length, dtype=jnp.int32).astype(jnp.float32)[:, None] * frequency[None, :]
    cosine, sine = jnp.cos(angles), jnp.sin(angles)
    return jnp.concatenate([cosine, cosine], axis=1), jnp.concatenate([-sine, sine], axis=1)


def turn(rows, cosine, sine):
    wide = rows.astype(jnp.float32)
    return (wide * cosine + pltpu.roll(wide, HEAD_DIM // 2, 1) * sine).astype(jnp.bfloat16)


def turn_back(grads, cosine, sine):
    return (grads * cosine + pltpu.roll(grads * sine, HEAD_DIM // 2, 1)).astype(jnp.bfloat16)


def block_scores(q_block, k_part, first_row, seg_col, seg_row):
    scores = dot_last(q_block, k_part) * HEAD_DIM ** (-0.5)
    shape = scores.shape
    allowed = (rows_iota(shape) + first_row >= lanes_iota(shape)) & (seg_col == seg_row)
    return jnp.where(allowed, scores, -1e30)


def place_of(order_ref, block):
    return pl.ds(pl.multiple_of(order_ref[block] * SPAN, SPAN), SPAN)


def load_keys(order_ref, qkv_ref, q_width, cos_ref, sin_ref, k_rot, value):
    for block in range(qkv_ref.shape[0] // SPAN):
        there, here = place_of(order_ref, block), slice(block * SPAN, (block + 1) * SPAN)
        k_rot[here, :] = turn(qkv_ref[there, q_width : q_width + HEAD_DIM], cos_ref[here, :], sin_ref[here, :])
        value[here, :] = qkv_ref[there, q_width + HEAD_DIM : q_width + 2 * HEAD_DIM]


def load_rows(order_ref, ref, start, count, lanes):
    blocks = range(start // SPAN, (start + count) // SPAN)
    return jnp.concatenate([ref[place_of(order_ref, block), lanes] for block in blocks], axis=0)


def store_rows(order_ref, ref, start, lanes, values):
    for part in range(values.shape[0] // SPAN):
        ref[place_of(order_ref, start // SPAN + part), lanes] = values[part * SPAN : (part + 1) * SPAN, :]


def attend_forward_kernel(
    query_heads, block, order_ref, qkv_ref, cos_ref, sin_ref, aux_ref, seg_ref, out_ref, lse_ref, k_rot, value
):
    length = qkv_ref.shape[0]
    load_keys(order_ref, qkv_ref, query_heads * HEAD_DIM, cos_ref, sin_ref, k_rot, value)
    for start in range(0, length, block):
        rows = slice(start, start + block)
        end = start + block
        for head in range(query_heads):
            lanes = slice(head * HEAD_DIM, (head + 1) * HEAD_DIM)
            q_rows = load_rows(order_ref, qkv_ref, start, block, lanes)
            q_block = turn(q_rows, cos_ref[rows, :], sin_ref[rows, :])
            scores = block_scores(q_block, k_rot[:end, :], start, aux_ref[rows, 0:1], seg_ref[:, :end])
            top = jnp.max(scores, axis=1, keepdims=True)
            raised = jnp.exp(scores - top)
            total = jnp.sum(raised, axis=1, keepdims=True)
            probs = (raised * (1.0 / total)).astype(jnp.bfloat16)
            store_rows(order_ref, out_ref, start, lanes, dot_plain(probs, value[:end, :]).astype(jnp.bfloat16))
            lse_ref[rows, head : head + 1] = top + jnp.log(total)


def attend_backward_kernel(
    query_heads,
    block,
    order_ref,
    qkv_ref,
    cos_ref,
    sin_ref,
    aux_ref,
    seg_ref,
    lse_ref,
    grad_ref,
    out_ref,
    k_rot,
    value,
    dk,
    dv,
):
    f32, bf16 = jnp.float32, jnp.bfloat16
    length = qkv_ref.shape[0]
    q_width = query_heads * HEAD_DIM
    load_keys(order_ref, qkv_ref, q_width, cos_ref, sin_ref, k_rot, value)
    dk[...] = jnp.zeros(dk.shape, f32)
    dv[...] = jnp.zeros(dv.shape, f32)
    for start in range(0, length, block):
        rows = slice(start, start + block)
        end = start + block
        for head in range(query_heads):
            lanes = slice(head * HEAD_DIM, (head + 1) * HEAD_DIM)
            cosine, sine = cos_ref[rows, :], sin_ref[rows, :]
            q_block = turn(load_rows(order_ref, qkv_ref, start, block, lanes), cosine, sine)
            scores = block_scores(q_block, k_rot[:end, :], start, aux_ref[rows, 0:1], seg_ref[:, :end])
            probs = jnp.exp(scores - lse_ref[rows, head : head + 1])
            grad = load_rows(order_ref, grad_ref, start, block, lanes)
            grad_probs = dot_last(grad, value[:end, :])
            mean = jnp.sum(grad_probs * probs, axis=1, keepdims=True)
            grad_scores = (probs * (grad_probs - mean) * HEAD_DIM ** (-0.5)).astype(bf16)
            grad_query = turn_back(dot_plain(grad_scores, k_rot[:end, :]), cosine, sine)
            store_rows(order_ref, out_ref, start, lanes, grad_query)
            dk[:end, :] += dot_first(grad_scores, q_block)
            dv[:end, :] += dot_first(probs.astype(bf16), grad)
    k_lanes = slice(q_width, q_width + HEAD_DIM)
    v_lanes = slice(q_width + HEAD_DIM, q_width + 2 * HEAD_DIM)
    store_rows(order_ref, out_ref, 0, k_lanes, turn_back(dk[...], cos_ref[...], sin_ref[...]))
    store_rows(order_ref, out_ref, 0, v_lanes, dv[...].astype(bf16))


def attend_specs(arrays):
    return [pl.BlockSpec(memory_space=pltpu.SMEM)] + [pl.BlockSpec(memory_space=pltpu.VMEM)] * arrays


def attend_forward(order, early, tables, aux, seg_row, query_heads):
    length = early.shape[0]
    return pl.pallas_call(
        functools.partial(attend_forward_kernel, query_heads, min(ATT_ROWS, length)),
        in_specs=attend_specs(5),
        out_shape=[
            jax.ShapeDtypeStruct((length, query_heads * HEAD_DIM), jnp.bfloat16),
            jax.ShapeDtypeStruct((length, 8), jnp.float32),
        ],
        scratch_shapes=[pltpu.VMEM((length, HEAD_DIM), jnp.bfloat16), pltpu.VMEM((length, HEAD_DIM), jnp.bfloat16)],
        compiler_params=pltpu.CompilerParams(vmem_limit_bytes=VMEM_BYTES),
        cost_estimate=work(5),
        name="attend_forward",
    )(order, early, tables[0], tables[1], aux, seg_row)


def attend_backward(order, early, tables, aux, seg_row, lse, grad, query_heads):
    length = early.shape[0]
    return pl.pallas_call(
        functools.partial(attend_backward_kernel, query_heads, min(ATT_ROWS, length)),
        in_specs=attend_specs(7),
        out_shape=jax.ShapeDtypeStruct((length, (query_heads + 2) * HEAD_DIM), jnp.bfloat16),
        scratch_shapes=[
            pltpu.VMEM((length, HEAD_DIM), jnp.bfloat16),
            pltpu.VMEM((length, HEAD_DIM), jnp.bfloat16),
            pltpu.VMEM((length, HEAD_DIM), jnp.float32),
            pltpu.VMEM((length, HEAD_DIM), jnp.float32),
        ],
        compiler_params=pltpu.CompilerParams(vmem_limit_bytes=VMEM_BYTES),
        cost_estimate=work(7),
        name="attend_backward",
    )(order, early, tables[0], tables[1], aux, seg_row, lse, grad)


def after_kernel(*refs):
    pass


def after(value, *others):
    return pl.pallas_call(
        after_kernel,
        in_specs=[pl.BlockSpec(memory_space=pl.ANY)] * (1 + len(others)),
        out_specs=pl.BlockSpec(memory_space=pl.ANY),
        out_shape=jax.ShapeDtypeStruct(value.shape, value.dtype),
        input_output_aliases={0: 0},
        name="after",
    )(value, *others)


def move_blocks(tiles, width, here, there):
    per = 128 // width
    lane = lanes_iota(tiles[0].shape)
    moved = []
    for tile in range(len(tiles)):
        out = None
        for part in range(per):
            source = there(tile * per + part)
            piece = tiles[source // per]
            shift = ((part - source % per) * width) % 128
            if shift:
                piece = pltpu.roll(piece, shift, 1)
            out = piece if out is None else jnp.where(lane >= part * width, piece, out)
        moved.append(out)
    return moved


def to_gathered_tiles(tiles, width, seq, fsdp):
    return move_blocks(tiles, width, None, lambda b: (b % seq) * fsdp + b // seq)


def from_gathered_tiles(tiles, width, seq, fsdp):
    return move_blocks(tiles, width, None, lambda b: (b % fsdp) * seq + b // fsdp)


def tiles_of(array):
    return [array[:, lane : lane + 128] for lane in range(0, array.shape[1], 128)]


def add_arrived(own, arrived):
    total = own[...]
    for ref in arrived:
        total = total + ref[...].astype(jnp.float32)
    return total


def row_sum(tiles):
    total = tiles[0]
    for tile in tiles[1:]:
        total = total + tile
    return jnp.sum(total, axis=1, keepdims=True)


def middle_kernel(places, count, skip, own, rows, gain, *refs):
    arrived, (hidden_ref, middle_ref) = refs[:count], refs[count + skip :]
    middle = rows[...].astype(jnp.float32) + add_arrived(own, arrived)
    middle_ref[...] = middle
    mean = jnp.sum(middle * middle, axis=1, keepdims=True) / middle.shape[1]
    hidden = middle * lax.rsqrt(mean + EPSILON) * gain[0:1, :]
    moved = to_gathered_tiles(tiles_of(hidden), *places)
    hidden_ref[...] = jnp.concatenate(moved, axis=1).astype(jnp.bfloat16)


def norm_back_kernel(places, count, skip, keep_wide, own, rows, passed, gain, *refs):
    arrived, outs = refs[:count], refs[count + skip :]
    grads = add_arrived(own, arrived)
    grads = jnp.concatenate(from_gathered_tiles(tiles_of(grads), *places), axis=1)
    wide = rows[...].astype(jnp.float32)
    width = wide.shape[1]
    scale = lax.rsqrt(jnp.sum(wide * wide, axis=1, keepdims=True) / width + EPSILON)
    normed = wide * scale
    weighted = grads * gain[0:1, :]
    mean = jnp.sum(weighted * normed, axis=1, keepdims=True) / width
    total = passed[...].astype(jnp.float32) + scale * (weighted - normed * mean)
    outs[0][...] = total.astype(jnp.bfloat16)
    if keep_wide:
        outs[1][...] = total
    gain_grad = outs[-1]

    @pl.when(pl.program_id(0) == 0)
    def _():
        gain_grad[...] = jnp.zeros(gain_grad.shape, jnp.float32)

    gain_grad[0:1, :] += jnp.sum(normed * grads, axis=0, keepdims=True)


def add_rows_kernel(count, own, rows, gain, *refs):
    refs[-1][...] = (rows[...] + add_arrived(own, refs[:count])).astype(refs[-1].dtype)


def rows_call(kernel, tokens, width, inputs, gain, arrived, outs, deps, name):
    block = pl.BlockSpec((SPAN, width), lambda i: (i, 0))
    whole = pl.BlockSpec((8, width), lambda i: (0, 0))
    out_specs = [whole if shape[0] == 8 else block for shape, dtype in outs]
    return pl.pallas_call(
        kernel,
        grid=(tokens // SPAN,),
        in_specs=[block] * len(inputs)
        + [whole]
        + [block] * len(arrived)
        + [pl.BlockSpec(memory_space=pl.ANY)] * len(deps),
        out_specs=out_specs,
        out_shape=[jax.ShapeDtypeStruct(shape, dtype) for shape, dtype in outs],
        compiler_params=pltpu.CompilerParams(
            dimension_semantics=("arbitrary",), vmem_limit_bytes=VMEM_BYTES
        ),
        cost_estimate=work(5),
        name=name,
    )(*inputs, gain, *arrived, *deps)


def norm_pieces_kernel(gain, *refs):
    pieces, out = refs[:-1], refs[-1]
    for block, piece in enumerate(pieces):

        @pl.when(pl.program_id(0) == block)
        def _(piece=piece):
            wide = piece[...].astype(jnp.float32)
            mean = jnp.sum(wide * wide, axis=1, keepdims=True) / wide.shape[1]
            out[...] = (wide * lax.rsqrt(mean + EPSILON) * gain[0:1, :]).astype(jnp.bfloat16)


def norm_pieces(pieces, spots, gain):
    width = pieces[0].shape[1]
    length = len(spots) * SPAN
    return pl.pallas_call(
        norm_pieces_kernel,
        grid=(len(spots),),
        in_specs=[pl.BlockSpec((8, width), lambda i: (0, 0))]
        + [pl.BlockSpec((SPAN, width), functools.partial(lambda half, i: (half, 0), half)) for piece, half in spots],
        out_specs=pl.BlockSpec((SPAN, width), lambda i: (i, 0)),
        out_shape=jax.ShapeDtypeStruct((length, width), jnp.bfloat16),
        compiler_params=pltpu.CompilerParams(
            dimension_semantics=("arbitrary",), vmem_limit_bytes=VMEM_BYTES
        ),
        cost_estimate=work(5),
        name="norm_pieces",
    )(gain, *[pieces[piece] for piece, half in spots])


def assemble_kernel(count, spots, *refs):
    pieces, out, held, sems = refs[:count], refs[-3], refs[-2], refs[-1]
    places = [pl.ds(block * SPAN, SPAN) for block in range(len(spots))]
    loads = [
        pltpu.make_async_copy(pieces[piece].at[places[half]], held.at[places[b]], sems.at[0, b])
        for b, (piece, half) in enumerate(spots)
    ]
    stores = [
        pltpu.make_async_copy(held.at[places[b]], out.at[places[b]], sems.at[1, b]) for b in range(len(spots))
    ]
    for load in loads:
        load.start()
    for load, store in zip(loads, stores):
        load.wait()
        store.start()
    for store in stores:
        store.wait()


def assemble(pieces, spots):
    width = pieces[0].shape[1]
    length = len(spots) * SPAN
    return pl.pallas_call(
        functools.partial(assemble_kernel, len(pieces), spots),
        in_specs=[pl.BlockSpec(memory_space=pl.ANY)] * len(pieces),
        out_specs=pl.BlockSpec(memory_space=pl.ANY),
        out_shape=jax.ShapeDtypeStruct((length, width), pieces[0].dtype),
        scratch_shapes=[
            pltpu.VMEM((length, width), pieces[0].dtype),
            pltpu.SemaphoreType.DMA((2, len(spots))),
        ],
        compiler_params=pltpu.CompilerParams(vmem_limit_bytes=VMEM_BYTES),
        cost_estimate=work(3),
        name="assemble",
    )(*pieces)


def start_rows_kernel(places, halves, rows, cot, out):
    @pl.when(pl.program_id(0) < halves)
    def _():
        moved = to_gathered_tiles(tiles_of(rows[...].astype(jnp.float32)), *places)
        out[...] = jnp.concatenate(moved, axis=1).astype(out.dtype)

    @pl.when(pl.program_id(0) >= halves)
    def _():
        out[...] = cot[...]


def start_rows(rows, cot, places):
    tokens, width = rows.shape
    halves = tokens // SPAN

    return pl.pallas_call(
        functools.partial(start_rows_kernel, places, halves),
        grid=(2 * halves,),
        in_specs=[
            pl.BlockSpec((SPAN, width), lambda i: (jnp.minimum(i, halves - 1), 0)),
            pl.BlockSpec((SPAN, width), lambda i: (jnp.maximum(i - halves, 0), 0)),
        ],
        out_specs=pl.BlockSpec((SPAN, width), lambda i: (i, 0)),
        out_shape=jax.ShapeDtypeStruct((2 * tokens, width), rows.dtype),
        compiler_params=pltpu.CompilerParams(
            dimension_semantics=("arbitrary",), vmem_limit_bytes=VMEM_BYTES
        ),
        cost_estimate=work(2),
        name="start_rows",
    )(rows, cot)


def product_kernel(back, pairs, skip, sets, *refs):
    lefts, rights, outs = refs[:pairs], refs[pairs : 2 * pairs], refs[2 * pairs + skip :]
    blocks = lefts[0].shape[0] // SPAN
    where = {block: (out, place) for out, held in enumerate(sets) for place, block in enumerate(held)}
    for block in range(0, blocks, 2):
        total = None
        for left, right in zip(lefts, rights):
            rows = left[block * SPAN : (block + 2) * SPAN, :]
            part = dot_last(rows, right[...]) if back else dot_plain(rows, right[...])
            total = part if total is None else total + part
        for half in range(2):
            out, place = where[block + half]
            part = total[half * SPAN : (half + 1) * SPAN, :]
            outs[out][place * SPAN : (place + 1) * SPAN, :] = part.astype(outs[out].dtype)


def product_rows(lefts, rights, back, sets, dtypes, deps=()):
    length = lefts[0].shape[0]
    width = rights[0].shape[0 if back else 1]
    slab = 512
    specs = [pl.BlockSpec(left.shape, lambda n: (0, 0)) for left in lefts]
    for right in rights:
        if back:
            specs.append(pl.BlockSpec((slab, right.shape[1]), lambda n: (n, 0)))
        else:
            specs.append(pl.BlockSpec((right.shape[0], slab), lambda n: (0, n)))
    return pl.pallas_call(
        functools.partial(product_kernel, back, len(lefts), len(deps), sets),
        grid=(width // slab,),
        in_specs=specs + [pl.BlockSpec(memory_space=pl.ANY)] * len(deps),
        out_specs=[pl.BlockSpec((len(held) * SPAN, slab), lambda n: (0, n)) for held in sets],
        out_shape=[
            jax.ShapeDtypeStruct((len(held) * SPAN, width), dtype) for held, dtype in zip(sets, dtypes)
        ],
        compiler_params=pltpu.CompilerParams(
            dimension_semantics=("arbitrary",), vmem_limit_bytes=VMEM_BYTES
        ),
        cost_estimate=work(sum(2 * length * left.shape[1] * width for left in lefts) / 0.66e9),
        name="product_rows",
    )(*lefts, *rights, *deps)


def feed_kernel(units, slab, hidden, cot, gate_w, up_w, down_w, act_ref, grad_ref):
    here = pl.multiple_of(pl.program_id(0) * slab, slab)
    for row in range(0, hidden.shape[0], 256):
        rows = slice(row, row + 256)
        gate_pre = dot_plain(hidden[rows, :], gate_w[...])
        up_pre = dot_plain(hidden[rows, :], up_w[...])
        grad_act = dot_last(cot[rows, :], down_w[...])
        sig = jax.nn.sigmoid(gate_pre)
        silu = gate_pre * sig
        act_ref[rows, :] = (silu * up_pre).astype(jnp.bfloat16)
        grad_gate = grad_act * up_pre * sig * (1.0 + gate_pre * (1.0 - sig))
        grad_ref[rows, pl.ds(here, slab)] = grad_gate.astype(jnp.bfloat16)
        grad_ref[rows, pl.ds(units + here, slab)] = (grad_act * silu).astype(jnp.bfloat16)


def feed_products(hidden, cot, gate_up_w, down_w):
    length, width = hidden.shape
    units = down_w.shape[0]
    slab = min(256, units)
    steps = units // slab
    whole = pl.BlockSpec((length, width), lambda n: (0, 0))
    return pl.pallas_call(
        functools.partial(feed_kernel, units, slab),
        grid=(steps,),
        in_specs=[
            whole,
            whole,
            pl.BlockSpec((width, slab), lambda n: (0, n)),
            pl.BlockSpec((width, slab), lambda n: (0, steps + n)),
            pl.BlockSpec((slab, width), lambda n: (n, 0)),
        ],
        out_specs=[
            pl.BlockSpec((length, slab), lambda n: (0, n)),
            pl.BlockSpec((length, 2 * units), lambda n: (0, 0)),
        ],
        out_shape=[
            jax.ShapeDtypeStruct((length, units), jnp.bfloat16),
            jax.ShapeDtypeStruct((length, 2 * units), jnp.bfloat16),
        ],
        compiler_params=pltpu.CompilerParams(
            dimension_semantics=("arbitrary",), vmem_limit_bytes=VMEM_BYTES
        ),
        cost_estimate=work(6 * length * width * units / 0.6e9),
        name="feed_products",
    )(hidden, cot, gate_up_w, gate_up_w, down_w)


def sums_kernel(pairs, before, skip, *refs):
    out = refs[-1]
    total = refs[2 * pairs][...] if before else None
    for left, right in zip(refs[:pairs], refs[pairs : 2 * pairs]):
        part = dot_first(left[...], right[...])
        total = part if total is None else total + part
    out[...] = total.astype(out.dtype)


def weight_sums(lefts, rights, dtype, before=None, deps=()):
    length, rows = lefts[0].shape
    columns = rights[0].shape[1]
    wide = columns if columns <= 1408 else 1024
    tall = next(t for t in (1024, 768, 512, 384, 256, 128) if rows % t == 0 and t * wide <= 1024 * 1024)
    block = pl.BlockSpec((tall, wide), lambda i, j: (i, j))
    extra = [] if before is None else [before]
    return pl.pallas_call(
        functools.partial(sums_kernel, len(lefts), len(extra), len(deps)),
        grid=(rows // tall, columns // wide),
        in_specs=[pl.BlockSpec((length, tall), lambda i, j: (0, i)) for left in lefts]
        + [pl.BlockSpec((length, wide), lambda i, j: (0, j)) for right in rights]
        + [block] * len(extra)
        + [pl.BlockSpec(memory_space=pl.ANY)] * len(deps),
        out_specs=block,
        out_shape=jax.ShapeDtypeStruct((rows, columns), dtype),
        compiler_params=pltpu.CompilerParams(
            dimension_semantics=("arbitrary", "arbitrary"), vmem_limit_bytes=VMEM_BYTES
        ),
        cost_estimate=work(sum(2 * length * rows * columns for left in lefts) / 0.66e9),
        name="weight_sums",
    )(*lefts, *rights, *extra, *deps)


def gathered_rows_kernel(places, rows, out):
    moved = to_gathered_tiles(tiles_of(rows[...].astype(jnp.float32)), *places)
    out[...] = jnp.concatenate(moved, axis=1).astype(out.dtype)


def gathered_rows(rows, places):
    tokens, width = rows.shape
    block = pl.BlockSpec((SPAN, width), lambda i: (i, 0))
    return pl.pallas_call(
        functools.partial(gathered_rows_kernel, places),
        grid=(tokens // SPAN,),
        in_specs=[block],
        out_specs=block,
        out_shape=jax.ShapeDtypeStruct((tokens, width), rows.dtype),
        compiler_params=pltpu.CompilerParams(
            dimension_semantics=("arbitrary",), vmem_limit_bytes=VMEM_BYTES
        ),
        cost_estimate=work(1.5),
        name="gathered_rows",
    )(rows)


def matmul_rows(left, right):
    return jnp.einsum("tc,cd->td", left, right, preferred_element_type=jnp.float32)


def matmul_back(left, right):
    return jnp.einsum("td,cd->tc", left, right, preferred_element_type=jnp.float32)


def weight_grad(left, right):
    return jnp.einsum("tc,td->cd", left, right, preferred_element_type=jnp.float32)


def peers(count, flip):
    return [(i, i ^ flip) for i in range(count)]


def swap(value, flip):
    return lax.ppermute(value, "seq", peers(lax.axis_size("seq"), flip))


def block_order(tokens):
    return [(flip, half) for flip in range(lax.axis_size("seq")) for half in range(tokens // SPAN)]


def block_places(tokens):
    halves = tokens // SPAN
    blocks = jnp.arange(lax.axis_size("seq") * halves, dtype=jnp.int32)
    return ((blocks // halves) ^ lax.axis_index("seq")) * halves + blocks % halves


def fetch_tokens(rows):
    return [rows] + [swap(rows, flip) for flip in range(1, lax.axis_size("seq"))]


def scatter_tokens(lefts, rights, back, tokens, hold=(), deps=()):
    f32, bf16 = jnp.float32, jnp.bfloat16
    halves = tokens // SPAN
    count = lax.axis_size("seq")
    sets = tuple(tuple(range(flip * halves, (flip + 1) * halves)) for flip in range(count))
    own, *parts = product_rows(lefts, rights, back, sets, (f32,) + (bf16,) * (count - 1), deps)
    arrived = [swap(after(part, *hold) if hold else part, flip + 1) for flip, part in enumerate(parts)]
    return own, tuple(arrived), tuple(parts)


def add_small(vector):
    for axis in ("fsdp", "seq"):
        count = lax.axis_size(axis)
        flip = 1
        while flip < count:
            vector = vector + lax.ppermute(vector, axis, peers(count, flip))
            flip *= 2
    return vector


def trade(stacked):
    return lax.all_to_all(stacked, "seq", split_axis=0, concat_axis=0, tiled=True)


def gather_weights(rows):
    return lax.all_gather(rows.reshape(-1, rows.shape[-1]), "fsdp", axis=0, tiled=True)


def spread_sums(grad):
    return lax.psum_scatter(grad, "fsdp", scatter_dimension=0, tiled=True)


def to_gathered(rows):
    seq, fsdp = lax.axis_size("seq"), lax.axis_size("fsdp")
    shape = rows.shape
    split = rows.reshape(shape[:-1] + (seq, fsdp, -1))
    return jnp.swapaxes(split, -3, -2).reshape(shape)


def from_gathered(rows):
    seq, fsdp = lax.axis_size("seq"), lax.axis_size("fsdp")
    shape = rows.shape
    split = rows.reshape(shape[:-1] + (fsdp, seq, -1))
    return jnp.swapaxes(split, -3, -2).reshape(shape)


def on_device(
    inputs,
    cotangent,
    segments,
    norm_in,
    ssm_in,
    attn_in,
    conv_w,
    conv_b,
    a_log,
    dt_bias,
    d_skip,
    ssm_out,
    attn_out,
    norm_ffn,
    w_gate,
    w_up,
    w_down,
):
    f32, bf16 = jnp.float32, jnp.bfloat16
    seq = lax.axis_size("seq")
    fsdp = lax.axis_size("fsdp")
    index = lax.axis_index("seq")
    rows = ssm_in.shape[0]
    tokens = inputs.shape[2]
    length = segments.shape[2]
    heads = SSM_HEADS // seq
    inner = heads * SSM_DIM
    query_heads = Q_HEADS // seq
    q_width = query_heads * HEAD_DIM
    qkv_width = q_width + 2 * HEAD_DIM
    groups = Q_HEADS // KV_HEADS
    kv_of = [(s * query_heads) // groups for s in range(seq)]
    head_start = index * heads
    inner_start = index * inner
    z_end, x_end, bc_end = SSM_INNER, 2 * SSM_INNER, 2 * SSM_INNER + 2 * STATE
    q_end = Q_HEADS * HEAD_DIM
    kv_end = q_end + KV_HEADS * HEAD_DIM

    def by_seq(block):
        return jnp.swapaxes(block.reshape(rows, seq, -1), 0, 1)

    def for_all(block):
        return jnp.broadcast_to(block[None], (seq,) + block.shape)

    def by_kv(block):
        return jnp.stack([block[:, h * HEAD_DIM : (h + 1) * HEAD_DIM] for h in kv_of])

    channels = conv_b.shape[0]
    conv_pack = jnp.concatenate([conv_w, conv_b[None]], axis=0).reshape(-1)
    conv_cols = -(-conv_pack.shape[0] // rows)
    conv_pack = jnp.pad(conv_pack, (0, conv_cols * rows - conv_pack.shape[0])).reshape(rows, conv_cols)
    misc = jnp.concatenate([norm_in[:, None], norm_ffn[:, None], conv_pack], axis=1)
    misc = jnp.pad(misc, ((0, 0), (0, 128 - misc.shape[1])))
    early_send = jnp.concatenate(
        [by_seq(attn_in[:, :q_end]), by_kv(attn_in[:, q_end:kv_end]), by_kv(attn_in[:, kv_end:]), for_all(misc)],
        axis=2,
    )
    halves = tokens // SPAN
    places = (rows, seq, fsdp)
    spots = block_order(tokens)
    mine = gathered_rows(inputs[0, 0], places)
    dt_block = jnp.pad(by_seq(ssm_in[:, bc_end:]), ((0, 0), (0, 0), (0, 128 - heads)))
    first_send = jnp.concatenate(
        [by_seq(ssm_in[:, z_end:x_end]), for_all(ssm_in[:, x_end:bc_end]), dt_block], axis=2
    )
    start_mine = trade(jnp.concatenate([early_send, first_send], axis=2))
    early_mine, first_mine = start_mine[:, :, : early_send.shape[2]], start_mine[:, :, early_send.shape[2] :]
    later_send = jnp.concatenate([by_seq(ssm_in[:, :z_end]), by_seq(w_gate), by_seq(w_up)], axis=2)
    pieces = [fetch_tokens(after(mine, start_mine))]
    out_send = jnp.concatenate([ssm_out, attn_out], axis=0)
    early_w = gather_weights(early_mine)
    first_w = gather_weights(first_mine)
    out_rows = ssm_out.shape[0]
    units = w_down.shape[0] * fsdp
    small = early_w[:, qkv_width:]

    def gain_rows(gain):
        return jnp.broadcast_to(gain.astype(f32)[None], (8, gain.shape[0]))

    gain_in_gathered = gain_rows(small[:, 0])
    gain_in = gain_rows(from_gathered(small[:, 0]))
    gain_ffn = gain_rows(from_gathered(small[:, 1]))
    conv_all = small[:, 2 : 2 + conv_cols].reshape(fsdp, seq, -1)[:, :, : (CONV + 1) * channels]
    conv_all = conv_all.reshape(fsdp, seq, CONV + 1, channels).transpose(2, 1, 0, 3)
    conv_all = conv_all.reshape(CONV + 1, CONV_CH).astype(f32)
    conv_local = jnp.concatenate(
        [lax.dynamic_slice_in_dim(conv_all, inner_start, inner, 1), conv_all[:, SSM_INNER:]], axis=1
    )
    conv_table = jnp.pad(conv_local, ((0, 8 - CONV - 1), (0, 0)))
    rate_local = lax.dynamic_slice_in_dim(a_log.astype(f32), head_start, heads)
    bias_local = lax.dynamic_slice_in_dim(dt_bias.astype(f32), head_start, heads)
    skip_local = lax.dynamic_slice_in_dim(d_skip.astype(f32), head_start, heads)
    head_table = jnp.pad(jnp.stack([bias_local, rate_local]), ((0, 6), (0, 128 - heads)))
    skip_table = jnp.broadcast_to(jnp.repeat(skip_local, SSM_DIM)[None], (8, inner))
    tables = rotary_tables(length)
    order = block_places(tokens)

    micro = range(MICRO)
    auxes = [token_aux(segments[m, 0]) for m in micro]
    seg_blocks = [segments[m, 0].astype(f32).reshape(-1, 1, SPAN) for m in micro]
    seg_rows = [segments[m, 0].astype(f32)[None] for m in micro]
    width = inputs.shape[3]
    head_tables = (conv_table, head_table, skip_table)

    hiddens, earlies, attendeds, lses, firsts, ys, all_starts = [], [], [], [], [], [], []
    gate_zs, gateds, mixeds, cot_alls = [], [], [], []
    def mixer_start(m, deps=()):
        if deps:
            pieces[m][0] = after(pieces[m][0], *deps)
        hidden = norm_pieces(pieces[m], spots, gain_in_gathered)
        early = matmul_rows(hidden, early_w).astype(bf16)
        attended, lse = attend_forward(order, early, tables, auxes[m], seg_rows[m], query_heads)
        hiddens.append(hidden)
        earlies.append(early)
        attendeds.append(attended)
        lses.append(lse)

    def mixer_scan(m, deps):
        hiddens[m] = after(hiddens[m], *deps)
        first = matmul_rows(hiddens[m], first_w).astype(bf16)
        y_rows, starts = ssd_forward(order, first, auxes[m], seg_blocks[m], *head_tables, heads)
        firsts.append(first)
        ys.append(y_rows)
        all_starts.append(starts)

    def mixer_gate(m, deps):
        hiddens[m] = after(hiddens[m], *deps)
        gate_z = matmul_rows(hiddens[m], z_w)
        gate_zs.append(gate_z)
        gateds.append((ys[m].astype(f32) * jax.nn.silu(gate_z)).astype(bf16))

    def mixer_out(m, deps, hold=()):
        mixeds.append(
            scatter_tokens([gateds[m], attendeds[m]], [ssm_out_w, attn_out_w], False, tokens, hold, deps)
        )

    def fetch_cotangent(m, deps):
        cot_alls.append(assemble(fetch_tokens(after(cotangent[m, 0], *deps)), spots))

    mixer_start(0)
    later_mine = trade(after(later_send, attendeds[0]))
    pieces.append(fetch_tokens(after(start_rows(inputs[1, 0], cotangent[0, 0], places), later_mine)))
    z_mine, ffn_mine = later_mine[:, :, :inner], later_mine[:, :, inner:]
    z_w = gather_weights(z_mine)
    out_send = after(out_send, z_mine)
    out_w = gather_weights(out_send)
    gate_up_w = gather_weights(after(ffn_mine, out_send))
    mixer_scan(0, [attendeds[0], later_mine])
    down_w = gather_weights(after(w_down, firsts[0]))
    out_w = out_w.reshape(fsdp, -1, out_w.shape[1])
    ssm_out_w, attn_out_w = out_w[:, :out_rows].reshape(inner, -1), out_w[:, out_rows:].reshape(q_width, -1)
    side_w = jnp.concatenate([early_w[:, :qkv_width], z_w], axis=1)
    mixer_gate(0, [ys[0]])
    mixer_out(0, [gateds[0]])
    mixer_start(1, [mixeds[0][0]])
    cot_alls.append(assemble(pieces[1], [(flip, half + halves) for flip, half in spots]))
    mixer_scan(1, [attendeds[1]])

    middles, ffn_hiddens, activateds, grad_gus, grad_hiddens = [], [], [], [], []
    grad_middles, lows, gain_ffn_grads, grads_mixed = [], [], [], []

    def middle_forward(m, deps, hold=()):
        own, arrived, parts = mixeds[m]
        hidden, middle = rows_call(
            functools.partial(middle_kernel, places, len(arrived), len(deps)),
            tokens,
            width,
            [own, inputs[m, 0]],
            gain_ffn,
            arrived,
            [((tokens, width), bf16), ((tokens, width), f32)],
            deps,
            "middle",
        )
        middles.append(middle)
        if hold:
            hidden = after(hidden, *hold)
        ffn_hiddens.append(assemble(fetch_tokens(hidden), spots))

    def feed_forward(m, deps, late=()):
        ffn_hiddens[m] = after(ffn_hiddens[m], *deps)
        activated, grad_gu = feed_products(ffn_hiddens[m], cot_alls[m], gate_up_w, down_w)
        activateds.append(activated)
        grad_gus.append(grad_gu)
        grad_hiddens.append(scatter_tokens([grad_gu], [gate_up_w], True, tokens, (), late))

    def middle_back(m, deps):
        own, arrived, parts = grad_hiddens[m]
        low, wide, gain_grad = rows_call(
            functools.partial(norm_back_kernel, places, len(arrived), len(deps), True),
            tokens,
            width,
            [own, middles[m], cotangent[m, 0]],
            gain_ffn,
            arrived,
            [((tokens, width), bf16), ((tokens, width), f32), ((8, width), f32)],
            deps,
            "middle_back",
        )
        grad_middles.append(wide)
        lows.append(low)
        gain_ffn_grads.append(gain_grad[0])
        grads_mixed.append(assemble(fetch_tokens(low), spots))

    grad_ys, grad_sides, outs, back, in_backs, outputs = [], [], [], [], [], []

    def heads_back(m, deps):
        grad_mixed = after(grads_mixed[m], *deps)
        grads_mixed[m] = grad_mixed
        grad_gated = matmul_back(grad_mixed, ssm_out_w)
        grad_attended = matmul_back(grad_mixed, attn_out_w).astype(bf16)
        gate_z = gate_zs[m]
        sig = jax.nn.sigmoid(gate_z)
        y_wide = ys[m].astype(f32)
        grad_ys.append((grad_gated * gate_z * sig).astype(bf16))
        grad_z = (grad_gated * y_wide * sig * (1.0 + gate_z * (1.0 - sig))).astype(bf16)
        grad_qkv = attend_backward(
            order, earlies[m], tables, auxes[m], seg_rows[m], lses[m], grad_attended, query_heads
        )
        grad_sides.append(jnp.concatenate([grad_qkv, grad_z], axis=1))

    def output_rows(m, deps, hold=()):
        outs.append(scatter_tokens([activateds[m]], [down_w], False, tokens, hold, deps))

    def scan_back(m, deps):
        grad_y = after(grad_ys[m], *deps)
        back.append(
            ssd_backward(order, firsts[m], auxes[m], seg_blocks[m], *head_tables, all_starts[m], grad_y, heads)
        )

    def hidden_back(m, deps, hold=()):
        in_backs.append(
            scatter_tokens([back[m][0], grad_sides[m]], [first_w, side_w], True, tokens, hold, deps)
        )

    def finish_input(m, deps=()):
        own, arrived, parts = in_backs[m]
        low, gain_grad = rows_call(
            functools.partial(norm_back_kernel, places, len(arrived), len(deps), False),
            tokens,
            width,
            [own, inputs[m, 0], grad_middles[m]],
            gain_in,
            arrived,
            [((tokens, width), bf16), ((8, width), f32)],
            deps,
            "input_back",
        )
        return low, gain_grad[0]

    def finish_output(m, deps=()):
        own, arrived, parts = outs[m]
        return rows_call(
            functools.partial(add_rows_kernel, len(arrived)),
            tokens,
            width,
            [own, middles[m]],
            gain_ffn,
            arrived,
            [((tokens, width), bf16)],
            deps,
            "output_rows",
        )[0]

    def both(lefts, rights):
        return (weight_grad(lefts[0], rights[0]) + weight_grad(lefts[1], rights[1])).astype(bf16)

    def back_to_rows(part):
        return trade(part.reshape(seq, rows, -1)).astype(f32)

    middle_forward(0, [ys[1]])
    mixer_gate(1, [middles[0]])
    mixer_out(1, [gateds[1]])
    mixeds[1] = (
        mixeds[1][0],
        tuple(swap(after(part, ffn_hiddens[0]), flip + 1) for flip, part in enumerate(mixeds[1][2])),
        (),
    )
    feed_forward(0, ())
    gate_up_sum = weight_sums(ffn_hiddens[:1], grad_gus[:1], f32, None, [grad_hiddens[0][0], *mixeds[1][1]])
    down_sum = weight_sums(activateds[:1], cot_alls[:1], f32, None, [gate_up_sum])
    middle_back(0, [down_sum])
    middle_forward(1, (), [grads_mixed[0]])
    fetch_cotangent(1, [grads_mixed[0]])
    heads_back(0, ())
    output_rows(0, grad_sides, [ffn_hiddens[1], cot_alls[1]])
    scan_back(0, [outs[0][0]])
    hidden_back(0, ())
    feed_forward(1, [in_backs[0][0]])
    outputs.append(finish_output(0, [grad_hiddens[1][0]]))
    gate_up_sum = weight_sums(ffn_hiddens[1:], grad_gus[1:], bf16, gate_up_sum, [outputs[0]])
    gate_up_part = spread_sums(gate_up_sum)
    middle_back(1, [gate_up_sum])

    def send_late(scattered):
        late = [swap(after(part, grads_mixed[1]), flip + 1) for flip, part in enumerate(scattered[2])]
        return scattered[0], tuple(late), ()

    down_sum = weight_sums(activateds[1:], cot_alls[1:], bf16, down_sum, [lows[1]])
    down_part = spread_sums(down_sum)
    in_backs[0] = send_late(in_backs[0])
    output_rows(1, [down_sum], [grads_mixed[1]])
    ssm_out_sum = weight_sums(gateds, grads_mixed, bf16, None, [outs[1][0]])
    attn_out_sum = weight_sums(attendeds, grads_mixed, bf16, None, [ssm_out_sum])
    out_sum = jnp.concatenate(
        [ssm_out_sum.reshape(fsdp, -1, width), attn_out_sum.reshape(fsdp, -1, width)], axis=1
    ).reshape(inner + q_width, width)
    out_part = spread_sums(out_sum)
    heads_back(1, [out_sum, gate_up_part])
    outputs.append(finish_output(1, [grad_sides[1]]))
    side_sum = weight_sums(hiddens, grad_sides, bf16, None, [outputs[1]])
    side_part = spread_sums(side_sum)
    gate_up_back = back_to_rows(gate_up_part)
    side_back = back_to_rows(side_part)
    scan_back(1, [side_sum, down_part])
    low, gain_grad = finish_input(0, [back[1][0]])
    input_grads, gain_in_grads = [low], [gain_grad]
    first_sum = weight_sums(hiddens, [b[0] for b in back], bf16, None, [low, gate_up_back, out_part])
    first_part = spread_sums(first_sum)
    hidden_back(1, [first_sum])
    first_back = back_to_rows(first_part)
    conv_grad = (back[0][1] + back[1][1])[: CONV + 1]
    head_grad = back[0][2] + back[1][2]
    skip_sum = jnp.sum((back[0][3] + back[1][3])[0].reshape(heads, SSM_DIM), axis=1)
    conv_whole = jnp.zeros((CONV + 1, CONV_CH), f32)
    conv_whole = lax.dynamic_update_slice_in_dim(conv_whole, conv_grad[:, :inner], inner_start, 1)
    conv_whole = lax.dynamic_update_slice_in_dim(conv_whole, conv_grad[:, inner:], SSM_INNER, 1)
    head_sums = lax.dynamic_update_slice_in_dim(
        jnp.zeros((3, SSM_HEADS), f32), jnp.stack([head_grad[0, :heads], head_grad[1, :heads], skip_sum]), head_start, 1
    )
    small_sums = [conv_whole.reshape(-1), head_sums.reshape(-1), gain_ffn_grads[0] + gain_ffn_grads[1]]
    ends = [0]
    for piece in small_sums:
        ends.append(ends[-1] + piece.shape[0])
    total = add_small(after(jnp.concatenate(small_sums), in_backs[1][0]))
    low, gain_grad = finish_input(1, [total])
    input_grads.append(low)
    gain_in_total = add_small(gain_in_grads[0] + gain_grad)

    out_part = after(out_part, first_back).astype(f32)

    def own_columns(block):
        return jnp.swapaxes(block, 0, 1).reshape(rows, -1)

    def kv_columns(block):
        return jnp.concatenate(
            [sum(block[s] for s in range(seq) if kv_of[s] == h) for h in range(KV_HEADS)], axis=1
        )

    gate_grad = own_columns(gate_up_back[:, :, :units])
    up_grad = own_columns(gate_up_back[:, :, units:])
    ssm_in_grad = jnp.concatenate(
        [
            own_columns(side_back[:, :, qkv_width:]),
            own_columns(first_back[:, :, :inner]),
            jnp.sum(first_back[:, :, inner : inner + 2 * STATE], axis=0),
            own_columns(first_back[:, :, inner + 2 * STATE : inner + 2 * STATE + heads]),
        ],
        axis=1,
    )
    attn_in_grad = jnp.concatenate(
        [
            own_columns(side_back[:, :, :q_width]),
            kv_columns(side_back[:, :, q_width : q_width + HEAD_DIM]),
            kv_columns(side_back[:, :, q_width + HEAD_DIM : qkv_width]),
        ],
        axis=1,
    )

    conv_total, head_total, gain_ffn_total = (total[a:b] for a, b in zip(ends[:-1], ends[1:]))
    place = index * fsdp + lax.axis_index("fsdp")
    conv_total = lax.dynamic_slice_in_dim(conv_total.reshape(CONV + 1, CONV_CH), place * channels, channels, 1)
    head_total = head_total.reshape(3, SSM_HEADS)
    return (
        jnp.stack(outputs)[:, None],
        jnp.stack(input_grads)[:, None],
        lax.dynamic_slice_in_dim(gain_in_total, place * rows, rows),
        ssm_in_grad,
        attn_in_grad,
        conv_total[:CONV],
        conv_total[CONV],
        head_total[0],
        head_total[1],
        head_total[2],
        out_part[:out_rows],
        out_part[out_rows:],
        lax.dynamic_slice_in_dim(gain_ffn_total, place * rows, rows),
        gate_grad,
        up_grad,
        after(down_part, first_back).astype(f32),
    )


def solution(mesh):
    return jax.shard_map(
        on_device,
        mesh=mesh,
        in_specs=(
            P(None, "fsdp", "seq", None),
            P(None, "fsdp", "seq", None),
            P(None, "fsdp", None),
            P(("seq", "fsdp")),
            P(("seq", "fsdp"), None),
            P(("seq", "fsdp"), None),
            P(None, ("seq", "fsdp")),
            P(("seq", "fsdp")),
            P(),
            P(),
            P(),
            P(("seq", "fsdp"), None),
            P(("seq", "fsdp"), None),
            P(("seq", "fsdp")),
            P(("seq", "fsdp"), None),
            P(("seq", "fsdp"), None),
            P(("seq", "fsdp"), None),
        ),
        out_specs=(
            P(None, "fsdp", "seq", None),
            P(None, "fsdp", "seq", None),
            P(("seq", "fsdp")),
            P(("seq", "fsdp"), None),
            P(("seq", "fsdp"), None),
            P(None, ("seq", "fsdp")),
            P(("seq", "fsdp")),
            P(),
            P(),
            P(),
            P(("seq", "fsdp"), None),
            P(("seq", "fsdp"), None),
            P(("seq", "fsdp")),
            P(("seq", "fsdp"), None),
            P(("seq", "fsdp"), None),
            P(("seq", "fsdp"), None),
        ),
        check_vma=False,
    )
```

```python
import functools

import jax
import jax.numpy as jnp
from jax import lax
from jax.experimental import pallas as pl
from jax.experimental.pallas import tpu as pltpu
from jax.sharding import PartitionSpec as P

SSM_HEADS = 48
SSM_DIM = 64
STATE = 256
CONV = 4
Q_HEADS = 8
KV_HEADS = 2
HEAD_DIM = 128
MICRO = 2
SPAN = 128
SSM_INNER = 3072
CONV_CH = 3584
ATT_ROWS = 256
VMEM_BYTES = 48 * 1024 * 1024


PRECISE = lax.Precision.HIGHEST
EPSILON = 1e-05
ROPE_BASE = 10000.0


def work(us):
    return pl.CostEstimate(flops=int(us * 1150000000), bytes_accessed=0, transcendentals=0)


def lanes_iota(shape):
    return lax.broadcasted_iota(jnp.int32, shape, 1)


def rows_iota(shape):
    return lax.broadcasted_iota(jnp.int32, shape, 0)


def dot_last(left, right):
    return lax.dot_general(left, right, (((1,), (1,)), ((), ())), preferred_element_type=jnp.float32)


def dot_first(left, right):
    return lax.dot_general(left, right, (((0,), (0,)), ((), ())), preferred_element_type=jnp.float32)


def dot_plain(left, right):
    return jnp.dot(left, right, preferred_element_type=jnp.float32)


def head_steps(block, head_ref, heads):
    pre = block.astype(jnp.float32) + head_ref[0:1, :]
    live = lanes_iota(pre.shape) < heads
    pre = jnp.where(live, pre, 0.0)
    step = jnp.maximum(pre, 0.0) + jnp.log1p(jnp.exp(-jnp.abs(pre)))
    step = jnp.where(live, step, 0.0)
    rate = -jnp.exp(head_ref[1:2, :])
    decay = rate * step
    lower = (rows_iota((SPAN, SPAN)) >= lanes_iota((SPAN, SPAN))).astype(jnp.float32)
    total = jnp.dot(lower, decay, precision=PRECISE, preferred_element_type=jnp.float32)
    return step, rate, decay, total, pre


def over_lanes(column):
    return jnp.broadcast_to(column, (column.shape[0], 128))


def convolve(ubuf, near, conv_ref, lanes):
    acc = conv_ref[CONV : CONV + 1, lanes] + conv_ref[CONV - 1 : CONV, lanes] * ubuf[8 : 8 + SPAN, lanes]
    for offset in range(1, CONV):
        shifted = ubuf[8 - offset : 8 - offset + SPAN, lanes]
        weight = conv_ref[CONV - 1 - offset : CONV - offset, lanes]
        acc = acc + weight * (shifted * near[offset])
    return acc


def pair_of(values, first_head, low_lanes):
    one = jnp.broadcast_to(values[:, first_head : first_head + 1], (SPAN, 128))
    two = jnp.broadcast_to(values[:, first_head + 1 : first_head + 2], (SPAN, 128))
    return one, two, jnp.where(low_lanes, one, two)


def ssd_forward_kernel(
    heads,
    order_ref,
    first_ref,
    aux_ref,
    seg_ref,
    conv_ref,
    head_ref,
    skip_ref,
    y_ref,
    start_ref,
    ubuf,
    taps,
    state,
):
    f32, bf16 = jnp.float32, jnp.bfloat16
    inner = heads * SSM_DIM
    width = inner + 2 * STATE

    @pl.when(pl.program_id(0) == 0)
    def _():
        ubuf[SPAN : SPAN + 8, :] = jnp.zeros((8, width), f32)
        state[...] = jnp.zeros((STATE, inner), f32)

    ubuf[0:8, :] = ubuf[SPAN : SPAN + 8, :]
    ubuf[8 : 8 + SPAN, :] = first_ref[:, :width].astype(f32)
    near = [None] + [over_lanes(aux_ref[:, 2 + offset : 3 + offset]) for offset in range(1, CONV)]
    for lane in range(0, width, 128):
        lanes = slice(lane, lane + 128)
        pre = convolve(ubuf, near, conv_ref, lanes)
        taps[:, lanes] = (pre * jax.nn.sigmoid(pre)).astype(bf16)
    step, rate, decay, total, unused = head_steps(first_ref[:, width:], head_ref, heads)
    total_rows = total.T
    low_lanes = lanes_iota((SPAN, 128)) < SSM_DIM
    same = (aux_ref[:, 0:1] == seg_ref[0]) & (rows_iota((SPAN, SPAN)) >= lanes_iota((SPAN, SPAN)))
    b_rows = taps[:, inner : inner + STATE]
    c_rows = taps[:, inner + STATE :]
    b_cols = b_rows.astype(f32).T.astype(bf16)
    scores = dot_last(c_rows, b_rows)
    carry_keep, end_keep = over_lanes(aux_ref[:, 1:2]), over_lanes(aux_ref[:, 2:3])
    for pair in range(heads // 2):
        lanes = slice(pair * 128, pair * 128 + 128)
        sum_one, sum_two, sums = pair_of(total, 2 * pair, low_lanes)
        steps = pair_of(step, 2 * pair, low_lanes)[2]
        row_one = total_rows[2 * pair : 2 * pair + 1, :]
        row_two = total_rows[2 * pair + 1 : 2 * pair + 2, :]
        mix_one = (jnp.exp(jnp.where(same, sum_one - row_one, -1e30)) * scores).astype(bf16)
        mix_two = (jnp.exp(jnp.where(same, sum_two - row_two, -1e30)) * scores).astype(bf16)
        x = taps[:, lanes].astype(f32)
        stepped = (x * steps).astype(bf16)
        none = jnp.zeros_like(stepped)
        split = jnp.concatenate(
            [jnp.where(low_lanes, stepped, none), jnp.where(low_lanes, none, stepped)], axis=0
        )
        held = state[:, lanes]
        held_low = held.astype(bf16)
        start_ref[0, :, lanes] = held_low
        y = dot_plain(jnp.concatenate([mix_one, mix_two], axis=1), split)
        y = y + jnp.exp(sums) * carry_keep * dot_plain(c_rows, held_low)
        y_ref[:, lanes] = (y + skip_ref[0:1, lanes] * x).astype(bf16)
        last = sums[SPAN - 1 : SPAN, :]
        weighted = (jnp.exp(last - sums) * end_keep * stepped.astype(f32)).astype(bf16)
        kept = jnp.exp(last) * aux_ref[SPAN - 1 : SPAN, 1:2]
        state[:, lanes] = held * kept + dot_plain(b_cols, weighted)


def halves_of(values):
    high = values.astype(jnp.bfloat16)
    return [high, (values - high.astype(jnp.float32)).astype(jnp.bfloat16)]


def ssd_backward_kernel(
    heads,
    order_ref,
    first_ref,
    before_ref,
    aux_ref,
    seg_ref,
    conv_ref,
    head_ref,
    skip_ref,
    start_ref,
    dy_ref,
    grad_ref,
    conv_grad_ref,
    head_grad_ref,
    skip_grad_ref,
    ubuf,
    taps,
    slope,
    gbuf,
    dstate,
):
    f32, bf16 = jnp.float32, jnp.bfloat16
    inner = heads * SSM_DIM
    width = inner + 2 * STATE

    @pl.when(pl.program_id(0) == 0)
    def _():
        gbuf[0:8, :] = jnp.zeros((8, width), f32)
        dstate[...] = jnp.zeros((STATE, inner), f32)
        conv_grad_ref[...] = jnp.zeros(conv_grad_ref.shape, f32)
        head_grad_ref[...] = jnp.zeros(head_grad_ref.shape, f32)
        skip_grad_ref[...] = jnp.zeros(skip_grad_ref.shape, f32)

    ubuf[0:8, :] = before_ref[8:16, :width].astype(f32)
    ubuf[8 : 8 + SPAN, :] = first_ref[:, :width].astype(f32)
    gbuf[SPAN : SPAN + 8, :] = gbuf[0:8, :]
    near = [None] + [over_lanes(aux_ref[:, 2 + offset : 3 + offset]) for offset in range(1, CONV)]
    for lane in range(0, width, 128):
        lanes = slice(lane, lane + 128)
        pre = convolve(ubuf, near, conv_ref, lanes)
        sig = jax.nn.sigmoid(pre)
        taps[:, lanes] = (pre * sig).astype(bf16)
        slope[:, lanes] = sig * (1.0 + pre * (1.0 - sig))
    step, rate, decay, total, pre_step = head_steps(first_ref[:, width:], head_ref, heads)
    total_rows = total.T
    square = (SPAN, SPAN)
    low_lanes = lanes_iota((SPAN, 128)) < SSM_DIM
    low_row = lanes_iota((1, 128)) < SSM_DIM
    head_row = lanes_iota((1, 128))
    same = (aux_ref[:, 0:1] == seg_ref[0]) & (rows_iota(square) >= lanes_iota(square))
    b_rows = taps[:, inner : inner + STATE]
    c_rows = taps[:, inner + STATE :]
    c_cols = c_rows.astype(f32).T.astype(bf16)
    scores = dot_last(c_rows, b_rows)
    carry_keep, end_keep = over_lanes(aux_ref[:, 1:2]), over_lanes(aux_ref[:, 2:3])
    head_lane = lanes_iota((SPAN, 128))
    is_last = rows_iota((SPAN, 1)) == SPAN - 1
    grad_scores = jnp.zeros(square, f32)
    grad_b = jnp.zeros((SPAN, STATE), f32)
    grad_c = jnp.zeros((SPAN, STATE), f32)
    grad_total = jnp.zeros((SPAN, 128), f32)
    grad_step = jnp.zeros((SPAN, 128), f32)
    for pair in range(heads // 2):
        lanes = slice(pair * 128, pair * 128 + 128)
        sum_one, sum_two, sums = pair_of(total, 2 * pair, low_lanes)
        steps = pair_of(step, 2 * pair, low_lanes)[2]
        row_one = total_rows[2 * pair : 2 * pair + 1, :]
        row_two = total_rows[2 * pair + 1 : 2 * pair + 2, :]
        decay_one = jnp.exp(jnp.where(same, sum_one - row_one, -1e30))
        decay_two = jnp.exp(jnp.where(same, sum_two - row_two, -1e30))
        mix_one = (decay_one * scores).astype(bf16)
        mix_two = (decay_two * scores).astype(bf16)
        x = taps[:, lanes].astype(f32)
        stepped = (x * steps).astype(bf16)
        none = jnp.zeros_like(stepped)
        x_one = jnp.where(low_lanes, stepped, none)
        x_two = jnp.where(low_lanes, none, stepped)
        dy_low = dy_ref[:, lanes]
        dy = dy_low.astype(f32)
        dy_one = jnp.where(low_lanes, dy_low, none)
        dy_two = jnp.where(low_lanes, none, dy_low)
        grad_scores = grad_scores + dot_last(dy_one, stepped) * decay_one + dot_last(dy_two, stepped) * decay_two
        y = dot_plain(
            jnp.concatenate([mix_one, mix_two], axis=1), jnp.concatenate([x_one, x_two], axis=0)
        )
        grad_in = dot_first(
            jnp.concatenate([mix_one, mix_two], axis=0), jnp.concatenate([dy_one, dy_two], axis=0)
        )
        held = start_ref[0, :, lanes]
        dheld = dstate[:, lanes]
        dheld_low = dheld.astype(bf16)
        grown = jnp.exp(sums) * carry_keep
        y = y + grown * dot_plain(c_rows, held)
        grown_dy = (grown * dy).astype(bf16)
        last = sums[SPAN - 1 : SPAN, :]
        fade = jnp.exp(last - sums) * end_keep
        stepped_wide = stepped.astype(f32)
        weighted = (fade * stepped_wide).astype(bf16)
        from_end = dot_plain(b_rows, dheld_low)
        grad_in = grad_in + fade * from_end
        grad_c = grad_c + dot_last(grown_dy, held)
        grad_b = grad_b + dot_last(weighted, dheld_low)
        kept = jnp.exp(last) * aux_ref[SPAN - 1 : SPAN, 1:2]
        ends = jnp.sum(fade * stepped_wide * from_end, axis=0, keepdims=True) + kept * jnp.sum(
            dheld * held.astype(f32), axis=0, keepdims=True
        )
        dstate[:, lanes] = dheld * kept + dot_plain(c_cols, grown_dy)
        gaps = dy * y - stepped_wide * grad_in
        by_step = x * grad_in
        ends_one = jnp.sum(jnp.where(low_row, ends, 0.0), axis=1, keepdims=True)
        ends_two = jnp.sum(jnp.where(low_row, 0.0, ends), axis=1, keepdims=True)
        ends_here = jnp.where(head_row == 2 * pair, ends_one, jnp.where(head_row == 2 * pair + 1, ends_two, 0.0))
        of_head = (lanes_iota(square) == 2 * pair + rows_iota(square) // SSM_DIM).astype(bf16)
        by_head = dot_plain(jnp.concatenate(halves_of(gaps) + halves_of(by_step), axis=0), of_head)
        grad_total = grad_total + by_head[:SPAN] + by_head[SPAN : 2 * SPAN] + jnp.where(is_last, ends_here, 0.0)
        grad_step = grad_step + by_head[2 * SPAN : 3 * SPAN] + by_head[3 * SPAN :]
        skip = skip_ref[0:1, lanes]
        skip_grad_ref[0:1, lanes] += jnp.sum(dy * x, axis=0, keepdims=True)
        gbuf[0:SPAN, lanes] = (steps * grad_in + skip * dy) * slope[:, lanes]
    low_scores = grad_scores.astype(bf16)
    grad_c = grad_c + dot_plain(low_scores, b_rows)
    grad_b = grad_b + dot_first(low_scores, c_rows)
    gbuf[0:SPAN, inner : inner + STATE] = grad_b * slope[:, inner : inner + STATE]
    gbuf[0:SPAN, inner + STATE : width] = grad_c * slope[:, inner + STATE : width]

    upper = (rows_iota(square) <= lanes_iota(square)).astype(f32)
    grad_decay = jnp.dot(upper, grad_total, precision=PRECISE, preferred_element_type=f32)
    grad_pre = (grad_step + rate * grad_decay) * jax.nn.sigmoid(pre_step)
    grad_pre = jnp.where(head_lane < heads, grad_pre, 0.0)
    grad_ref[:, width:] = grad_pre.astype(bf16)
    head_grad_ref[0:1, :] += jnp.sum(grad_decay * decay, axis=0, keepdims=True)
    head_grad_ref[1:2, :] += jnp.sum(grad_pre, axis=0, keepdims=True)

    ahead = [None] + [over_lanes(aux_ref[:, 5 + offset : 6 + offset]) for offset in range(1, CONV)]
    for lane in range(0, width, 128):
        lanes = slice(lane, lane + 128)
        grad = gbuf[0:SPAN, lanes]
        conv_grad_ref[CONV : CONV + 1, lanes] += jnp.sum(grad, axis=0, keepdims=True)
        conv_grad_ref[CONV - 1 : CONV, lanes] += jnp.sum(grad * ubuf[8 : 8 + SPAN, lanes], axis=0, keepdims=True)
        acc = conv_ref[CONV - 1 : CONV, lanes] * grad
        for offset in range(1, CONV):
            at = CONV - 1 - offset
            shifted = ubuf[8 - offset : 8 - offset + SPAN, lanes] * near[offset]
            conv_grad_ref[at : at + 1, lanes] += jnp.sum(grad * shifted, axis=0, keepdims=True)
            later = gbuf[offset : offset + SPAN, lanes] * ahead[offset]
            acc = acc + conv_ref[at : at + 1, lanes] * later
        grad_ref[:, lanes] = acc.astype(bf16)


def token_aux(segment):
    length = segment.shape[0]
    ends = segment.reshape(-1, SPAN)[:, -1]
    end_of = jnp.repeat(ends, SPAN)
    before = jnp.repeat(jnp.concatenate([jnp.full((1,), -1, segment.dtype), ends[:-1]]), SPAN)
    columns = [segment, segment == before, segment == end_of]
    for offset in range(1, CONV):
        columns.append(jnp.pad(segment, (offset, 0), constant_values=-1)[:length] == segment)
    for offset in range(1, CONV):
        columns.append(jnp.pad(segment, (0, offset), constant_values=-1)[offset:] == segment)
    columns = [column.astype(jnp.float32) for column in columns]
    return jnp.stack(columns + [jnp.zeros((length,), jnp.float32)] * (16 - len(columns)), axis=1)


def ssd_specs(heads, at):
    inner = heads * SSM_DIM
    width = inner + 2 * STATE
    return [
        pl.BlockSpec((SPAN, width + 128), lambda i, order: (order[at(i)], 0)),
        pl.BlockSpec((SPAN, 16), lambda i, order: (at(i), 0)),
        pl.BlockSpec((1, 1, SPAN), lambda i, order: (at(i), 0, 0)),
        pl.BlockSpec((8, width), lambda i, order: (0, 0)),
        pl.BlockSpec((8, 128), lambda i, order: (0, 0)),
        pl.BlockSpec((8, inner), lambda i, order: (0, 0)),
    ]


def ssd_forward(order, first, aux, seg_rows, conv, head, skip, heads):
    length = first.shape[0]
    inner = heads * SSM_DIM
    width = inner + 2 * STATE
    blocks = length // SPAN
    return pl.pallas_call(
        functools.partial(ssd_forward_kernel, heads),
        grid_spec=pltpu.PrefetchScalarGridSpec(
            num_scalar_prefetch=1,
            grid=(blocks,),
            in_specs=ssd_specs(heads, lambda i: i),
            out_specs=[
                pl.BlockSpec((SPAN, inner), lambda i, order: (order[i], 0)),
                pl.BlockSpec((1, STATE, inner), lambda i, order: (i, 0, 0)),
            ],
            scratch_shapes=[
                pltpu.VMEM((SPAN + 8, width), jnp.float32),
                pltpu.VMEM((SPAN, width), jnp.bfloat16),
                pltpu.VMEM((STATE, inner), jnp.float32),
            ],
        ),
        out_shape=[
            jax.ShapeDtypeStruct((length, inner), jnp.bfloat16),
            jax.ShapeDtypeStruct((blocks, STATE, inner), jnp.bfloat16),
        ],
        compiler_params=pltpu.CompilerParams(
            dimension_semantics=("arbitrary",), vmem_limit_bytes=VMEM_BYTES
        ),
        cost_estimate=work(0),
        name="ssd_forward",
    )(order, first, aux, seg_rows, conv, head, skip)


def ssd_backward(order, first, aux, seg_rows, conv, head, skip, starts, dy, heads):
    length = first.shape[0]
    inner = heads * SSM_DIM
    width = inner + 2 * STATE
    blocks = length // SPAN
    per_block = SPAN // 16

    def at(i):
        return blocks - 1 - i

    specs = ssd_specs(heads, at)
    specs.insert(
        1,
        pl.BlockSpec(
            (16, width + 128), lambda i, order: (order[jnp.maximum(at(i) - 1, 0)] * per_block + per_block - 1, 0)
        ),
    )
    specs += [
        pl.BlockSpec((1, STATE, inner), lambda i, order: (at(i), 0, 0)),
        pl.BlockSpec((SPAN, inner), lambda i, order: (order[at(i)], 0)),
    ]
    return pl.pallas_call(
        functools.partial(ssd_backward_kernel, heads),
        grid_spec=pltpu.PrefetchScalarGridSpec(
            num_scalar_prefetch=1,
            grid=(blocks,),
            in_specs=specs,
            out_specs=[
                pl.BlockSpec((SPAN, width + 128), lambda i, order: (order[at(i)], 0)),
                pl.BlockSpec((8, width), lambda i, order: (0, 0)),
                pl.BlockSpec((8, 128), lambda i, order: (0, 0)),
                pl.BlockSpec((8, inner), lambda i, order: (0, 0)),
            ],
            scratch_shapes=[
                pltpu.VMEM((SPAN + 8, width), jnp.float32),
                pltpu.VMEM((SPAN, width), jnp.bfloat16),
                pltpu.VMEM((SPAN, width), jnp.float32),
                pltpu.VMEM((SPAN + 8, width), jnp.float32),
                pltpu.VMEM((STATE, inner), jnp.float32),
            ],
        ),
        out_shape=[
            jax.ShapeDtypeStruct((length, width + 128), jnp.bfloat16),
            jax.ShapeDtypeStruct((8, width), jnp.float32),
            jax.ShapeDtypeStruct((8, 128), jnp.float32),
            jax.ShapeDtypeStruct((8, inner), jnp.float32),
        ],
        compiler_params=pltpu.CompilerParams(
            dimension_semantics=("arbitrary",), vmem_limit_bytes=VMEM_BYTES
        ),
        cost_estimate=work(53),
        name="ssd_backward",
    )(order, first, first, aux, seg_rows, conv, head, skip, starts, dy)


def rotary_tables(length):
    half = HEAD_DIM // 2
    frequency = ROPE_BASE ** (-jnp.arange(half).astype(jnp.float32) / half)
    angles = jnp.arange(length, dtype=jnp.int32).astype(jnp.float32)[:, None] * frequency[None, :]
    cosine, sine = jnp.cos(angles), jnp.sin(angles)
    return jnp.concatenate([cosine, cosine], axis=1), jnp.concatenate([-sine, sine], axis=1)


def turn(rows, cosine, sine):
    wide = rows.astype(jnp.float32)
    return (wide * cosine + pltpu.roll(wide, HEAD_DIM // 2, 1) * sine).astype(jnp.bfloat16)


def turn_back(grads, cosine, sine):
    return (grads * cosine + pltpu.roll(grads * sine, HEAD_DIM // 2, 1)).astype(jnp.bfloat16)


def block_scores(q_block, k_part, first_row, seg_col, seg_row):
    scores = dot_last(q_block, k_part) * HEAD_DIM ** (-0.5)
    shape = scores.shape
    allowed = (rows_iota(shape) + first_row >= lanes_iota(shape)) & (seg_col == seg_row)
    return jnp.where(allowed, scores, -1e30)


def place_of(order_ref, block):
    return pl.ds(pl.multiple_of(order_ref[block] * SPAN, SPAN), SPAN)


def load_keys(order_ref, qkv_ref, q_width, cos_ref, sin_ref, k_rot, value):
    for block in range(qkv_ref.shape[0] // SPAN):
        there, here = place_of(order_ref, block), slice(block * SPAN, (block + 1) * SPAN)
        k_rot[here, :] = turn(qkv_ref[there, q_width : q_width + HEAD_DIM], cos_ref[here, :], sin_ref[here, :])
        value[here, :] = qkv_ref[there, q_width + HEAD_DIM : q_width + 2 * HEAD_DIM]


def load_rows(order_ref, ref, start, count, lanes):
    blocks = range(start // SPAN, (start + count) // SPAN)
    return jnp.concatenate([ref[place_of(order_ref, block), lanes] for block in blocks], axis=0)


def store_rows(order_ref, ref, start, lanes, values):
    for part in range(values.shape[0] // SPAN):
        ref[place_of(order_ref, start // SPAN + part), lanes] = values[part * SPAN : (part + 1) * SPAN, :]


def attend_forward_kernel(
    query_heads, block, order_ref, qkv_ref, cos_ref, sin_ref, aux_ref, seg_ref, out_ref, lse_ref, k_rot, value
):
    length = qkv_ref.shape[0]
    load_keys(order_ref, qkv_ref, query_heads * HEAD_DIM, cos_ref, sin_ref, k_rot, value)
    for start in range(0, length, block):
        rows = slice(start, start + block)
        end = start + block
        for head in range(query_heads):
            lanes = slice(head * HEAD_DIM, (head + 1) * HEAD_DIM)
            q_rows = load_rows(order_ref, qkv_ref, start, block, lanes)
            q_block = turn(q_rows, cos_ref[rows, :], sin_ref[rows, :])
            scores = block_scores(q_block, k_rot[:end, :], start, aux_ref[rows, 0:1], seg_ref[:, :end])
            top = jnp.max(scores, axis=1, keepdims=True)
            raised = jnp.exp(scores - top)
            total = jnp.sum(raised, axis=1, keepdims=True)
            probs = (raised * (1.0 / total)).astype(jnp.bfloat16)
            store_rows(order_ref, out_ref, start, lanes, dot_plain(probs, value[:end, :]).astype(jnp.bfloat16))
            lse_ref[rows, head : head + 1] = top + jnp.log(total)


def attend_backward_kernel(
    query_heads,
    block,
    order_ref,
    qkv_ref,
    cos_ref,
    sin_ref,
    aux_ref,
    seg_ref,
    lse_ref,
    grad_ref,
    out_ref,
    k_rot,
    value,
    dk,
    dv,
):
    f32, bf16 = jnp.float32, jnp.bfloat16
    length = qkv_ref.shape[0]
    q_width = query_heads * HEAD_DIM
    load_keys(order_ref, qkv_ref, q_width, cos_ref, sin_ref, k_rot, value)
    dk[...] = jnp.zeros(dk.shape, f32)
    dv[...] = jnp.zeros(dv.shape, f32)
    for start in range(0, length, block):
        rows = slice(start, start + block)
        end = start + block
        for head in range(query_heads):
            lanes = slice(head * HEAD_DIM, (head + 1) * HEAD_DIM)
            cosine, sine = cos_ref[rows, :], sin_ref[rows, :]
            q_block = turn(load_rows(order_ref, qkv_ref, start, block, lanes), cosine, sine)
            scores = block_scores(q_block, k_rot[:end, :], start, aux_ref[rows, 0:1], seg_ref[:, :end])
            probs = jnp.exp(scores - lse_ref[rows, head : head + 1])
            grad = load_rows(order_ref, grad_ref, start, block, lanes)
            grad_probs = dot_last(grad, value[:end, :])
            mean = jnp.sum(grad_probs * probs, axis=1, keepdims=True)
            grad_scores = (probs * (grad_probs - mean) * HEAD_DIM ** (-0.5)).astype(bf16)
            grad_query = turn_back(dot_plain(grad_scores, k_rot[:end, :]), cosine, sine)
            store_rows(order_ref, out_ref, start, lanes, grad_query)
            dk[:end, :] += dot_first(grad_scores, q_block)
            dv[:end, :] += dot_first(probs.astype(bf16), grad)
    k_lanes = slice(q_width, q_width + HEAD_DIM)
    v_lanes = slice(q_width + HEAD_DIM, q_width + 2 * HEAD_DIM)
    store_rows(order_ref, out_ref, 0, k_lanes, turn_back(dk[...], cos_ref[...], sin_ref[...]))
    store_rows(order_ref, out_ref, 0, v_lanes, dv[...].astype(bf16))


def attend_specs(arrays):
    return [pl.BlockSpec(memory_space=pltpu.SMEM)] + [pl.BlockSpec(memory_space=pltpu.VMEM)] * arrays


def attend_forward(order, early, tables, aux, seg_row, query_heads):
    length = early.shape[0]
    return pl.pallas_call(
        functools.partial(attend_forward_kernel, query_heads, min(ATT_ROWS, length)),
        in_specs=attend_specs(5),
        out_shape=[
            jax.ShapeDtypeStruct((length, query_heads * HEAD_DIM), jnp.bfloat16),
            jax.ShapeDtypeStruct((length, 8), jnp.float32),
        ],
        scratch_shapes=[pltpu.VMEM((length, HEAD_DIM), jnp.bfloat16), pltpu.VMEM((length, HEAD_DIM), jnp.bfloat16)],
        compiler_params=pltpu.CompilerParams(vmem_limit_bytes=VMEM_BYTES),
        cost_estimate=work(5),
        name="attend_forward",
    )(order, early, tables[0], tables[1], aux, seg_row)


def attend_backward(order, early, tables, aux, seg_row, lse, grad, query_heads):
    length = early.shape[0]
    return pl.pallas_call(
        functools.partial(attend_backward_kernel, query_heads, min(ATT_ROWS, length)),
        in_specs=attend_specs(7),
        out_shape=jax.ShapeDtypeStruct((length, (query_heads + 2) * HEAD_DIM), jnp.bfloat16),
        scratch_shapes=[
            pltpu.VMEM((length, HEAD_DIM), jnp.bfloat16),
            pltpu.VMEM((length, HEAD_DIM), jnp.bfloat16),
            pltpu.VMEM((length, HEAD_DIM), jnp.float32),
            pltpu.VMEM((length, HEAD_DIM), jnp.float32),
        ],
        compiler_params=pltpu.CompilerParams(vmem_limit_bytes=VMEM_BYTES),
        cost_estimate=work(7),
        name="attend_backward",
    )(order, early, tables[0], tables[1], aux, seg_row, lse, grad)


def after_kernel(*refs):
    pass


def after(value, *others):
    return pl.pallas_call(
        after_kernel,
        in_specs=[pl.BlockSpec(memory_space=pl.ANY)] * (1 + len(others)),
        out_specs=pl.BlockSpec(memory_space=pl.ANY),
        out_shape=jax.ShapeDtypeStruct(value.shape, value.dtype),
        input_output_aliases={0: 0},
        name="after",
    )(value, *others)


def move_blocks(tiles, width, here, there):
    per = 128 // width
    lane = lanes_iota(tiles[0].shape)
    moved = []
    for tile in range(len(tiles)):
        out = None
        for part in range(per):
            source = there(tile * per + part)
            piece = tiles[source // per]
            shift = ((part - source % per) * width) % 128
            if shift:
                piece = pltpu.roll(piece, shift, 1)
            out = piece if out is None else jnp.where(lane >= part * width, piece, out)
        moved.append(out)
    return moved


def to_gathered_tiles(tiles, width, seq, fsdp):
    return move_blocks(tiles, width, None, lambda b: (b % seq) * fsdp + b // seq)


def from_gathered_tiles(tiles, width, seq, fsdp):
    return move_blocks(tiles, width, None, lambda b: (b % fsdp) * seq + b // fsdp)


def tiles_of(array):
    return [array[:, lane : lane + 128] for lane in range(0, array.shape[1], 128)]


def add_arrived(own, arrived):
    total = own[...]
    for ref in arrived:
        total = total + ref[...].astype(jnp.float32)
    return total


def row_sum(tiles):
    total = tiles[0]
    for tile in tiles[1:]:
        total = total + tile
    return jnp.sum(total, axis=1, keepdims=True)


def middle_kernel(places, count, skip, own, rows, gain, *refs):
    arrived, (hidden_ref, middle_ref) = refs[:count], refs[count + skip :]
    middle = rows[...].astype(jnp.float32) + add_arrived(own, arrived)
    middle_ref[...] = middle
    mean = jnp.sum(middle * middle, axis=1, keepdims=True) / middle.shape[1]
    hidden = middle * lax.rsqrt(mean + EPSILON) * gain[0:1, :]
    moved = to_gathered_tiles(tiles_of(hidden), *places)
    hidden_ref[...] = jnp.concatenate(moved, axis=1).astype(jnp.bfloat16)


def norm_back_kernel(places, count, skip, keep_wide, own, rows, passed, gain, *refs):
    arrived, outs = refs[:count], refs[count + skip :]
    grads = add_arrived(own, arrived)
    grads = jnp.concatenate(from_gathered_tiles(tiles_of(grads), *places), axis=1)
    wide = rows[...].astype(jnp.float32)
    width = wide.shape[1]
    scale = lax.rsqrt(jnp.sum(wide * wide, axis=1, keepdims=True) / width + EPSILON)
    normed = wide * scale
    weighted = grads * gain[0:1, :]
    mean = jnp.sum(weighted * normed, axis=1, keepdims=True) / width
    total = passed[...].astype(jnp.float32) + scale * (weighted - normed * mean)
    outs[0][...] = total.astype(jnp.bfloat16)
    if keep_wide:
        outs[1][...] = total


def add_rows_kernel(count, own, rows, gain, *refs):
    refs[-1][...] = (rows[...] + add_arrived(own, refs[:count])).astype(refs[-1].dtype)


def rows_call(kernel, tokens, width, inputs, gain, arrived, outs, deps, name):
    block = pl.BlockSpec((SPAN, width), lambda i: (i, 0))
    whole = pl.BlockSpec((8, width), lambda i: (0, 0))
    out_specs = [whole if shape[0] == 8 else block for shape, dtype in outs]
    return pl.pallas_call(
        kernel,
        grid=(tokens // SPAN,),
        in_specs=[block] * len(inputs)
        + [whole]
        + [block] * len(arrived)
        + [pl.BlockSpec(memory_space=pl.ANY)] * len(deps),
        out_specs=out_specs,
        out_shape=[jax.ShapeDtypeStruct(shape, dtype) for shape, dtype in outs],
        compiler_params=pltpu.CompilerParams(
            dimension_semantics=("arbitrary",), vmem_limit_bytes=VMEM_BYTES
        ),
        cost_estimate=work(5),
        name=name,
    )(*inputs, gain, *arrived, *deps)


def norm_pieces_kernel(gain, *refs):
    pieces, out = refs[:-1], refs[-1]
    for block, piece in enumerate(pieces):

        @pl.when(pl.program_id(0) == block)
        def _(piece=piece):
            wide = piece[...].astype(jnp.float32)
            mean = jnp.sum(wide * wide, axis=1, keepdims=True) / wide.shape[1]
            out[...] = (wide * lax.rsqrt(mean + EPSILON) * gain[0:1, :]).astype(jnp.bfloat16)


def norm_pieces(pieces, spots, gain):
    width = pieces[0].shape[1]
    length = len(spots) * SPAN
    return pl.pallas_call(
        norm_pieces_kernel,
        grid=(len(spots),),
        in_specs=[pl.BlockSpec((8, width), lambda i: (0, 0))]
        + [pl.BlockSpec((SPAN, width), functools.partial(lambda half, i: (half, 0), half)) for piece, half in spots],
        out_specs=pl.BlockSpec((SPAN, width), lambda i: (i, 0)),
        out_shape=jax.ShapeDtypeStruct((length, width), jnp.bfloat16),
        compiler_params=pltpu.CompilerParams(
            dimension_semantics=("arbitrary",), vmem_limit_bytes=VMEM_BYTES
        ),
        cost_estimate=work(5),
        name="norm_pieces",
    )(gain, *[pieces[piece] for piece, half in spots])


def assemble_kernel(count, spots, *refs):
    pieces, out, held, sems = refs[:count], refs[-3], refs[-2], refs[-1]
    places = [pl.ds(block * SPAN, SPAN) for block in range(len(spots))]
    loads = [
        pltpu.make_async_copy(pieces[piece].at[places[half]], held.at[places[b]], sems.at[0, b])
        for b, (piece, half) in enumerate(spots)
    ]
    stores = [
        pltpu.make_async_copy(held.at[places[b]], out.at[places[b]], sems.at[1, b]) for b in range(len(spots))
    ]
    for load in loads:
        load.start()
    for load, store in zip(loads, stores):
        load.wait()
        store.start()
    for store in stores:
        store.wait()


def assemble(pieces, spots):
    width = pieces[0].shape[1]
    length = len(spots) * SPAN
    return pl.pallas_call(
        functools.partial(assemble_kernel, len(pieces), spots),
        in_specs=[pl.BlockSpec(memory_space=pl.ANY)] * len(pieces),
        out_specs=pl.BlockSpec(memory_space=pl.ANY),
        out_shape=jax.ShapeDtypeStruct((length, width), pieces[0].dtype),
        scratch_shapes=[
            pltpu.VMEM((length, width), pieces[0].dtype),
            pltpu.SemaphoreType.DMA((2, len(spots))),
        ],
        compiler_params=pltpu.CompilerParams(vmem_limit_bytes=VMEM_BYTES),
        cost_estimate=work(3),
        name="assemble",
    )(*pieces)


def start_rows_kernel(places, halves, rows, *refs):
    cots, out = refs[:-1], refs[-1]
    part = pl.program_id(0) // halves

    @pl.when(part == 0)
    def _():
        moved = to_gathered_tiles(tiles_of(rows[...].astype(jnp.float32)), *places)
        out[...] = jnp.concatenate(moved, axis=1).astype(out.dtype)

    for place, cot in enumerate(cots):

        @pl.when(part == place + 1)
        def _(cot=cot):
            out[...] = cot[...]


def start_rows(rows, cots, places):
    tokens, width = rows.shape
    halves = tokens // SPAN
    parts = 1 + len(cots)

    def block(part):
        return pl.BlockSpec((SPAN, width), lambda i: (jnp.clip(i - part * halves, 0, halves - 1), 0))

    return pl.pallas_call(
        functools.partial(start_rows_kernel, places, halves),
        grid=(parts * halves,),
        in_specs=[block(part) for part in range(parts)],
        out_specs=pl.BlockSpec((SPAN, width), lambda i: (i, 0)),
        out_shape=jax.ShapeDtypeStruct((parts * tokens, width), rows.dtype),
        compiler_params=pltpu.CompilerParams(
            dimension_semantics=("arbitrary",), vmem_limit_bytes=VMEM_BYTES
        ),
        cost_estimate=work(2),
        name="start_rows",
    )(rows, *cots)


def product_kernel(back, pairs, skip, sets, *refs):
    lefts, rights, outs = refs[:pairs], refs[pairs : 2 * pairs], refs[2 * pairs + skip :]
    blocks = lefts[0].shape[0] // SPAN
    where = {block: (out, place) for out, held in enumerate(sets) for place, block in enumerate(held)}
    for block in range(0, blocks, 2):
        total = None
        for left, right in zip(lefts, rights):
            rows = left[block * SPAN : (block + 2) * SPAN, :]
            part = dot_last(rows, right[...]) if back else dot_plain(rows, right[...])
            total = part if total is None else total + part
        for half in range(2):
            out, place = where[block + half]
            part = total[half * SPAN : (half + 1) * SPAN, :]
            outs[out][place * SPAN : (place + 1) * SPAN, :] = part.astype(outs[out].dtype)


def product_rows(lefts, rights, back, sets, dtypes, deps=(), weight=1):
    length = lefts[0].shape[0]
    width = rights[0].shape[0 if back else 1]
    slab = 512
    specs = [pl.BlockSpec(left.shape, lambda n: (0, 0)) for left in lefts]
    for right in rights:
        if back:
            specs.append(pl.BlockSpec((slab, right.shape[1]), lambda n: (n, 0)))
        else:
            specs.append(pl.BlockSpec((right.shape[0], slab), lambda n: (0, n)))
    return pl.pallas_call(
        functools.partial(product_kernel, back, len(lefts), len(deps), sets),
        grid=(width // slab,),
        in_specs=specs + [pl.BlockSpec(memory_space=pl.ANY)] * len(deps),
        out_specs=[pl.BlockSpec((len(held) * SPAN, slab), lambda n: (0, n)) for held in sets],
        out_shape=[
            jax.ShapeDtypeStruct((len(held) * SPAN, width), dtype) for held, dtype in zip(sets, dtypes)
        ],
        compiler_params=pltpu.CompilerParams(
            dimension_semantics=("arbitrary",), vmem_limit_bytes=VMEM_BYTES
        ),
        cost_estimate=work(weight * sum(2 * length * left.shape[1] * width for left in lefts) / 0.66e9),
        name="product_rows",
    )(*lefts, *rights, *deps)


def feed_kernel(units, slab, hidden, cot, gate_w, up_w, down_w, act_ref, grad_ref):
    here = pl.multiple_of(pl.program_id(0) * slab, slab)
    for row in range(0, hidden.shape[0], 256):
        rows = slice(row, row + 256)
        gate_pre = dot_plain(hidden[rows, :], gate_w[...])
        up_pre = dot_plain(hidden[rows, :], up_w[...])
        grad_act = dot_last(cot[rows, :], down_w[...])
        sig = jax.nn.sigmoid(gate_pre)
        silu = gate_pre * sig
        act_ref[rows, :] = (silu * up_pre).astype(jnp.bfloat16)
        grad_gate = grad_act * up_pre * sig * (1.0 + gate_pre * (1.0 - sig))
        grad_ref[rows, pl.ds(here, slab)] = grad_gate.astype(jnp.bfloat16)
        grad_ref[rows, pl.ds(units + here, slab)] = (grad_act * silu).astype(jnp.bfloat16)


def feed_products(hidden, cot, gate_up_w, down_w):
    length, width = hidden.shape
    units = down_w.shape[0]
    slab = min(256, units)
    steps = units // slab
    whole = pl.BlockSpec((length, width), lambda n: (0, 0))
    return pl.pallas_call(
        functools.partial(feed_kernel, units, slab),
        grid=(steps,),
        in_specs=[
            whole,
            whole,
            pl.BlockSpec((width, slab), lambda n: (0, n)),
            pl.BlockSpec((width, slab), lambda n: (0, steps + n)),
            pl.BlockSpec((slab, width), lambda n: (n, 0)),
        ],
        out_specs=[
            pl.BlockSpec((length, slab), lambda n: (0, n)),
            pl.BlockSpec((length, 2 * units), lambda n: (0, 0)),
        ],
        out_shape=[
            jax.ShapeDtypeStruct((length, units), jnp.bfloat16),
            jax.ShapeDtypeStruct((length, 2 * units), jnp.bfloat16),
        ],
        compiler_params=pltpu.CompilerParams(
            dimension_semantics=("arbitrary",), vmem_limit_bytes=VMEM_BYTES
        ),
        cost_estimate=work(6 * length * width * units / 0.6e9),
        name="feed_products",
    )(hidden, cot, gate_up_w, gate_up_w, down_w)


def sums_kernel(pairs, before, skip, *refs):
    out = refs[-1]
    total = refs[2 * pairs][...] if before else None
    for left, right in zip(refs[:pairs], refs[pairs : 2 * pairs]):
        part = dot_first(left[...], right[...])
        total = part if total is None else total + part
    out[...] = total.astype(out.dtype)


def weight_sums(lefts, rights, dtype, before=None, deps=()):
    length, rows = lefts[0].shape
    columns = rights[0].shape[1]
    wide = columns if columns <= 1408 else 1024
    tall = next(t for t in (1024, 768, 512, 384, 256, 128) if rows % t == 0 and t * wide <= 1024 * 1024)
    block = pl.BlockSpec((tall, wide), lambda i, j: (i, j))
    extra = [] if before is None else [before]
    return pl.pallas_call(
        functools.partial(sums_kernel, len(lefts), len(extra), len(deps)),
        grid=(rows // tall, columns // wide),
        in_specs=[pl.BlockSpec((length, tall), lambda i, j: (0, i)) for left in lefts]
        + [pl.BlockSpec((length, wide), lambda i, j: (0, j)) for right in rights]
        + [block] * len(extra)
        + [pl.BlockSpec(memory_space=pl.ANY)] * len(deps),
        out_specs=block,
        out_shape=jax.ShapeDtypeStruct((rows, columns), dtype),
        compiler_params=pltpu.CompilerParams(
            dimension_semantics=("arbitrary", "arbitrary"), vmem_limit_bytes=VMEM_BYTES
        ),
        cost_estimate=work(sum(2 * length * rows * columns for left in lefts) / 0.66e9),
        name="weight_sums",
    )(*lefts, *rights, *extra, *deps)


def gathered_rows_kernel(places, rows, out):
    moved = to_gathered_tiles(tiles_of(rows[...].astype(jnp.float32)), *places)
    out[...] = jnp.concatenate(moved, axis=1).astype(out.dtype)


def gathered_rows(rows, places):
    tokens, width = rows.shape
    block = pl.BlockSpec((SPAN, width), lambda i: (i, 0))
    return pl.pallas_call(
        functools.partial(gathered_rows_kernel, places),
        grid=(tokens // SPAN,),
        in_specs=[block],
        out_specs=block,
        out_shape=jax.ShapeDtypeStruct((tokens, width), rows.dtype),
        compiler_params=pltpu.CompilerParams(
            dimension_semantics=("arbitrary",), vmem_limit_bytes=VMEM_BYTES
        ),
        cost_estimate=work(1.5),
        name="gathered_rows",
    )(rows)


def matmul_rows(left, right):
    return jnp.einsum("tc,cd->td", left, right, preferred_element_type=jnp.float32)


def matmul_back(left, right):
    return jnp.einsum("td,cd->tc", left, right, preferred_element_type=jnp.float32)


def weight_grad(left, right):
    return jnp.einsum("tc,td->cd", left, right, preferred_element_type=jnp.float32)


def peers(count, flip):
    return [(i, i ^ flip) for i in range(count)]


def swap(value, flip):
    return lax.ppermute(value, "seq", peers(lax.axis_size("seq"), flip))


def block_order(tokens):
    return [(flip, half) for flip in range(lax.axis_size("seq")) for half in range(tokens // SPAN)]


def block_places(tokens):
    halves = tokens // SPAN
    blocks = jnp.arange(lax.axis_size("seq") * halves, dtype=jnp.int32)
    return ((blocks // halves) ^ lax.axis_index("seq")) * halves + blocks % halves


def fetch_tokens(rows):
    return [rows] + [swap(rows, flip) for flip in range(1, lax.axis_size("seq"))]


def scatter_tokens(lefts, rights, back, tokens, hold=(), deps=(), weight=1):
    f32, bf16 = jnp.float32, jnp.bfloat16
    halves = tokens // SPAN
    count = lax.axis_size("seq")
    sets = tuple(tuple(range(flip * halves, (flip + 1) * halves)) for flip in range(count))
    own, *parts = product_rows(lefts, rights, back, sets, (f32,) + (bf16,) * (count - 1), deps, weight)
    arrived = [swap(after(part, *hold) if hold else part, flip + 1) for flip, part in enumerate(parts)]
    return own, tuple(arrived), tuple(parts)


def add_over(vector, axis):
    count = lax.axis_size(axis)
    flip = 1
    while flip < count:
        vector = vector + lax.ppermute(vector, axis, peers(count, flip))
        flip *= 2
    return vector


def trade(stacked):
    return lax.all_to_all(stacked, "seq", split_axis=0, concat_axis=0, tiled=True)


def gather_weights(rows):
    return lax.all_gather(rows.reshape(-1, rows.shape[-1]), "fsdp", axis=0, tiled=True)


def spread_sums(grad):
    return lax.psum_scatter(grad, "fsdp", scatter_dimension=0, tiled=True)


def to_gathered(rows):
    seq, fsdp = lax.axis_size("seq"), lax.axis_size("fsdp")
    shape = rows.shape
    split = rows.reshape(shape[:-1] + (seq, fsdp, -1))
    return jnp.swapaxes(split, -3, -2).reshape(shape)


def from_gathered(rows):
    seq, fsdp = lax.axis_size("seq"), lax.axis_size("fsdp")
    shape = rows.shape
    split = rows.reshape(shape[:-1] + (fsdp, seq, -1))
    return jnp.swapaxes(split, -3, -2).reshape(shape)


def on_device(
    inputs,
    cotangent,
    segments,
    norm_in,
    ssm_in,
    attn_in,
    conv_w,
    conv_b,
    a_log,
    dt_bias,
    d_skip,
    ssm_out,
    attn_out,
    norm_ffn,
    w_gate,
    w_up,
    w_down,
):
    f32, bf16 = jnp.float32, jnp.bfloat16
    seq = lax.axis_size("seq")
    fsdp = lax.axis_size("fsdp")
    index = lax.axis_index("seq")
    rows = ssm_in.shape[0]
    tokens = inputs.shape[2]
    length = segments.shape[2]
    heads = SSM_HEADS // seq
    inner = heads * SSM_DIM
    query_heads = Q_HEADS // seq
    q_width = query_heads * HEAD_DIM
    qkv_width = q_width + 2 * HEAD_DIM
    groups = Q_HEADS // KV_HEADS
    kv_of = [(s * query_heads) // groups for s in range(seq)]
    head_start = index * heads
    inner_start = index * inner
    z_end, x_end, bc_end = SSM_INNER, 2 * SSM_INNER, 2 * SSM_INNER + 2 * STATE
    q_end = Q_HEADS * HEAD_DIM
    kv_end = q_end + KV_HEADS * HEAD_DIM

    def by_seq(block):
        return jnp.swapaxes(block.reshape(rows, seq, -1), 0, 1)

    def for_all(block):
        return jnp.broadcast_to(block[None], (seq,) + block.shape)

    def by_kv(block):
        return jnp.stack([block[:, h * HEAD_DIM : (h + 1) * HEAD_DIM] for h in kv_of])

    channels = conv_b.shape[0]
    conv_pack = jnp.concatenate([conv_w, conv_b[None]], axis=0).reshape(-1)
    conv_cols = -(-conv_pack.shape[0] // rows)
    conv_pack = jnp.pad(conv_pack, (0, conv_cols * rows - conv_pack.shape[0])).reshape(rows, conv_cols)
    misc = jnp.concatenate([norm_in[:, None], norm_ffn[:, None], conv_pack], axis=1)
    misc = jnp.pad(misc, ((0, 0), (0, 128 - misc.shape[1])))
    early_send = jnp.concatenate(
        [by_seq(attn_in[:, :q_end]), by_kv(attn_in[:, q_end:kv_end]), by_kv(attn_in[:, kv_end:]), for_all(misc)],
        axis=2,
    )
    halves = tokens // SPAN
    places = (rows, seq, fsdp)
    spots = block_order(tokens)
    mine = gathered_rows(inputs[0, 0], places)
    dt_block = jnp.pad(by_seq(ssm_in[:, bc_end:]), ((0, 0), (0, 0), (0, 128 - heads)))
    first_send = jnp.concatenate(
        [by_seq(ssm_in[:, z_end:x_end]), for_all(ssm_in[:, x_end:bc_end]), dt_block], axis=2
    )
    start_mine = trade(jnp.concatenate([early_send, first_send], axis=2))
    early_mine, first_mine = start_mine[:, :, : early_send.shape[2]], start_mine[:, :, early_send.shape[2] :]
    later_send = jnp.concatenate([by_seq(ssm_in[:, :z_end]), by_seq(w_gate), by_seq(w_up)], axis=2)
    pieces = [fetch_tokens(after(mine, start_mine))]
    out_send = jnp.concatenate([ssm_out, attn_out], axis=0)
    early_w = gather_weights(early_mine)
    first_w = gather_weights(first_mine)
    out_rows = ssm_out.shape[0]
    units = w_down.shape[0] * fsdp
    small = early_w[:, qkv_width:]

    def gain_rows(gain):
        return jnp.broadcast_to(gain.astype(f32)[None], (8, gain.shape[0]))

    gain_in_gathered = gain_rows(small[:, 0])
    gain_in = gain_rows(from_gathered(small[:, 0]))
    gain_ffn = gain_rows(from_gathered(small[:, 1]))
    conv_all = small[:, 2 : 2 + conv_cols].reshape(fsdp, seq, -1)[:, :, : (CONV + 1) * channels]
    conv_all = conv_all.reshape(fsdp, seq, CONV + 1, channels).transpose(2, 1, 0, 3)
    conv_all = conv_all.reshape(CONV + 1, CONV_CH).astype(f32)
    conv_local = jnp.concatenate(
        [lax.dynamic_slice_in_dim(conv_all, inner_start, inner, 1), conv_all[:, SSM_INNER:]], axis=1
    )
    conv_table = jnp.pad(conv_local, ((0, 8 - CONV - 1), (0, 0)))
    rate_local = lax.dynamic_slice_in_dim(a_log.astype(f32), head_start, heads)
    bias_local = lax.dynamic_slice_in_dim(dt_bias.astype(f32), head_start, heads)
    skip_local = lax.dynamic_slice_in_dim(d_skip.astype(f32), head_start, heads)
    head_table = jnp.pad(jnp.stack([bias_local, rate_local]), ((0, 6), (0, 128 - heads)))
    skip_table = jnp.broadcast_to(jnp.repeat(skip_local, SSM_DIM)[None], (8, inner))
    tables = rotary_tables(length)
    order = block_places(tokens)

    micro = range(MICRO)
    auxes = [token_aux(segments[m, 0]) for m in micro]
    seg_blocks = [segments[m, 0].astype(f32).reshape(-1, 1, SPAN) for m in micro]
    seg_rows = [segments[m, 0].astype(f32)[None] for m in micro]
    width = inputs.shape[3]
    head_tables = (conv_table, head_table, skip_table)

    hiddens, earlies, attendeds, lses, firsts, ys, all_starts = [], [], [], [], [], [], []
    gate_zs, gateds, mixeds, cot_alls = [], [], [], []
    def mixer_start(m, deps=()):
        if deps:
            pieces[m][0] = after(pieces[m][0], *deps)
        hidden = norm_pieces(pieces[m], spots, gain_in_gathered)
        early = matmul_rows(hidden, early_w).astype(bf16)
        attended, lse = attend_forward(order, early, tables, auxes[m], seg_rows[m], query_heads)
        hiddens.append(hidden)
        earlies.append(early)
        attendeds.append(attended)
        lses.append(lse)

    def mixer_scan(m, deps):
        hiddens[m] = after(hiddens[m], *deps)
        first = matmul_rows(hiddens[m], first_w).astype(bf16)
        y_rows, starts = ssd_forward(order, first, auxes[m], seg_blocks[m], *head_tables, heads)
        firsts.append(first)
        ys.append(y_rows)
        all_starts.append(starts)

    def mixer_gate(m, deps):
        hiddens[m] = after(hiddens[m], *deps)
        gate_z = matmul_rows(hiddens[m], z_w)
        gate_zs.append(gate_z)
        gateds.append((ys[m].astype(f32) * jax.nn.silu(gate_z)).astype(bf16))

    def mixer_out(m, deps, hold=()):
        mixeds.append(
            scatter_tokens([gateds[m], attendeds[m]], [ssm_out_w, attn_out_w], False, tokens, hold, deps, m)
        )

    later_mine = trade(after(later_send, *pieces[0][1:]))
    mixer_start(0, [later_mine])
    start_second = start_rows(inputs[1, 0], [cotangent[m, 0] for m in micro], places)
    pieces.append(fetch_tokens(after(start_second, later_mine)))
    z_mine, ffn_mine = later_mine[:, :, :inner], later_mine[:, :, inner:]
    z_w = gather_weights(z_mine)
    out_send = after(out_send, z_mine)
    out_w = gather_weights(out_send)
    gate_up_w = gather_weights(after(ffn_mine, out_send))
    mixer_scan(0, [attendeds[0], later_mine, start_second])
    down_w = gather_weights(after(w_down, firsts[0]))
    out_w = out_w.reshape(fsdp, -1, out_w.shape[1])
    ssm_out_w, attn_out_w = out_w[:, :out_rows].reshape(inner, -1), out_w[:, out_rows:].reshape(q_width, -1)
    side_w = jnp.concatenate([early_w[:, :qkv_width], z_w], axis=1)
    mixer_gate(0, [ys[0]])
    mixer_out(0, [gateds[0]])
    mixer_start(1, [mixeds[0][0]])
    for m in micro:
        cot_alls.append(assemble(pieces[1], [(flip, half + (1 + m) * halves) for flip, half in spots]))

    middles, ffn_hiddens, activateds, grad_gus, grad_hiddens = [], [], [], [], []
    grad_middles, lows, grads_mixed = [], [], []

    def middle_forward(m, deps, hold=()):
        own, arrived, parts = mixeds[m]
        hidden, middle = rows_call(
            functools.partial(middle_kernel, places, len(arrived), len(deps)),
            tokens,
            width,
            [own, inputs[m, 0]],
            gain_ffn,
            arrived,
            [((tokens, width), bf16), ((tokens, width), f32)],
            deps,
            "middle",
        )
        middles.append(middle)
        if hold:
            hidden = after(hidden, *hold)
        ffn_hiddens.append(assemble(fetch_tokens(hidden), spots))

    def feed_forward(m, deps, late=()):
        ffn_hiddens[m] = after(ffn_hiddens[m], *deps)
        activated, grad_gu = feed_products(ffn_hiddens[m], cot_alls[m], gate_up_w, down_w)
        activateds.append(activated)
        grad_gus.append(grad_gu)
        grad_hiddens.append(scatter_tokens([grad_gu], [gate_up_w], True, tokens, (), late))

    def middle_back(m, deps):
        own, arrived, parts = grad_hiddens[m]
        low, wide = rows_call(
            functools.partial(norm_back_kernel, places, len(arrived), len(deps), True),
            tokens,
            width,
            [own, middles[m], cotangent[m, 0]],
            gain_ffn,
            arrived,
            [((tokens, width), bf16), ((tokens, width), f32)],
            deps,
            "middle_back",
        )
        grad_middles.append(wide)
        lows.append(low)
        grads_mixed.append(assemble(fetch_tokens(low), spots))

    grad_ys, grad_sides, outs, back, in_backs, outputs = [], [], [], [], [], []

    def heads_back(m, deps):
        grad_mixed = after(grads_mixed[m], *deps)
        grads_mixed[m] = grad_mixed
        grad_gated = matmul_back(grad_mixed, ssm_out_w)
        grad_attended = matmul_back(grad_mixed, attn_out_w).astype(bf16)
        gate_z = gate_zs[m]
        sig = jax.nn.sigmoid(gate_z)
        y_wide = ys[m].astype(f32)
        grad_ys.append((grad_gated * gate_z * sig).astype(bf16))
        grad_z = (grad_gated * y_wide * sig * (1.0 + gate_z * (1.0 - sig))).astype(bf16)
        grad_qkv = attend_backward(
            order, earlies[m], tables, auxes[m], seg_rows[m], lses[m], grad_attended, query_heads
        )
        grad_sides.append(jnp.concatenate([grad_qkv, grad_z], axis=1))

    def output_rows(m, deps, hold=()):
        outs.append(scatter_tokens([activateds[m]], [down_w], False, tokens, hold, deps))

    def scan_back(m, deps):
        grad_y = after(grad_ys[m], *deps)
        back.append(
            ssd_backward(order, firsts[m], auxes[m], seg_blocks[m], *head_tables, all_starts[m], grad_y, heads)
        )

    def hidden_back(m, deps, hold=()):
        in_backs.append(
            scatter_tokens([back[m][0], grad_sides[m]], [first_w, side_w], True, tokens, hold, deps)
        )

    def finish_input(m, deps=()):
        own, arrived, parts = in_backs[m]
        return rows_call(
            functools.partial(norm_back_kernel, places, len(arrived), len(deps), False),
            tokens,
            width,
            [own, inputs[m, 0], grad_middles[m]],
            gain_in,
            arrived,
            [((tokens, width), bf16)],
            deps,
            "input_back",
        )[0]

    def finish_output(m, deps=()):
        own, arrived, parts = outs[m]
        return rows_call(
            functools.partial(add_rows_kernel, len(arrived)),
            tokens,
            width,
            [own, middles[m]],
            gain_ffn,
            arrived,
            [((tokens, width), bf16)],
            deps,
            "output_rows",
        )[0]

    def both(lefts, rights):
        return (weight_grad(lefts[0], rights[0]) + weight_grad(lefts[1], rights[1])).astype(bf16)

    def back_to_rows(part):
        return trade(part.reshape(seq, rows, -1)).astype(f32)

    middle_forward(0, [attendeds[1]])
    mixer_scan(1, [middles[0]])
    mixer_gate(1, [ys[1]])
    mixer_out(1, [gateds[1]])
    mixeds[1] = (
        mixeds[1][0],
        tuple(swap(after(part, ffn_hiddens[0]), flip + 1) for flip, part in enumerate(mixeds[1][2])),
        (),
    )
    feed_forward(0, ())
    gate_up_sum = weight_sums(ffn_hiddens[:1], grad_gus[:1], f32, None, [grad_hiddens[0][0], *mixeds[1][1]])
    down_sum = weight_sums(activateds[:1], cot_alls[:1], f32, None, [gate_up_sum])
    middle_back(0, [down_sum])
    middle_forward(1, (), [grads_mixed[0]])
    heads_back(0, ())
    output_rows(0, grad_sides, [ffn_hiddens[1]])
    feed_forward(1, [outs[0][0]])
    outputs.append(finish_output(0, [grad_hiddens[1][0]]))
    gate_up_sum = weight_sums(ffn_hiddens[1:], grad_gus[1:], bf16, gate_up_sum, [outputs[0]])
    gate_up_part = spread_sums(gate_up_sum)
    scan_back(0, [gate_up_sum])
    side_sum = weight_sums(hiddens[:1], grad_sides[:1], f32, None, [back[0][0]])
    ssm_out_sum = weight_sums(gateds[:1], grads_mixed[:1], f32, None, [side_sum])
    attn_out_sum = weight_sums(attendeds[:1], grads_mixed[:1], f32, None, [ssm_out_sum])
    middle_back(1, [attn_out_sum])

    down_sum = weight_sums(activateds[1:], cot_alls[1:], bf16, down_sum, [lows[1]])
    down_part = spread_sums(down_sum)
    hidden_back(0, [down_sum], [grads_mixed[1]])
    output_rows(1, [in_backs[0][0]], [grads_mixed[1]])
    first_sum = weight_sums(hiddens[:1], [back[0][0]], f32, None, [outs[1][0]])
    ssm_out_sum = weight_sums(gateds[1:], grads_mixed[1:], bf16, ssm_out_sum, [first_sum])
    attn_out_sum = weight_sums(attendeds[1:], grads_mixed[1:], bf16, attn_out_sum, [ssm_out_sum])
    out_sum = jnp.concatenate(
        [ssm_out_sum.reshape(fsdp, -1, width), attn_out_sum.reshape(fsdp, -1, width)], axis=1
    ).reshape(inner + q_width, width)
    out_part = spread_sums(out_sum)
    heads_back(1, [out_sum])
    outputs.append(finish_output(1, [grad_sides[1]]))
    side_sum = weight_sums(hiddens[1:], grad_sides[1:], bf16, side_sum, [outputs[1], gate_up_part])
    side_part = spread_sums(side_sum)
    gate_up_back = back_to_rows(gate_up_part)
    side_back = back_to_rows(side_part)
    scan_back(1, [side_sum, down_part])
    low = finish_input(0, [back[1][0]])
    input_grads = [low]
    conv_grad = (back[0][1] + back[1][1])[: CONV + 1]
    head_grad = back[0][2] + back[1][2]
    skip_sum = jnp.sum((back[0][3] + back[1][3])[0].reshape(heads, SSM_DIM), axis=1)
    conv_whole = jnp.zeros((CONV + 1, CONV_CH), f32)
    conv_whole = lax.dynamic_update_slice_in_dim(conv_whole, conv_grad[:, :inner], inner_start, 1)
    conv_whole = lax.dynamic_update_slice_in_dim(conv_whole, conv_grad[:, inner:], SSM_INNER, 1)
    head_sums = lax.dynamic_update_slice_in_dim(
        jnp.zeros((3, SSM_HEADS), f32), jnp.stack([head_grad[0, :heads], head_grad[1, :heads], skip_sum]), head_start, 1
    )
    small_sums = [conv_whole.reshape(-1), head_sums.reshape(-1)]
    ends = [0]
    for piece in small_sums:
        ends.append(ends[-1] + piece.shape[0])
    total = add_over(jnp.concatenate(small_sums), "seq")
    first_sum = weight_sums(hiddens[1:], [back[1][0]], bf16, first_sum, [low, gate_up_back, out_part, total])
    first_part = spread_sums(first_sum)
    first_back = back_to_rows(first_part)
    hidden_back(1, [first_sum])
    total = add_over(after(total, in_backs[1][0]), "fsdp")
    input_grads.append(finish_input(1))

    out_part = after(out_part, in_backs[1][0]).astype(f32)

    def own_columns(block):
        return jnp.swapaxes(block, 0, 1).reshape(rows, -1)

    def kv_columns(block):
        return jnp.concatenate(
            [sum(block[s] for s in range(seq) if kv_of[s] == h) for h in range(KV_HEADS)], axis=1
        )

    gate_grad = own_columns(gate_up_back[:, :, :units])
    up_grad = own_columns(gate_up_back[:, :, units:])
    ssm_in_grad = jnp.concatenate(
        [
            own_columns(side_back[:, :, qkv_width:]),
            own_columns(first_back[:, :, :inner]),
            jnp.sum(first_back[:, :, inner : inner + 2 * STATE], axis=0),
            own_columns(first_back[:, :, inner + 2 * STATE : inner + 2 * STATE + heads]),
        ],
        axis=1,
    )
    attn_in_grad = jnp.concatenate(
        [
            own_columns(side_back[:, :, :q_width]),
            kv_columns(side_back[:, :, q_width : q_width + HEAD_DIM]),
            kv_columns(side_back[:, :, q_width + HEAD_DIM : qkv_width]),
        ],
        axis=1,
    )

    conv_total, head_total = (total[a:b] for a, b in zip(ends[:-1], ends[1:]))
    def gain_grad(gain, *pairs):
        total = sum(jnp.sum(weight.astype(f32) * grad, axis=1) for weight, grad in pairs)
        return total / gain.astype(f32)

    place = index * fsdp + lax.axis_index("fsdp")
    conv_total = lax.dynamic_slice_in_dim(conv_total.reshape(CONV + 1, CONV_CH), place * channels, channels, 1)
    head_total = head_total.reshape(3, SSM_HEADS)
    return (
        jnp.stack(outputs)[:, None],
        jnp.stack(input_grads)[:, None],
        gain_grad(norm_in, (ssm_in, ssm_in_grad), (attn_in, attn_in_grad)),
        ssm_in_grad,
        attn_in_grad,
        conv_total[:CONV],
        conv_total[CONV],
        head_total[0],
        head_total[1],
        head_total[2],
        out_part[:out_rows],
        out_part[out_rows:],
        gain_grad(norm_ffn, (w_gate, gate_grad), (w_up, up_grad)),
        gate_grad,
        up_grad,
        after(down_part, in_backs[1][0]).astype(f32),
    )


def solution(mesh):
    return jax.shard_map(
        on_device,
        mesh=mesh,
        in_specs=(
            P(None, "fsdp", "seq", None),
            P(None, "fsdp", "seq", None),
            P(None, "fsdp", None),
            P(("seq", "fsdp")),
            P(("seq", "fsdp"), None),
            P(("seq", "fsdp"), None),
            P(None, ("seq", "fsdp")),
            P(("seq", "fsdp")),
            P(),
            P(),
            P(),
            P(("seq", "fsdp"), None),
            P(("seq", "fsdp"), None),
            P(("seq", "fsdp")),
            P(("seq", "fsdp"), None),
            P(("seq", "fsdp"), None),
            P(("seq", "fsdp"), None),
        ),
        out_specs=(
            P(None, "fsdp", "seq", None),
            P(None, "fsdp", "seq", None),
            P(("seq", "fsdp")),
            P(("seq", "fsdp"), None),
            P(("seq", "fsdp"), None),
            P(None, ("seq", "fsdp")),
            P(("seq", "fsdp")),
            P(),
            P(),
            P(),
            P(("seq", "fsdp"), None),
            P(("seq", "fsdp"), None),
            P(("seq", "fsdp")),
            P(("seq", "fsdp"), None),
            P(("seq", "fsdp"), None),
            P(("seq", "fsdp"), None),
        ),
        check_vma=False,
    )
```

```python
import functools

import jax
import jax.numpy as jnp
from jax import lax
from jax.experimental import pallas as pl
from jax.experimental.pallas import tpu as pltpu
from jax.sharding import PartitionSpec as P

SSM_HEADS = 48
SSM_DIM = 64
STATE = 256
CONV = 4
Q_HEADS = 8
KV_HEADS = 2
HEAD_DIM = 128
MICRO = 2
SPAN = 128
SSM_INNER = 3072
CONV_CH = 3584
ATT_ROWS = 256
VMEM_BYTES = 48 * 1024 * 1024


PRECISE = lax.Precision.HIGHEST
EPSILON = 1e-05
ROPE_BASE = 10000.0


def work(us):
    return pl.CostEstimate(flops=int(us * 1150000000), bytes_accessed=0, transcendentals=0)


def lanes_iota(shape):
    return lax.broadcasted_iota(jnp.int32, shape, 1)


def rows_iota(shape):
    return lax.broadcasted_iota(jnp.int32, shape, 0)


def dot_last(left, right):
    return lax.dot_general(left, right, (((1,), (1,)), ((), ())), preferred_element_type=jnp.float32)


def dot_first(left, right):
    return lax.dot_general(left, right, (((0,), (0,)), ((), ())), preferred_element_type=jnp.float32)


def dot_plain(left, right):
    return jnp.dot(left, right, preferred_element_type=jnp.float32)


def head_steps(block, head_ref, heads):
    pre = block.astype(jnp.float32) + head_ref[0:1, :]
    live = lanes_iota(pre.shape) < heads
    pre = jnp.where(live, pre, 0.0)
    step = jnp.maximum(pre, 0.0) + jnp.log1p(jnp.exp(-jnp.abs(pre)))
    step = jnp.where(live, step, 0.0)
    rate = -jnp.exp(head_ref[1:2, :])
    decay = rate * step
    lower = (rows_iota((SPAN, SPAN)) >= lanes_iota((SPAN, SPAN))).astype(jnp.float32)
    total = jnp.dot(lower, decay, precision=PRECISE, preferred_element_type=jnp.float32)
    return step, rate, decay, total, pre


def over_lanes(column):
    return jnp.broadcast_to(column, (column.shape[0], 128))


def convolve(ubuf, near, conv_ref, lanes):
    acc = conv_ref[CONV : CONV + 1, lanes] + conv_ref[CONV - 1 : CONV, lanes] * ubuf[8 : 8 + SPAN, lanes]
    for offset in range(1, CONV):
        shifted = ubuf[8 - offset : 8 - offset + SPAN, lanes]
        weight = conv_ref[CONV - 1 - offset : CONV - offset, lanes]
        acc = acc + weight * (shifted * near[offset])
    return acc


def pair_of(values, first_head, low_lanes):
    one = jnp.broadcast_to(values[:, first_head : first_head + 1], (SPAN, 128))
    two = jnp.broadcast_to(values[:, first_head + 1 : first_head + 2], (SPAN, 128))
    return one, two, jnp.where(low_lanes, one, two)


def ssd_forward_kernel(
    heads,
    order_ref,
    first_ref,
    aux_ref,
    seg_ref,
    conv_ref,
    head_ref,
    skip_ref,
    y_ref,
    start_ref,
    ubuf,
    taps,
    state,
):
    f32, bf16 = jnp.float32, jnp.bfloat16
    inner = heads * SSM_DIM
    width = inner + 2 * STATE

    @pl.when(pl.program_id(0) == 0)
    def _():
        ubuf[SPAN : SPAN + 8, :] = jnp.zeros((8, width), f32)
        state[...] = jnp.zeros((STATE, inner), f32)

    ubuf[0:8, :] = ubuf[SPAN : SPAN + 8, :]
    ubuf[8 : 8 + SPAN, :] = first_ref[:, :width].astype(f32)
    near = [None] + [over_lanes(aux_ref[:, 2 + offset : 3 + offset]) for offset in range(1, CONV)]
    for lane in range(0, width, 128):
        lanes = slice(lane, lane + 128)
        pre = convolve(ubuf, near, conv_ref, lanes)
        taps[:, lanes] = (pre * jax.nn.sigmoid(pre)).astype(bf16)
    step, rate, decay, total, unused = head_steps(first_ref[:, width:], head_ref, heads)
    total_rows = total.T
    low_lanes = lanes_iota((SPAN, 128)) < SSM_DIM
    same = (aux_ref[:, 0:1] == seg_ref[0]) & (rows_iota((SPAN, SPAN)) >= lanes_iota((SPAN, SPAN)))
    b_rows = taps[:, inner : inner + STATE]
    c_rows = taps[:, inner + STATE :]
    b_cols = b_rows.astype(f32).T.astype(bf16)
    scores = dot_last(c_rows, b_rows)
    carry_keep, end_keep = over_lanes(aux_ref[:, 1:2]), over_lanes(aux_ref[:, 2:3])
    for pair in range(heads // 2):
        lanes = slice(pair * 128, pair * 128 + 128)
        sum_one, sum_two, sums = pair_of(total, 2 * pair, low_lanes)
        steps = pair_of(step, 2 * pair, low_lanes)[2]
        row_one = total_rows[2 * pair : 2 * pair + 1, :]
        row_two = total_rows[2 * pair + 1 : 2 * pair + 2, :]
        mix_one = (jnp.exp(jnp.where(same, sum_one - row_one, -1e30)) * scores).astype(bf16)
        mix_two = (jnp.exp(jnp.where(same, sum_two - row_two, -1e30)) * scores).astype(bf16)
        x = taps[:, lanes].astype(f32)
        stepped = (x * steps).astype(bf16)
        none = jnp.zeros_like(stepped)
        split = jnp.concatenate(
            [jnp.where(low_lanes, stepped, none), jnp.where(low_lanes, none, stepped)], axis=0
        )
        held = state[:, lanes]
        held_low = held.astype(bf16)
        start_ref[0, :, lanes] = held_low
        y = dot_plain(jnp.concatenate([mix_one, mix_two], axis=1), split)
        y = y + jnp.exp(sums) * carry_keep * dot_plain(c_rows, held_low)
        y_ref[:, lanes] = (y + skip_ref[0:1, lanes] * x).astype(bf16)
        last = sums[SPAN - 1 : SPAN, :]
        weighted = (jnp.exp(last - sums) * end_keep * stepped.astype(f32)).astype(bf16)
        kept = jnp.exp(last) * aux_ref[SPAN - 1 : SPAN, 1:2]
        state[:, lanes] = held * kept + dot_plain(b_cols, weighted)


def halves_of(values):
    high = values.astype(jnp.bfloat16)
    return [high, (values - high.astype(jnp.float32)).astype(jnp.bfloat16)]


def ssd_backward_kernel(
    heads,
    order_ref,
    first_ref,
    before_ref,
    aux_ref,
    seg_ref,
    conv_ref,
    head_ref,
    skip_ref,
    start_ref,
    dy_ref,
    grad_ref,
    conv_grad_ref,
    head_grad_ref,
    skip_grad_ref,
    ubuf,
    taps,
    slope,
    gbuf,
    dstate,
):
    f32, bf16 = jnp.float32, jnp.bfloat16
    inner = heads * SSM_DIM
    width = inner + 2 * STATE

    @pl.when(pl.program_id(0) == 0)
    def _():
        gbuf[0:8, :] = jnp.zeros((8, width), f32)
        dstate[...] = jnp.zeros((STATE, inner), f32)
        conv_grad_ref[...] = jnp.zeros(conv_grad_ref.shape, f32)
        head_grad_ref[...] = jnp.zeros(head_grad_ref.shape, f32)
        skip_grad_ref[...] = jnp.zeros(skip_grad_ref.shape, f32)

    ubuf[0:8, :] = before_ref[8:16, :width].astype(f32)
    ubuf[8 : 8 + SPAN, :] = first_ref[:, :width].astype(f32)
    gbuf[SPAN : SPAN + 8, :] = gbuf[0:8, :]
    near = [None] + [over_lanes(aux_ref[:, 2 + offset : 3 + offset]) for offset in range(1, CONV)]
    for lane in range(0, width, 128):
        lanes = slice(lane, lane + 128)
        pre = convolve(ubuf, near, conv_ref, lanes)
        sig = jax.nn.sigmoid(pre)
        taps[:, lanes] = (pre * sig).astype(bf16)
        slope[:, lanes] = sig * (1.0 + pre * (1.0 - sig))
    step, rate, decay, total, pre_step = head_steps(first_ref[:, width:], head_ref, heads)
    total_rows = total.T
    square = (SPAN, SPAN)
    low_lanes = lanes_iota((SPAN, 128)) < SSM_DIM
    low_row = lanes_iota((1, 128)) < SSM_DIM
    head_row = lanes_iota((1, 128))
    same = (aux_ref[:, 0:1] == seg_ref[0]) & (rows_iota(square) >= lanes_iota(square))
    b_rows = taps[:, inner : inner + STATE]
    c_rows = taps[:, inner + STATE :]
    c_cols = c_rows.astype(f32).T.astype(bf16)
    scores = dot_last(c_rows, b_rows)
    carry_keep, end_keep = over_lanes(aux_ref[:, 1:2]), over_lanes(aux_ref[:, 2:3])
    head_lane = lanes_iota((SPAN, 128))
    is_last = rows_iota((SPAN, 1)) == SPAN - 1
    grad_scores = jnp.zeros(square, f32)
    grad_b = jnp.zeros((SPAN, STATE), f32)
    grad_c = jnp.zeros((SPAN, STATE), f32)
    grad_total = jnp.zeros((SPAN, 128), f32)
    grad_step = jnp.zeros((SPAN, 128), f32)
    for pair in range(heads // 2):
        lanes = slice(pair * 128, pair * 128 + 128)
        sum_one, sum_two, sums = pair_of(total, 2 * pair, low_lanes)
        steps = pair_of(step, 2 * pair, low_lanes)[2]
        row_one = total_rows[2 * pair : 2 * pair + 1, :]
        row_two = total_rows[2 * pair + 1 : 2 * pair + 2, :]
        decay_one = jnp.exp(jnp.where(same, sum_one - row_one, -1e30))
        decay_two = jnp.exp(jnp.where(same, sum_two - row_two, -1e30))
        mix_one = (decay_one * scores).astype(bf16)
        mix_two = (decay_two * scores).astype(bf16)
        x = taps[:, lanes].astype(f32)
        stepped = (x * steps).astype(bf16)
        none = jnp.zeros_like(stepped)
        x_one = jnp.where(low_lanes, stepped, none)
        x_two = jnp.where(low_lanes, none, stepped)
        dy_low = dy_ref[:, lanes]
        dy = dy_low.astype(f32)
        dy_one = jnp.where(low_lanes, dy_low, none)
        dy_two = jnp.where(low_lanes, none, dy_low)
        grad_scores = grad_scores + dot_last(dy_one, stepped) * decay_one + dot_last(dy_two, stepped) * decay_two
        y = dot_plain(
            jnp.concatenate([mix_one, mix_two], axis=1), jnp.concatenate([x_one, x_two], axis=0)
        )
        grad_in = dot_first(
            jnp.concatenate([mix_one, mix_two], axis=0), jnp.concatenate([dy_one, dy_two], axis=0)
        )
        held = start_ref[0, :, lanes]
        dheld = dstate[:, lanes]
        dheld_low = dheld.astype(bf16)
        grown = jnp.exp(sums) * carry_keep
        y = y + grown * dot_plain(c_rows, held)
        grown_dy = (grown * dy).astype(bf16)
        last = sums[SPAN - 1 : SPAN, :]
        fade = jnp.exp(last - sums) * end_keep
        stepped_wide = stepped.astype(f32)
        weighted = (fade * stepped_wide).astype(bf16)
        from_end = dot_plain(b_rows, dheld_low)
        grad_in = grad_in + fade * from_end
        grad_c = grad_c + dot_last(grown_dy, held)
        grad_b = grad_b + dot_last(weighted, dheld_low)
        kept = jnp.exp(last) * aux_ref[SPAN - 1 : SPAN, 1:2]
        ends = jnp.sum(fade * stepped_wide * from_end, axis=0, keepdims=True) + kept * jnp.sum(
            dheld * held.astype(f32), axis=0, keepdims=True
        )
        dstate[:, lanes] = dheld * kept + dot_plain(c_cols, grown_dy)
        gaps = dy * y - stepped_wide * grad_in
        by_step = x * grad_in
        ends_one = jnp.sum(jnp.where(low_row, ends, 0.0), axis=1, keepdims=True)
        ends_two = jnp.sum(jnp.where(low_row, 0.0, ends), axis=1, keepdims=True)
        ends_here = jnp.where(head_row == 2 * pair, ends_one, jnp.where(head_row == 2 * pair + 1, ends_two, 0.0))
        of_head = (lanes_iota(square) == 2 * pair + rows_iota(square) // SSM_DIM).astype(bf16)
        by_head = dot_plain(jnp.concatenate(halves_of(gaps) + halves_of(by_step), axis=0), of_head)
        grad_total = grad_total + by_head[:SPAN] + by_head[SPAN : 2 * SPAN] + jnp.where(is_last, ends_here, 0.0)
        grad_step = grad_step + by_head[2 * SPAN : 3 * SPAN] + by_head[3 * SPAN :]
        skip = skip_ref[0:1, lanes]
        skip_grad_ref[0:1, lanes] += jnp.sum(dy * x, axis=0, keepdims=True)
        gbuf[0:SPAN, lanes] = (steps * grad_in + skip * dy) * slope[:, lanes]
    low_scores = grad_scores.astype(bf16)
    grad_c = grad_c + dot_plain(low_scores, b_rows)
    grad_b = grad_b + dot_first(low_scores, c_rows)
    gbuf[0:SPAN, inner : inner + STATE] = grad_b * slope[:, inner : inner + STATE]
    gbuf[0:SPAN, inner + STATE : width] = grad_c * slope[:, inner + STATE : width]

    upper = (rows_iota(square) <= lanes_iota(square)).astype(f32)
    grad_decay = jnp.dot(upper, grad_total, precision=PRECISE, preferred_element_type=f32)
    grad_pre = (grad_step + rate * grad_decay) * jax.nn.sigmoid(pre_step)
    grad_pre = jnp.where(head_lane < heads, grad_pre, 0.0)
    grad_ref[:, width:] = grad_pre.astype(bf16)
    head_grad_ref[0:1, :] += jnp.sum(grad_decay * decay, axis=0, keepdims=True)
    head_grad_ref[1:2, :] += jnp.sum(grad_pre, axis=0, keepdims=True)

    ahead = [None] + [over_lanes(aux_ref[:, 5 + offset : 6 + offset]) for offset in range(1, CONV)]
    for lane in range(0, width, 128):
        lanes = slice(lane, lane + 128)
        grad = gbuf[0:SPAN, lanes]
        conv_grad_ref[CONV : CONV + 1, lanes] += jnp.sum(grad, axis=0, keepdims=True)
        conv_grad_ref[CONV - 1 : CONV, lanes] += jnp.sum(grad * ubuf[8 : 8 + SPAN, lanes], axis=0, keepdims=True)
        acc = conv_ref[CONV - 1 : CONV, lanes] * grad
        for offset in range(1, CONV):
            at = CONV - 1 - offset
            shifted = ubuf[8 - offset : 8 - offset + SPAN, lanes] * near[offset]
            conv_grad_ref[at : at + 1, lanes] += jnp.sum(grad * shifted, axis=0, keepdims=True)
            later = gbuf[offset : offset + SPAN, lanes] * ahead[offset]
            acc = acc + conv_ref[at : at + 1, lanes] * later
        grad_ref[:, lanes] = acc.astype(bf16)


def token_aux(segment):
    length = segment.shape[0]
    ends = segment.reshape(-1, SPAN)[:, -1]
    end_of = jnp.repeat(ends, SPAN)
    before = jnp.repeat(jnp.concatenate([jnp.full((1,), -1, segment.dtype), ends[:-1]]), SPAN)
    columns = [segment, segment == before, segment == end_of]
    for offset in range(1, CONV):
        columns.append(jnp.pad(segment, (offset, 0), constant_values=-1)[:length] == segment)
    for offset in range(1, CONV):
        columns.append(jnp.pad(segment, (0, offset), constant_values=-1)[offset:] == segment)
    columns = [column.astype(jnp.float32) for column in columns]
    return jnp.stack(columns + [jnp.zeros((length,), jnp.float32)] * (16 - len(columns)), axis=1)


def ssd_specs(heads, at):
    inner = heads * SSM_DIM
    width = inner + 2 * STATE
    return [
        pl.BlockSpec((SPAN, width + 128), lambda i, order: (order[at(i)], 0)),
        pl.BlockSpec((SPAN, 16), lambda i, order: (at(i), 0)),
        pl.BlockSpec((1, 1, SPAN), lambda i, order: (at(i), 0, 0)),
        pl.BlockSpec((8, width), lambda i, order: (0, 0)),
        pl.BlockSpec((8, 128), lambda i, order: (0, 0)),
        pl.BlockSpec((8, inner), lambda i, order: (0, 0)),
    ]


def ssd_forward(order, first, aux, seg_rows, conv, head, skip, heads):
    length = first.shape[0]
    inner = heads * SSM_DIM
    width = inner + 2 * STATE
    blocks = length // SPAN
    return pl.pallas_call(
        functools.partial(ssd_forward_kernel, heads),
        grid_spec=pltpu.PrefetchScalarGridSpec(
            num_scalar_prefetch=1,
            grid=(blocks,),
            in_specs=ssd_specs(heads, lambda i: i),
            out_specs=[
                pl.BlockSpec((SPAN, inner), lambda i, order: (order[i], 0)),
                pl.BlockSpec((1, STATE, inner), lambda i, order: (i, 0, 0)),
            ],
            scratch_shapes=[
                pltpu.VMEM((SPAN + 8, width), jnp.float32),
                pltpu.VMEM((SPAN, width), jnp.bfloat16),
                pltpu.VMEM((STATE, inner), jnp.float32),
            ],
        ),
        out_shape=[
            jax.ShapeDtypeStruct((length, inner), jnp.bfloat16),
            jax.ShapeDtypeStruct((blocks, STATE, inner), jnp.bfloat16),
        ],
        compiler_params=pltpu.CompilerParams(
            dimension_semantics=("arbitrary",), vmem_limit_bytes=VMEM_BYTES
        ),
        cost_estimate=work(0),
        name="ssd_forward",
    )(order, first, aux, seg_rows, conv, head, skip)


def ssd_backward(order, first, aux, seg_rows, conv, head, skip, starts, dy, heads):
    length = first.shape[0]
    inner = heads * SSM_DIM
    width = inner + 2 * STATE
    blocks = length // SPAN
    per_block = SPAN // 16

    def at(i):
        return blocks - 1 - i

    specs = ssd_specs(heads, at)
    specs.insert(
        1,
        pl.BlockSpec(
            (16, width + 128), lambda i, order: (order[jnp.maximum(at(i) - 1, 0)] * per_block + per_block - 1, 0)
        ),
    )
    specs += [
        pl.BlockSpec((1, STATE, inner), lambda i, order: (at(i), 0, 0)),
        pl.BlockSpec((SPAN, inner), lambda i, order: (order[at(i)], 0)),
    ]
    return pl.pallas_call(
        functools.partial(ssd_backward_kernel, heads),
        grid_spec=pltpu.PrefetchScalarGridSpec(
            num_scalar_prefetch=1,
            grid=(blocks,),
            in_specs=specs,
            out_specs=[
                pl.BlockSpec((SPAN, width + 128), lambda i, order: (order[at(i)], 0)),
                pl.BlockSpec((8, width), lambda i, order: (0, 0)),
                pl.BlockSpec((8, 128), lambda i, order: (0, 0)),
                pl.BlockSpec((8, inner), lambda i, order: (0, 0)),
            ],
            scratch_shapes=[
                pltpu.VMEM((SPAN + 8, width), jnp.float32),
                pltpu.VMEM((SPAN, width), jnp.bfloat16),
                pltpu.VMEM((SPAN, width), jnp.float32),
                pltpu.VMEM((SPAN + 8, width), jnp.float32),
                pltpu.VMEM((STATE, inner), jnp.float32),
            ],
        ),
        out_shape=[
            jax.ShapeDtypeStruct((length, width + 128), jnp.bfloat16),
            jax.ShapeDtypeStruct((8, width), jnp.float32),
            jax.ShapeDtypeStruct((8, 128), jnp.float32),
            jax.ShapeDtypeStruct((8, inner), jnp.float32),
        ],
        compiler_params=pltpu.CompilerParams(
            dimension_semantics=("arbitrary",), vmem_limit_bytes=VMEM_BYTES
        ),
        cost_estimate=work(53),
        name="ssd_backward",
    )(order, first, first, aux, seg_rows, conv, head, skip, starts, dy)


def rotary_tables(length):
    half = HEAD_DIM // 2
    frequency = ROPE_BASE ** (-jnp.arange(half).astype(jnp.float32) / half)
    angles = jnp.arange(length, dtype=jnp.int32).astype(jnp.float32)[:, None] * frequency[None, :]
    cosine, sine = jnp.cos(angles), jnp.sin(angles)
    return jnp.concatenate([cosine, cosine], axis=1), jnp.concatenate([-sine, sine], axis=1)


def turn(rows, cosine, sine):
    wide = rows.astype(jnp.float32)
    return (wide * cosine + pltpu.roll(wide, HEAD_DIM // 2, 1) * sine).astype(jnp.bfloat16)


def turn_back(grads, cosine, sine):
    return (grads * cosine + pltpu.roll(grads * sine, HEAD_DIM // 2, 1)).astype(jnp.bfloat16)


def block_scores(q_block, k_part, first_row, seg_col, seg_row):
    scores = dot_last(q_block, k_part) * HEAD_DIM ** (-0.5)
    shape = scores.shape
    allowed = (rows_iota(shape) + first_row >= lanes_iota(shape)) & (seg_col == seg_row)
    return jnp.where(allowed, scores, -1e30)


def place_of(order_ref, block):
    return pl.ds(pl.multiple_of(order_ref[block] * SPAN, SPAN), SPAN)


def load_keys(order_ref, qkv_ref, q_width, cos_ref, sin_ref, k_rot, value):
    for block in range(qkv_ref.shape[0] // SPAN):
        there, here = place_of(order_ref, block), slice(block * SPAN, (block + 1) * SPAN)
        k_rot[here, :] = turn(qkv_ref[there, q_width : q_width + HEAD_DIM], cos_ref[here, :], sin_ref[here, :])
        value[here, :] = qkv_ref[there, q_width + HEAD_DIM : q_width + 2 * HEAD_DIM]


def load_rows(order_ref, ref, start, count, lanes):
    blocks = range(start // SPAN, (start + count) // SPAN)
    return jnp.concatenate([ref[place_of(order_ref, block), lanes] for block in blocks], axis=0)


def store_rows(order_ref, ref, start, lanes, values):
    for part in range(values.shape[0] // SPAN):
        ref[place_of(order_ref, start // SPAN + part), lanes] = values[part * SPAN : (part + 1) * SPAN, :]


def attend_forward_kernel(
    query_heads, block, order_ref, qkv_ref, cos_ref, sin_ref, aux_ref, seg_ref, out_ref, lse_ref, k_rot, value
):
    length = qkv_ref.shape[0]
    load_keys(order_ref, qkv_ref, query_heads * HEAD_DIM, cos_ref, sin_ref, k_rot, value)
    for start in range(0, length, block):
        rows = slice(start, start + block)
        end = start + block
        for head in range(query_heads):
            lanes = slice(head * HEAD_DIM, (head + 1) * HEAD_DIM)
            q_rows = load_rows(order_ref, qkv_ref, start, block, lanes)
            q_block = turn(q_rows, cos_ref[rows, :], sin_ref[rows, :])
            scores = block_scores(q_block, k_rot[:end, :], start, aux_ref[rows, 0:1], seg_ref[:, :end])
            top = jnp.max(scores, axis=1, keepdims=True)
            raised = jnp.exp(scores - top)
            total = jnp.sum(raised, axis=1, keepdims=True)
            probs = (raised * (1.0 / total)).astype(jnp.bfloat16)
            store_rows(order_ref, out_ref, start, lanes, dot_plain(probs, value[:end, :]).astype(jnp.bfloat16))
            lse_ref[rows, head : head + 1] = top + jnp.log(total)


def attend_backward_kernel(
    query_heads,
    block,
    order_ref,
    qkv_ref,
    cos_ref,
    sin_ref,
    aux_ref,
    seg_ref,
    lse_ref,
    grad_ref,
    out_ref,
    k_rot,
    value,
    dk,
    dv,
):
    f32, bf16 = jnp.float32, jnp.bfloat16
    length = qkv_ref.shape[0]
    q_width = query_heads * HEAD_DIM
    load_keys(order_ref, qkv_ref, q_width, cos_ref, sin_ref, k_rot, value)
    dk[...] = jnp.zeros(dk.shape, f32)
    dv[...] = jnp.zeros(dv.shape, f32)
    for start in range(0, length, block):
        rows = slice(start, start + block)
        end = start + block
        for head in range(query_heads):
            lanes = slice(head * HEAD_DIM, (head + 1) * HEAD_DIM)
            cosine, sine = cos_ref[rows, :], sin_ref[rows, :]
            q_block = turn(load_rows(order_ref, qkv_ref, start, block, lanes), cosine, sine)
            scores = block_scores(q_block, k_rot[:end, :], start, aux_ref[rows, 0:1], seg_ref[:, :end])
            probs = jnp.exp(scores - lse_ref[rows, head : head + 1])
            grad = load_rows(order_ref, grad_ref, start, block, lanes)
            grad_probs = dot_last(grad, value[:end, :])
            mean = jnp.sum(grad_probs * probs, axis=1, keepdims=True)
            grad_scores = (probs * (grad_probs - mean) * HEAD_DIM ** (-0.5)).astype(bf16)
            grad_query = turn_back(dot_plain(grad_scores, k_rot[:end, :]), cosine, sine)
            store_rows(order_ref, out_ref, start, lanes, grad_query)
            dk[:end, :] += dot_first(grad_scores, q_block)
            dv[:end, :] += dot_first(probs.astype(bf16), grad)
    k_lanes = slice(q_width, q_width + HEAD_DIM)
    v_lanes = slice(q_width + HEAD_DIM, q_width + 2 * HEAD_DIM)
    store_rows(order_ref, out_ref, 0, k_lanes, turn_back(dk[...], cos_ref[...], sin_ref[...]))
    store_rows(order_ref, out_ref, 0, v_lanes, dv[...].astype(bf16))


def attend_specs(arrays):
    return [pl.BlockSpec(memory_space=pltpu.SMEM)] + [pl.BlockSpec(memory_space=pltpu.VMEM)] * arrays


def attend_forward(order, early, tables, aux, seg_row, query_heads):
    length = early.shape[0]
    return pl.pallas_call(
        functools.partial(attend_forward_kernel, query_heads, min(ATT_ROWS, length)),
        in_specs=attend_specs(5),
        out_shape=[
            jax.ShapeDtypeStruct((length, query_heads * HEAD_DIM), jnp.bfloat16),
            jax.ShapeDtypeStruct((length, 8), jnp.float32),
        ],
        scratch_shapes=[pltpu.VMEM((length, HEAD_DIM), jnp.bfloat16), pltpu.VMEM((length, HEAD_DIM), jnp.bfloat16)],
        compiler_params=pltpu.CompilerParams(vmem_limit_bytes=VMEM_BYTES),
        cost_estimate=work(5),
        name="attend_forward",
    )(order, early, tables[0], tables[1], aux, seg_row)


def attend_backward(order, early, tables, aux, seg_row, lse, grad, query_heads):
    length = early.shape[0]
    return pl.pallas_call(
        functools.partial(attend_backward_kernel, query_heads, min(ATT_ROWS, length)),
        in_specs=attend_specs(7),
        out_shape=jax.ShapeDtypeStruct((length, (query_heads + 2) * HEAD_DIM), jnp.bfloat16),
        scratch_shapes=[
            pltpu.VMEM((length, HEAD_DIM), jnp.bfloat16),
            pltpu.VMEM((length, HEAD_DIM), jnp.bfloat16),
            pltpu.VMEM((length, HEAD_DIM), jnp.float32),
            pltpu.VMEM((length, HEAD_DIM), jnp.float32),
        ],
        compiler_params=pltpu.CompilerParams(vmem_limit_bytes=VMEM_BYTES),
        cost_estimate=work(7),
        name="attend_backward",
    )(order, early, tables[0], tables[1], aux, seg_row, lse, grad)


def after_kernel(*refs):
    pass


def after(value, *others):
    return pl.pallas_call(
        after_kernel,
        in_specs=[pl.BlockSpec(memory_space=pl.ANY)] * (1 + len(others)),
        out_specs=pl.BlockSpec(memory_space=pl.ANY),
        out_shape=jax.ShapeDtypeStruct(value.shape, value.dtype),
        input_output_aliases={0: 0},
        name="after",
    )(value, *others)


def move_blocks(tiles, width, here, there):
    per = 128 // width
    lane = lanes_iota(tiles[0].shape)
    moved = []
    for tile in range(len(tiles)):
        out = None
        for part in range(per):
            source = there(tile * per + part)
            piece = tiles[source // per]
            shift = ((part - source % per) * width) % 128
            if shift:
                piece = pltpu.roll(piece, shift, 1)
            out = piece if out is None else jnp.where(lane >= part * width, piece, out)
        moved.append(out)
    return moved


def to_gathered_tiles(tiles, width, seq, fsdp):
    return move_blocks(tiles, width, None, lambda b: (b % seq) * fsdp + b // seq)


def from_gathered_tiles(tiles, width, seq, fsdp):
    return move_blocks(tiles, width, None, lambda b: (b % fsdp) * seq + b // fsdp)


def tiles_of(array):
    return [array[:, lane : lane + 128] for lane in range(0, array.shape[1], 128)]


def add_arrived(own, arrived):
    total = own[...]
    for ref in arrived:
        total = total + ref[...].astype(jnp.float32)
    return total


def row_sum(tiles):
    total = tiles[0]
    for tile in tiles[1:]:
        total = total + tile
    return jnp.sum(total, axis=1, keepdims=True)


def middle_kernel(places, count, skip, own, rows, gain, *refs):
    arrived, (hidden_ref, middle_ref) = refs[:count], refs[count + skip :]
    middle = rows[...].astype(jnp.float32) + add_arrived(own, arrived)
    middle_ref[...] = middle
    mean = jnp.sum(middle * middle, axis=1, keepdims=True) / middle.shape[1]
    hidden = middle * lax.rsqrt(mean + EPSILON) * gain[0:1, :]
    moved = to_gathered_tiles(tiles_of(hidden), *places)
    hidden_ref[...] = jnp.concatenate(moved, axis=1).astype(jnp.bfloat16)


def norm_back_kernel(places, count, skip, keep_wide, own, rows, passed, gain, *refs):
    arrived, outs = refs[:count], refs[count + skip :]
    grads = add_arrived(own, arrived)
    grads = jnp.concatenate(from_gathered_tiles(tiles_of(grads), *places), axis=1)
    wide = rows[...].astype(jnp.float32)
    width = wide.shape[1]
    scale = lax.rsqrt(jnp.sum(wide * wide, axis=1, keepdims=True) / width + EPSILON)
    normed = wide * scale
    weighted = grads * gain[0:1, :]
    mean = jnp.sum(weighted * normed, axis=1, keepdims=True) / width
    total = passed[...].astype(jnp.float32) + scale * (weighted - normed * mean)
    outs[0][...] = total.astype(jnp.bfloat16)
    if keep_wide:
        outs[1][...] = total


def add_rows_kernel(count, own, rows, gain, *refs):
    refs[-1][...] = (rows[...] + add_arrived(own, refs[:count])).astype(refs[-1].dtype)


def rows_call(kernel, tokens, width, inputs, gain, arrived, outs, deps, name):
    block = pl.BlockSpec((SPAN, width), lambda i: (i, 0))
    whole = pl.BlockSpec((8, width), lambda i: (0, 0))
    out_specs = [whole if shape[0] == 8 else block for shape, dtype in outs]
    return pl.pallas_call(
        kernel,
        grid=(tokens // SPAN,),
        in_specs=[block] * len(inputs)
        + [whole]
        + [block] * len(arrived)
        + [pl.BlockSpec(memory_space=pl.ANY)] * len(deps),
        out_specs=out_specs,
        out_shape=[jax.ShapeDtypeStruct(shape, dtype) for shape, dtype in outs],
        compiler_params=pltpu.CompilerParams(
            dimension_semantics=("arbitrary",), vmem_limit_bytes=VMEM_BYTES
        ),
        cost_estimate=work(5),
        name=name,
    )(*inputs, gain, *arrived, *deps)


def norm_pieces_kernel(gain, *refs):
    pieces, out = refs[:-1], refs[-1]
    for block, piece in enumerate(pieces):

        @pl.when(pl.program_id(0) == block)
        def _(piece=piece):
            wide = piece[...].astype(jnp.float32)
            mean = jnp.sum(wide * wide, axis=1, keepdims=True) / wide.shape[1]
            out[...] = (wide * lax.rsqrt(mean + EPSILON) * gain[0:1, :]).astype(jnp.bfloat16)


def norm_pieces(pieces, spots, gain):
    width = pieces[0].shape[1]
    length = len(spots) * SPAN
    return pl.pallas_call(
        norm_pieces_kernel,
        grid=(len(spots),),
        in_specs=[pl.BlockSpec((8, width), lambda i: (0, 0))]
        + [pl.BlockSpec((SPAN, width), functools.partial(lambda half, i: (half, 0), half)) for piece, half in spots],
        out_specs=pl.BlockSpec((SPAN, width), lambda i: (i, 0)),
        out_shape=jax.ShapeDtypeStruct((length, width), jnp.bfloat16),
        compiler_params=pltpu.CompilerParams(
            dimension_semantics=("arbitrary",), vmem_limit_bytes=VMEM_BYTES
        ),
        cost_estimate=work(5),
        name="norm_pieces",
    )(gain, *[pieces[piece] for piece, half in spots])


def assemble_kernel(count, spots, *refs):
    pieces, out, held, sems = refs[:count], refs[-3], refs[-2], refs[-1]
    places = [pl.ds(block * SPAN, SPAN) for block in range(len(spots))]
    loads = [
        pltpu.make_async_copy(pieces[piece].at[places[half]], held.at[places[b]], sems.at[0, b])
        for b, (piece, half) in enumerate(spots)
    ]
    stores = [
        pltpu.make_async_copy(held.at[places[b]], out.at[places[b]], sems.at[1, b]) for b in range(len(spots))
    ]
    for load in loads:
        load.start()
    for load, store in zip(loads, stores):
        load.wait()
        store.start()
    for store in stores:
        store.wait()


def assemble(pieces, spots):
    width = pieces[0].shape[1]
    length = len(spots) * SPAN
    return pl.pallas_call(
        functools.partial(assemble_kernel, len(pieces), spots),
        in_specs=[pl.BlockSpec(memory_space=pl.ANY)] * len(pieces),
        out_specs=pl.BlockSpec(memory_space=pl.ANY),
        out_shape=jax.ShapeDtypeStruct((length, width), pieces[0].dtype),
        scratch_shapes=[
            pltpu.VMEM((length, width), pieces[0].dtype),
            pltpu.SemaphoreType.DMA((2, len(spots))),
        ],
        compiler_params=pltpu.CompilerParams(vmem_limit_bytes=VMEM_BYTES),
        cost_estimate=work(3),
        name="assemble",
    )(*pieces)


def start_rows_kernel(places, halves, rows, *refs):
    cots, out = refs[:-1], refs[-1]
    part = pl.program_id(0) // halves

    @pl.when(part == 0)
    def _():
        moved = to_gathered_tiles(tiles_of(rows[...].astype(jnp.float32)), *places)
        out[...] = jnp.concatenate(moved, axis=1).astype(out.dtype)

    for place, cot in enumerate(cots):

        @pl.when(part == place + 1)
        def _(cot=cot):
            out[...] = cot[...]


def start_rows(rows, cots, places):
    tokens, width = rows.shape
    halves = tokens // SPAN
    parts = 1 + len(cots)

    def block(part):
        return pl.BlockSpec((SPAN, width), lambda i: (jnp.clip(i - part * halves, 0, halves - 1), 0))

    return pl.pallas_call(
        functools.partial(start_rows_kernel, places, halves),
        grid=(parts * halves,),
        in_specs=[block(part) for part in range(parts)],
        out_specs=pl.BlockSpec((SPAN, width), lambda i: (i, 0)),
        out_shape=jax.ShapeDtypeStruct((parts * tokens, width), rows.dtype),
        compiler_params=pltpu.CompilerParams(
            dimension_semantics=("arbitrary",), vmem_limit_bytes=VMEM_BYTES
        ),
        cost_estimate=work(2),
        name="start_rows",
    )(rows, *cots)


def product_kernel(back, pairs, skip, sets, *refs):
    lefts, rights, outs = refs[:pairs], refs[pairs : 2 * pairs], refs[2 * pairs + skip :]
    blocks = lefts[0].shape[0] // SPAN
    where = {block: (out, place) for out, held in enumerate(sets) for place, block in enumerate(held)}
    for block in range(0, blocks, 2):
        total = None
        for left, right in zip(lefts, rights):
            rows = left[block * SPAN : (block + 2) * SPAN, :]
            part = dot_last(rows, right[...]) if back else dot_plain(rows, right[...])
            total = part if total is None else total + part
        for half in range(2):
            out, place = where[block + half]
            part = total[half * SPAN : (half + 1) * SPAN, :]
            outs[out][place * SPAN : (place + 1) * SPAN, :] = part.astype(outs[out].dtype)


def product_rows(lefts, rights, back, sets, dtypes, deps=(), weight=1):
    length = lefts[0].shape[0]
    width = rights[0].shape[0 if back else 1]
    slab = 512
    specs = [pl.BlockSpec(left.shape, lambda n: (0, 0)) for left in lefts]
    for right in rights:
        if back:
            specs.append(pl.BlockSpec((slab, right.shape[1]), lambda n: (n, 0)))
        else:
            specs.append(pl.BlockSpec((right.shape[0], slab), lambda n: (0, n)))
    return pl.pallas_call(
        functools.partial(product_kernel, back, len(lefts), len(deps), sets),
        grid=(width // slab,),
        in_specs=specs + [pl.BlockSpec(memory_space=pl.ANY)] * len(deps),
        out_specs=[pl.BlockSpec((len(held) * SPAN, slab), lambda n: (0, n)) for held in sets],
        out_shape=[
            jax.ShapeDtypeStruct((len(held) * SPAN, width), dtype) for held, dtype in zip(sets, dtypes)
        ],
        compiler_params=pltpu.CompilerParams(
            dimension_semantics=("arbitrary",), vmem_limit_bytes=VMEM_BYTES
        ),
        cost_estimate=work(weight * sum(2 * length * left.shape[1] * width for left in lefts) / 0.66e9),
        name="product_rows",
    )(*lefts, *rights, *deps)


def feed_kernel(units, slab, hidden, cot, gate_w, up_w, down_w, act_ref, grad_ref):
    here = pl.multiple_of(pl.program_id(0) * slab, slab)
    for row in range(0, hidden.shape[0], 256):
        rows = slice(row, row + 256)
        gate_pre = dot_plain(hidden[rows, :], gate_w[...])
        up_pre = dot_plain(hidden[rows, :], up_w[...])
        grad_act = dot_last(cot[rows, :], down_w[...])
        sig = jax.nn.sigmoid(gate_pre)
        silu = gate_pre * sig
        act_ref[rows, :] = (silu * up_pre).astype(jnp.bfloat16)
        grad_gate = grad_act * up_pre * sig * (1.0 + gate_pre * (1.0 - sig))
        grad_ref[rows, pl.ds(here, slab)] = grad_gate.astype(jnp.bfloat16)
        grad_ref[rows, pl.ds(units + here, slab)] = (grad_act * silu).astype(jnp.bfloat16)


def feed_products(hidden, cot, gate_up_w, down_w):
    length, width = hidden.shape
    units = down_w.shape[0]
    slab = min(256, units)
    steps = units // slab
    whole = pl.BlockSpec((length, width), lambda n: (0, 0))
    return pl.pallas_call(
        functools.partial(feed_kernel, units, slab),
        grid=(steps,),
        in_specs=[
            whole,
            whole,
            pl.BlockSpec((width, slab), lambda n: (0, n)),
            pl.BlockSpec((width, slab), lambda n: (0, steps + n)),
            pl.BlockSpec((slab, width), lambda n: (n, 0)),
        ],
        out_specs=[
            pl.BlockSpec((length, slab), lambda n: (0, n)),
            pl.BlockSpec((length, 2 * units), lambda n: (0, 0)),
        ],
        out_shape=[
            jax.ShapeDtypeStruct((length, units), jnp.bfloat16),
            jax.ShapeDtypeStruct((length, 2 * units), jnp.bfloat16),
        ],
        compiler_params=pltpu.CompilerParams(
            dimension_semantics=("arbitrary",), vmem_limit_bytes=VMEM_BYTES
        ),
        cost_estimate=work(6 * length * width * units / 0.6e9),
        name="feed_products",
    )(hidden, cot, gate_up_w, gate_up_w, down_w)


def sums_kernel(pairs, before, skip, *refs):
    out = refs[-1]
    total = refs[2 * pairs][...] if before else None
    for left, right in zip(refs[:pairs], refs[pairs : 2 * pairs]):
        part = dot_first(left[...], right[...])
        total = part if total is None else total + part
    out[...] = total.astype(out.dtype)


def weight_sums(lefts, rights, dtype, before=None, deps=()):
    length, rows = lefts[0].shape
    columns = rights[0].shape[1]
    wide = columns if columns <= 1408 else 1024
    tall = next(t for t in (1024, 768, 512, 384, 256, 128) if rows % t == 0 and t * wide <= 1024 * 1024)
    block = pl.BlockSpec((tall, wide), lambda i, j: (i, j))
    extra = [] if before is None else [before]
    return pl.pallas_call(
        functools.partial(sums_kernel, len(lefts), len(extra), len(deps)),
        grid=(rows // tall, columns // wide),
        in_specs=[pl.BlockSpec((length, tall), lambda i, j: (0, i)) for left in lefts]
        + [pl.BlockSpec((length, wide), lambda i, j: (0, j)) for right in rights]
        + [block] * len(extra)
        + [pl.BlockSpec(memory_space=pl.ANY)] * len(deps),
        out_specs=block,
        out_shape=jax.ShapeDtypeStruct((rows, columns), dtype),
        compiler_params=pltpu.CompilerParams(
            dimension_semantics=("arbitrary", "arbitrary"), vmem_limit_bytes=VMEM_BYTES
        ),
        cost_estimate=work(sum(2 * length * rows * columns for left in lefts) / 0.66e9),
        name="weight_sums",
    )(*lefts, *rights, *extra, *deps)


def gathered_rows_kernel(places, rows, out):
    moved = to_gathered_tiles(tiles_of(rows[...].astype(jnp.float32)), *places)
    out[...] = jnp.concatenate(moved, axis=1).astype(out.dtype)


def gathered_rows(rows, places):
    tokens, width = rows.shape
    block = pl.BlockSpec((SPAN, width), lambda i: (i, 0))
    return pl.pallas_call(
        functools.partial(gathered_rows_kernel, places),
        grid=(tokens // SPAN,),
        in_specs=[block],
        out_specs=block,
        out_shape=jax.ShapeDtypeStruct((tokens, width), rows.dtype),
        compiler_params=pltpu.CompilerParams(
            dimension_semantics=("arbitrary",), vmem_limit_bytes=VMEM_BYTES
        ),
        cost_estimate=work(1.5),
        name="gathered_rows",
    )(rows)


def matmul_rows(left, right):
    return jnp.einsum("tc,cd->td", left, right, preferred_element_type=jnp.float32)


def matmul_back(left, right):
    return jnp.einsum("td,cd->tc", left, right, preferred_element_type=jnp.float32)


def weight_grad(left, right):
    return jnp.einsum("tc,td->cd", left, right, preferred_element_type=jnp.float32)


def peers(count, flip):
    return [(i, i ^ flip) for i in range(count)]


def swap(value, flip):
    return lax.ppermute(value, "seq", peers(lax.axis_size("seq"), flip))


def block_order(tokens):
    return [(flip, half) for flip in range(lax.axis_size("seq")) for half in range(tokens // SPAN)]


def block_places(tokens):
    halves = tokens // SPAN
    blocks = jnp.arange(lax.axis_size("seq") * halves, dtype=jnp.int32)
    return ((blocks // halves) ^ lax.axis_index("seq")) * halves + blocks % halves


def fetch_tokens(rows):
    return [rows] + [swap(rows, flip) for flip in range(1, lax.axis_size("seq"))]


def scatter_tokens(lefts, rights, back, tokens, hold=(), deps=(), weight=1):
    f32, bf16 = jnp.float32, jnp.bfloat16
    halves = tokens // SPAN
    count = lax.axis_size("seq")
    sets = tuple(tuple(range(flip * halves, (flip + 1) * halves)) for flip in range(count))
    own, *parts = product_rows(lefts, rights, back, sets, (f32,) + (bf16,) * (count - 1), deps, weight)
    arrived = [swap(after(part, *hold) if hold else part, flip + 1) for flip, part in enumerate(parts)]
    return own, tuple(arrived), tuple(parts)


def add_over(vector, axis):
    count = lax.axis_size(axis)
    flip = 1
    while flip < count:
        vector = vector + lax.ppermute(vector, axis, peers(count, flip))
        flip *= 2
    return vector


def trade(stacked):
    return lax.all_to_all(stacked, "seq", split_axis=0, concat_axis=0, tiled=True)


def gather_weights(rows):
    return lax.all_gather(rows.reshape(-1, rows.shape[-1]), "fsdp", axis=0, tiled=True)


def spread_sums(grad):
    return lax.psum_scatter(grad, "fsdp", scatter_dimension=0, tiled=True)


def to_gathered(rows):
    seq, fsdp = lax.axis_size("seq"), lax.axis_size("fsdp")
    shape = rows.shape
    split = rows.reshape(shape[:-1] + (seq, fsdp, -1))
    return jnp.swapaxes(split, -3, -2).reshape(shape)


def from_gathered(rows):
    seq, fsdp = lax.axis_size("seq"), lax.axis_size("fsdp")
    shape = rows.shape
    split = rows.reshape(shape[:-1] + (fsdp, seq, -1))
    return jnp.swapaxes(split, -3, -2).reshape(shape)


def on_device(
    inputs,
    cotangent,
    segments,
    norm_in,
    ssm_in,
    attn_in,
    conv_w,
    conv_b,
    a_log,
    dt_bias,
    d_skip,
    ssm_out,
    attn_out,
    norm_ffn,
    w_gate,
    w_up,
    w_down,
):
    f32, bf16 = jnp.float32, jnp.bfloat16
    seq = lax.axis_size("seq")
    fsdp = lax.axis_size("fsdp")
    index = lax.axis_index("seq")
    rows = ssm_in.shape[0]
    tokens = inputs.shape[2]
    length = segments.shape[2]
    heads = SSM_HEADS // seq
    inner = heads * SSM_DIM
    query_heads = Q_HEADS // seq
    q_width = query_heads * HEAD_DIM
    qkv_width = q_width + 2 * HEAD_DIM
    groups = Q_HEADS // KV_HEADS
    kv_of = [(s * query_heads) // groups for s in range(seq)]
    head_start = index * heads
    inner_start = index * inner
    z_end, x_end, bc_end = SSM_INNER, 2 * SSM_INNER, 2 * SSM_INNER + 2 * STATE
    q_end = Q_HEADS * HEAD_DIM
    kv_end = q_end + KV_HEADS * HEAD_DIM

    def by_seq(block):
        return jnp.swapaxes(block.reshape(rows, seq, -1), 0, 1)

    def for_all(block):
        return jnp.broadcast_to(block[None], (seq,) + block.shape)

    def by_kv(block):
        return jnp.stack([block[:, h * HEAD_DIM : (h + 1) * HEAD_DIM] for h in kv_of])

    channels = conv_b.shape[0]
    conv_pack = jnp.concatenate([conv_w, conv_b[None]], axis=0).reshape(-1)
    conv_cols = -(-conv_pack.shape[0] // rows)
    conv_pack = jnp.pad(conv_pack, (0, conv_cols * rows - conv_pack.shape[0])).reshape(rows, conv_cols)
    misc = jnp.concatenate([norm_in[:, None], norm_ffn[:, None], conv_pack], axis=1)
    misc = jnp.pad(misc, ((0, 0), (0, 128 - misc.shape[1])))
    early_send = jnp.concatenate(
        [by_seq(attn_in[:, :q_end]), by_kv(attn_in[:, q_end:kv_end]), by_kv(attn_in[:, kv_end:]), for_all(misc)],
        axis=2,
    )
    halves = tokens // SPAN
    places = (rows, seq, fsdp)
    spots = block_order(tokens)
    mine = gathered_rows(inputs[0, 0], places)
    dt_block = jnp.pad(by_seq(ssm_in[:, bc_end:]), ((0, 0), (0, 0), (0, 128 - heads)))
    first_send = jnp.concatenate(
        [by_seq(ssm_in[:, z_end:x_end]), for_all(ssm_in[:, x_end:bc_end]), dt_block], axis=2
    )
    start_mine = trade(jnp.concatenate([early_send, first_send], axis=2))
    early_mine, first_mine = start_mine[:, :, : early_send.shape[2]], start_mine[:, :, early_send.shape[2] :]
    later_send = jnp.concatenate([by_seq(ssm_in[:, :z_end]), by_seq(w_gate), by_seq(w_up)], axis=2)
    pieces = [fetch_tokens(after(mine, start_mine))]
    out_send = jnp.concatenate([ssm_out, attn_out], axis=0)
    early_w = gather_weights(early_mine)
    first_w = gather_weights(first_mine)
    out_rows = ssm_out.shape[0]
    units = w_down.shape[0] * fsdp
    small = early_w[:, qkv_width:]

    def gain_rows(gain):
        return jnp.broadcast_to(gain.astype(f32)[None], (8, gain.shape[0]))

    gain_in_gathered = gain_rows(small[:, 0])
    gain_in = gain_rows(from_gathered(small[:, 0]))
    gain_ffn = gain_rows(from_gathered(small[:, 1]))
    conv_all = small[:, 2 : 2 + conv_cols].reshape(fsdp, seq, -1)[:, :, : (CONV + 1) * channels]
    conv_all = conv_all.reshape(fsdp, seq, CONV + 1, channels).transpose(2, 1, 0, 3)
    conv_all = conv_all.reshape(CONV + 1, CONV_CH).astype(f32)
    conv_local = jnp.concatenate(
        [lax.dynamic_slice_in_dim(conv_all, inner_start, inner, 1), conv_all[:, SSM_INNER:]], axis=1
    )
    conv_table = jnp.pad(conv_local, ((0, 8 - CONV - 1), (0, 0)))
    rate_local = lax.dynamic_slice_in_dim(a_log.astype(f32), head_start, heads)
    bias_local = lax.dynamic_slice_in_dim(dt_bias.astype(f32), head_start, heads)
    skip_local = lax.dynamic_slice_in_dim(d_skip.astype(f32), head_start, heads)
    head_table = jnp.pad(jnp.stack([bias_local, rate_local]), ((0, 6), (0, 128 - heads)))
    skip_table = jnp.broadcast_to(jnp.repeat(skip_local, SSM_DIM)[None], (8, inner))
    tables = rotary_tables(length)
    order = block_places(tokens)

    micro = range(MICRO)
    auxes = [token_aux(segments[m, 0]) for m in micro]
    seg_blocks = [segments[m, 0].astype(f32).reshape(-1, 1, SPAN) for m in micro]
    seg_rows = [segments[m, 0].astype(f32)[None] for m in micro]
    width = inputs.shape[3]
    head_tables = (conv_table, head_table, skip_table)

    hiddens, earlies, attendeds, lses, firsts, ys, all_starts = [], [], [], [], [], [], []
    gate_zs, gateds, mixeds, cot_alls = [], [], [], []
    def mixer_start(m, deps=()):
        if deps:
            pieces[m][0] = after(pieces[m][0], *deps)
        hidden = norm_pieces(pieces[m], spots, gain_in_gathered)
        early = matmul_rows(hidden, early_w).astype(bf16)
        attended, lse = attend_forward(order, early, tables, auxes[m], seg_rows[m], query_heads)
        hiddens.append(hidden)
        earlies.append(early)
        attendeds.append(attended)
        lses.append(lse)

    def mixer_scan(m, deps):
        hiddens[m] = after(hiddens[m], *deps)
        first = matmul_rows(hiddens[m], first_w).astype(bf16)
        y_rows, starts = ssd_forward(order, first, auxes[m], seg_blocks[m], *head_tables, heads)
        firsts.append(first)
        ys.append(y_rows)
        all_starts.append(starts)

    def mixer_gate(m, deps):
        hiddens[m] = after(hiddens[m], *deps)
        gate_z = matmul_rows(hiddens[m], z_w)
        gate_zs.append(gate_z)
        gateds.append((ys[m].astype(f32) * jax.nn.silu(gate_z)).astype(bf16))

    def mixer_out(m, deps, hold=()):
        mixeds.append(
            scatter_tokens([gateds[m], attendeds[m]], [ssm_out_w, attn_out_w], False, tokens, hold, deps, m)
        )

    later_mine = trade(after(later_send, *pieces[0][1:]))
    mixer_start(0, [later_mine])
    start_second = start_rows(inputs[1, 0], [cotangent[m, 0] for m in micro], places)
    pieces.append(fetch_tokens(after(start_second, later_mine)))
    z_mine, ffn_mine = later_mine[:, :, :inner], later_mine[:, :, inner:]
    z_w = gather_weights(z_mine)
    out_send = after(out_send, z_mine)
    out_w = gather_weights(out_send)
    gate_up_w = gather_weights(after(ffn_mine, out_send))
    mixer_scan(0, [attendeds[0], later_mine, start_second])
    down_w = gather_weights(after(w_down, firsts[0]))
    out_w = out_w.reshape(fsdp, -1, out_w.shape[1])
    ssm_out_w, attn_out_w = out_w[:, :out_rows].reshape(inner, -1), out_w[:, out_rows:].reshape(q_width, -1)
    side_w = jnp.concatenate([early_w[:, :qkv_width], z_w], axis=1)
    mixer_gate(0, [ys[0]])
    mixer_out(0, [gateds[0]])
    mixer_start(1, [mixeds[0][0]])
    for m in micro:
        cot_alls.append(assemble(pieces[1], [(flip, half + (1 + m) * halves) for flip, half in spots]))

    middles, ffn_hiddens, activateds, grad_gus, grad_hiddens = [], [], [], [], []
    grad_middles, lows, grads_mixed = [], [], []

    def middle_forward(m, deps, hold=()):
        own, arrived, parts = mixeds[m]
        hidden, middle = rows_call(
            functools.partial(middle_kernel, places, len(arrived), len(deps)),
            tokens,
            width,
            [own, inputs[m, 0]],
            gain_ffn,
            arrived,
            [((tokens, width), bf16), ((tokens, width), f32)],
            deps,
            "middle",
        )
        middles.append(middle)
        if hold:
            hidden = after(hidden, *hold)
        ffn_hiddens.append(assemble(fetch_tokens(hidden), spots))

    def feed_forward(m, deps, late=()):
        ffn_hiddens[m] = after(ffn_hiddens[m], *deps)
        activated, grad_gu = feed_products(ffn_hiddens[m], cot_alls[m], gate_up_w, down_w)
        activateds.append(activated)
        grad_gus.append(grad_gu)
        grad_hiddens.append(scatter_tokens([grad_gu], [gate_up_w], True, tokens, (), late))

    def middle_back(m, deps):
        own, arrived, parts = grad_hiddens[m]
        low, wide = rows_call(
            functools.partial(norm_back_kernel, places, len(arrived), len(deps), True),
            tokens,
            width,
            [own, middles[m], cotangent[m, 0]],
            gain_ffn,
            arrived,
            [((tokens, width), bf16), ((tokens, width), f32)],
            deps,
            "middle_back",
        )
        grad_middles.append(wide)
        lows.append(low)
        grads_mixed.append(assemble(fetch_tokens(low), spots))

    grad_ys, grad_sides, outs, back, in_backs, outputs = [], [], [], [], [], []

    def heads_back(m, deps):
        grad_mixed = after(grads_mixed[m], *deps)
        grads_mixed[m] = grad_mixed
        grad_gated = matmul_back(grad_mixed, ssm_out_w)
        grad_attended = matmul_back(grad_mixed, attn_out_w).astype(bf16)
        gate_z = gate_zs[m]
        sig = jax.nn.sigmoid(gate_z)
        y_wide = ys[m].astype(f32)
        grad_ys.append((grad_gated * gate_z * sig).astype(bf16))
        grad_z = (grad_gated * y_wide * sig * (1.0 + gate_z * (1.0 - sig))).astype(bf16)
        grad_qkv = attend_backward(
            order, earlies[m], tables, auxes[m], seg_rows[m], lses[m], grad_attended, query_heads
        )
        grad_sides.append(jnp.concatenate([grad_qkv, grad_z], axis=1))

    def output_rows(m, deps, hold=()):
        outs.append(scatter_tokens([activateds[m]], [down_w], False, tokens, hold, deps))

    def scan_back(m, deps):
        grad_y = after(grad_ys[m], *deps)
        back.append(
            ssd_backward(order, firsts[m], auxes[m], seg_blocks[m], *head_tables, all_starts[m], grad_y, heads)
        )

    def hidden_back(m, deps, hold=()):
        in_backs.append(
            scatter_tokens([back[m][0], grad_sides[m]], [first_w, side_w], True, tokens, hold, deps)
        )

    def finish_input(m, deps=()):
        own, arrived, parts = in_backs[m]
        return rows_call(
            functools.partial(norm_back_kernel, places, len(arrived), len(deps), False),
            tokens,
            width,
            [own, inputs[m, 0], grad_middles[m]],
            gain_in,
            arrived,
            [((tokens, width), bf16)],
            deps,
            "input_back",
        )[0]

    def finish_output(m, deps=()):
        own, arrived, parts = outs[m]
        return rows_call(
            functools.partial(add_rows_kernel, len(arrived)),
            tokens,
            width,
            [own, middles[m]],
            gain_ffn,
            arrived,
            [((tokens, width), bf16)],
            deps,
            "output_rows",
        )[0]

    def both(lefts, rights):
        return (weight_grad(lefts[0], rights[0]) + weight_grad(lefts[1], rights[1])).astype(bf16)

    def back_to_rows(part):
        return trade(part.reshape(seq, rows, -1)).astype(f32)

    middle_forward(0, [attendeds[1]])
    mixer_scan(1, [middles[0]])
    mixer_gate(1, [ys[1]])
    mixer_out(1, [gateds[1]])
    mixeds[1] = (
        mixeds[1][0],
        tuple(swap(after(part, ffn_hiddens[0]), flip + 1) for flip, part in enumerate(mixeds[1][2])),
        (),
    )
    feed_forward(0, ())
    gate_up_sum = weight_sums(ffn_hiddens[:1], grad_gus[:1], f32, None, [grad_hiddens[0][0], *mixeds[1][1]])
    down_sum = weight_sums(activateds[:1], cot_alls[:1], f32, None, [gate_up_sum])
    middle_back(0, [down_sum])
    middle_forward(1, (), [grads_mixed[0]])
    heads_back(0, ())
    output_rows(0, grad_sides, [ffn_hiddens[1]])
    feed_forward(1, [outs[0][0]])
    outputs.append(finish_output(0, [grad_hiddens[1][0]]))
    gate_up_sum = weight_sums(ffn_hiddens[1:], grad_gus[1:], bf16, gate_up_sum, [outputs[0]])
    gate_up_part = spread_sums(gate_up_sum)
    scan_back(0, [gate_up_sum])
    side_sum = weight_sums(hiddens[:1], grad_sides[:1], f32, None, [back[0][0]])
    ssm_out_sum = weight_sums(gateds[:1], grads_mixed[:1], f32, None, [side_sum])
    attn_out_sum = weight_sums(attendeds[:1], grads_mixed[:1], f32, None, [ssm_out_sum])
    middle_back(1, [attn_out_sum])

    down_sum = weight_sums(activateds[1:], cot_alls[1:], bf16, down_sum, [lows[1]])
    down_part = spread_sums(down_sum)
    hidden_back(0, [down_sum], [grads_mixed[1]])
    output_rows(1, [in_backs[0][0]], [grads_mixed[1]])
    first_sum = weight_sums(hiddens[:1], [back[0][0]], f32, None, [outs[1][0]])
    ssm_out_sum = weight_sums(gateds[1:], grads_mixed[1:], bf16, ssm_out_sum, [first_sum])
    attn_out_sum = weight_sums(attendeds[1:], grads_mixed[1:], bf16, attn_out_sum, [ssm_out_sum])
    out_sum = jnp.concatenate(
        [ssm_out_sum.reshape(fsdp, -1, width), attn_out_sum.reshape(fsdp, -1, width)], axis=1
    ).reshape(inner + q_width, width)
    out_part = spread_sums(out_sum)
    heads_back(1, [out_sum])
    outputs.append(finish_output(1, [grad_sides[1]]))
    side_sum = weight_sums(hiddens[1:], grad_sides[1:], bf16, side_sum, [outputs[1]])
    side_part = spread_sums(side_sum)
    gate_up_back = back_to_rows(gate_up_part)
    side_back = back_to_rows(side_part)
    scan_back(1, [side_sum, gate_up_part])
    low = finish_input(0, [back[1][0]])
    input_grads = [low]
    conv_grad = (back[0][1] + back[1][1])[: CONV + 1]
    head_grad = back[0][2] + back[1][2]
    skip_sum = jnp.sum((back[0][3] + back[1][3])[0].reshape(heads, SSM_DIM), axis=1)
    conv_whole = jnp.zeros((CONV + 1, CONV_CH), f32)
    conv_whole = lax.dynamic_update_slice_in_dim(conv_whole, conv_grad[:, :inner], inner_start, 1)
    conv_whole = lax.dynamic_update_slice_in_dim(conv_whole, conv_grad[:, inner:], SSM_INNER, 1)
    head_sums = lax.dynamic_update_slice_in_dim(
        jnp.zeros((3, SSM_HEADS), f32), jnp.stack([head_grad[0, :heads], head_grad[1, :heads], skip_sum]), head_start, 1
    )
    small_sums = [conv_whole.reshape(-1), head_sums.reshape(-1)]
    ends = [0]
    for piece in small_sums:
        ends.append(ends[-1] + piece.shape[0])
    total = add_over(jnp.concatenate(small_sums), "seq")
    first_sum = weight_sums(hiddens[1:], [back[1][0]], bf16, first_sum, [low, gate_up_back, down_part, out_part, total])
    first_part = spread_sums(first_sum)
    first_back = back_to_rows(first_part)
    hidden_back(1, [first_sum])
    total = add_over(after(total, in_backs[1][0]), "fsdp")
    input_grads.append(finish_input(1))

    out_part = after(out_part, in_backs[1][0]).astype(f32)

    def own_columns(block):
        return jnp.swapaxes(block, 0, 1).reshape(rows, -1)

    def kv_columns(block):
        return jnp.concatenate(
            [sum(block[s] for s in range(seq) if kv_of[s] == h) for h in range(KV_HEADS)], axis=1
        )

    gate_grad = own_columns(gate_up_back[:, :, :units])
    up_grad = own_columns(gate_up_back[:, :, units:])
    ssm_in_grad = jnp.concatenate(
        [
            own_columns(side_back[:, :, qkv_width:]),
            own_columns(first_back[:, :, :inner]),
            jnp.sum(first_back[:, :, inner : inner + 2 * STATE], axis=0),
            own_columns(first_back[:, :, inner + 2 * STATE : inner + 2 * STATE + heads]),
        ],
        axis=1,
    )
    attn_in_grad = jnp.concatenate(
        [
            own_columns(side_back[:, :, :q_width]),
            kv_columns(side_back[:, :, q_width : q_width + HEAD_DIM]),
            kv_columns(side_back[:, :, q_width + HEAD_DIM : qkv_width]),
        ],
        axis=1,
    )

    conv_total, head_total = (total[a:b] for a, b in zip(ends[:-1], ends[1:]))
    def gain_grad(gain, *pairs):
        total = sum(jnp.sum(weight.astype(f32) * grad, axis=1) for weight, grad in pairs)
        return total / gain.astype(f32)

    place = index * fsdp + lax.axis_index("fsdp")
    conv_total = lax.dynamic_slice_in_dim(conv_total.reshape(CONV + 1, CONV_CH), place * channels, channels, 1)
    head_total = head_total.reshape(3, SSM_HEADS)
    return (
        jnp.stack(outputs)[:, None],
        jnp.stack(input_grads)[:, None],
        gain_grad(norm_in, (ssm_in, ssm_in_grad), (attn_in, attn_in_grad)),
        ssm_in_grad,
        attn_in_grad,
        conv_total[:CONV],
        conv_total[CONV],
        head_total[0],
        head_total[1],
        head_total[2],
        out_part[:out_rows],
        out_part[out_rows:],
        gain_grad(norm_ffn, (w_gate, gate_grad), (w_up, up_grad)),
        gate_grad,
        up_grad,
        after(down_part, in_backs[1][0]).astype(f32),
    )


def solution(mesh):
    return jax.shard_map(
        on_device,
        mesh=mesh,
        in_specs=(
            P(None, "fsdp", "seq", None),
            P(None, "fsdp", "seq", None),
            P(None, "fsdp", None),
            P(("seq", "fsdp")),
            P(("seq", "fsdp"), None),
            P(("seq", "fsdp"), None),
            P(None, ("seq", "fsdp")),
            P(("seq", "fsdp")),
            P(),
            P(),
            P(),
            P(("seq", "fsdp"), None),
            P(("seq", "fsdp"), None),
            P(("seq", "fsdp")),
            P(("seq", "fsdp"), None),
            P(("seq", "fsdp"), None),
            P(("seq", "fsdp"), None),
        ),
        out_specs=(
            P(None, "fsdp", "seq", None),
            P(None, "fsdp", "seq", None),
            P(("seq", "fsdp")),
            P(("seq", "fsdp"), None),
            P(("seq", "fsdp"), None),
            P(None, ("seq", "fsdp")),
            P(("seq", "fsdp")),
            P(),
            P(),
            P(),
            P(("seq", "fsdp"), None),
            P(("seq", "fsdp"), None),
            P(("seq", "fsdp")),
            P(("seq", "fsdp"), None),
            P(("seq", "fsdp"), None),
            P(("seq", "fsdp"), None),
        ),
        check_vma=False,
    )
```
